32 devices in a mesh: dp: 8 (over z, y), mp: 4 (over x, core).
Axes of the slice: x: 2, y: 2, z: 4, core: 2. Of those that a mesh axis runs over, the one named last changes fastest.
Arguments:
- tokens: bfloat16 [128, 128, 768], P('dp'), may hold values from -6 to 6
- lengths: int32 [128], P('dp'), may hold values from 16 to 128, as said below
- timesteps: int32 [128], P('dp'), may hold values from 0 to 999
- cotangent: float32 [128, 128, 768], P('dp'), may hold values from -6 to 6
- proj_input: float32 [768, 3, 768], P(None, None, 'mp'), may hold values from -0.25259074 to 0.25259074
- proj_output: float32 [768, 768], P('mp'), may hold values from -1.010363 to 1.010363
- proj_upward: float32 [768, 3072], P(None, 'mp'), may hold values from -0.25259074 to 0.25259074
- proj_downward: float32 [3072, 768], P('mp'), may hold values from -0.19846416 to 0.19846416
- norm_params: float32 [4, 768], replicated, may hold values from -1 to 1.5, as said below
- input_mean: float32 [768, 3, 768], P(None, None, 'mp'), may hold values from -0.64 to 0.64
- input_square: float32 [768, 3, 768], P(None, None, 'mp'), may hold values from 0.032768 to 0.49152
- output_mean: float32 [768, 768], P('mp'), may hold values from -0.64 to 0.64
- output_square: float32 [768, 768], P('mp'), may hold values from 0.032768 to 0.49152
- upward_mean: float32 [768, 3072], P(None, 'mp'), may hold values from -0.64 to 0.64
- upward_square: float32 [768, 3072], P(None, 'mp'), may hold values from 0.032768 to 0.49152
- downward_mean: float32 [3072, 768], P('mp'), may hold values from -0.64 to 0.64
- downward_square: float32 [3072, 768], P('mp'), may hold values from 0.032768 to 0.49152
- norms_mean: float32 [4, 768], replicated, may hold values from -0.64 to 0.64
- norms_square: float32 [4, 768], replicated, may hold values from 0.032768 to 0.49152
Outputs:
- result: float32 [128, 128, 768], P('dp')
- in_grad: float32 [128, 128, 768], P('dp')
- grad_norm: float32 [], replicated
- input_mean_new: float32 [768, 3, 768], P(None, None, 'mp')
- input_square_new: float32 [768, 3, 768], P(None, None, 'mp')
- input_next: float32 [768, 3, 768], P(None, None, 'mp')
- input_half: bfloat16 [768, 3, 768], P(None, None, 'mp')
- output_mean_new: float32 [768, 768], P('mp')
- output_square_new: float32 [768, 768], P('mp')
- output_next: float32 [768, 768], P('mp')
- output_half: bfloat16 [768, 768], P('mp')
- upward_mean_new: float32 [768, 3072], P(None, 'mp')
- upward_square_new: float32 [768, 3072], P(None, 'mp')
- upward_next: float32 [768, 3072], P(None, 'mp')
- upward_half: bfloat16 [768, 3072], P(None, 'mp')
- downward_mean_new: float32 [3072, 768], P('mp')
- downward_square_new: float32 [3072, 768], P('mp')
- downward_next: float32 [3072, 768], P('mp')
- downward_half: bfloat16 [3072, 768], P('mp')
- norms_mean_new: float32 [4, 768], replicated
- norms_square_new: float32 [4, 768], replicated
- norms_next: float32 [4, 768], replicated
The draws below stay inside these ranges and needn't reach their ends.
Inputs may be any that keep to these rules, and one draw needn't show every extreme that they name: `lengths`: every dp index holds one sequence with all 128 slots live. `norm_params`: rows 0 and 2 are gains, rows 1 and 3 biases.
All inputs are finite; a program needn't handle non-finite values.
Results may differ from the reference program's by a relative error of at most 0.012.
The reference program's roundings to bfloat16 on the way count: a program that leaves them out, or rounds other values in their place, can miss the bound.
Values sent between devices are 32-bit elements; how exact they have to be, the bound alone decides.
No kernel may reach another device: no remote copies, remote signals or barrier semaphores. Data moves between devices by JAX's collectives and lax.ppermute only.
A program may use at most 192 MiB of HBM per device.

```python
import math
import jax
import jax.numpy as jnp
from jax import lax

D = 768
HEADS = 12
HEAD_DIM = 64
FF = 3072
SEQ_LEN = 128
SEQ_DEV = 16
STEP = 10
SEQS = 128


def rising(count, low_end, high_end):
    ramping = jnp.arange(count, dtype=jnp.float32) / max(count - 1, 1)
    return jnp.exp(math.log(low_end) + ramping * (math.log(high_end) - math.log(low_end)))


def draw_lengths(key, part):
    key = jax.random.fold_in(key, 7)
    subkeys = jax.random.split(key, 4)
    selector = jax.random.randint(subkeys[0], (SEQS,), 0, 2)
    shorter = jax.random.randint(subkeys[1], (SEQS,), SEQ_LEN // 8, SEQ_LEN // 2 + 1)
    stories = jax.random.randint(subkeys[2], (SEQS,), 3 * SEQ_LEN // 8, SEQ_LEN + 1)
    baseline = jnp.where(selector > 0, stories, shorter)
    chosen = jax.random.randint(subkeys[3], (SEQS // SEQ_DEV,), 0, SEQ_DEV)
    slotted = jnp.arange(SEQS, dtype=jnp.int32) % SEQ_DEV
    filled = slotted == jnp.repeat(chosen, SEQ_DEV)
    return jnp.where(filled, SEQ_LEN, baseline).astype(jnp.int32)


def draw_proj_input(key, part):
    key = jax.random.fold_in(key, 1)
    shaped = (D, 3, HEADS * HEAD_DIM)
    noises = jnp.clip(jax.random.normal(key, shaped, jnp.float32), -4.0, 4.0)
    profile = rising(HEADS * HEAD_DIM, 0.7, 1.4)
    return noises * profile[None, None, :] * D ** (-0.5)


def draw_proj_output(key, part):
    key = jax.random.fold_in(key, 2)
    shaped = (HEADS * HEAD_DIM, D)
    noises = jnp.clip(jax.random.normal(key, shaped, jnp.float32), -4.0, 4.0)
    profile = rising(HEADS * HEAD_DIM, 0.7, 1.4)
    return noises * profile[:, None] * 4.0 * (HEADS * HEAD_DIM) ** (-0.5)


def draw_proj_upward(key, part):
    key = jax.random.fold_in(key, 3)
    shaped = (D, FF)
    noises = jnp.clip(jax.random.normal(key, shaped, jnp.float32), -4.0, 4.0)
    profile = rising(FF, 0.7, 1.4)
    return noises * profile[None, :] * D ** (-0.5)


def draw_proj_downward(key, part):
    key = jax.random.fold_in(key, 4)
    shaped = (FF, D)
    noises = jnp.clip(jax.random.normal(key, shaped, jnp.float32), -4.0, 4.0)
    profile = rising(FF, 0.7, 1.4)
    return noises * profile[:, None] * 1.5 * FF ** (-0.5)


def draw_norm_params(key, part):
    key = jax.random.fold_in(key, 5)
    noises = jnp.clip(jax.random.normal(key, (4, D), jnp.float32), -4.0, 4.0)
    selector = (jnp.arange(4) % 2 == 0)[:, None]
    return jnp.where(selector, 1.0 + 0.1 * noises, 0.2 * noises)


def moment_noise(key, shaped, bounded):
    return jnp.clip(jax.random.normal(key, shaped, jnp.float32), -bounded, bounded)


def draw_input_mean(key, part):
    key = jax.random.fold_in(key, 11)
    shaped = (D, 3, HEADS * HEAD_DIM)
    noises = moment_noise(key, shaped, 4.5)
    return noises * 0.001 * math.sqrt(SEQS * SEQ_LEN)


def draw_output_mean(key, part):
    key = jax.random.fold_in(key, 12)
    shaped = (HEADS * HEAD_DIM, D)
    noises = moment_noise(key, shaped, 4.5)
    return noises * 0.001 * math.sqrt(SEQS * SEQ_LEN)


def draw_upward_mean(key, part):
    key = jax.random.fold_in(key, 13)
    shaped = (D, FF)
    noises = moment_noise(key, shaped, 4.5)
    return noises * 0.001 * math.sqrt(SEQS * SEQ_LEN)


def draw_downward_mean(key, part):
    key = jax.random.fold_in(key, 14)
    shaped = (FF, D)
    noises = moment_noise(key, shaped, 4.5)
    return noises * 0.001 * math.sqrt(SEQS * SEQ_LEN)


def draw_norms_mean(key, part):
    key = jax.random.fold_in(key, 15)
    shaped = (4, D)
    noises = moment_noise(key, shaped, 4.5)
    return noises * 0.001 * math.sqrt(SEQS * SEQ_LEN)


def touch_ends(drawn, rng, least, largest):
    longest = drawn.shape.index(max(drawn.shape))
    spots = []
    for shift in (0, 1):
        where = [jax.random.randint(jax.random.fold_in(rng, axis), (), 0, length) for axis, length in enumerate(drawn.shape)]
        where[longest] = (where[longest] + shift) % drawn.shape[longest]
        spots.append(tuple(where))
    return drawn.at[spots[0]].set(least).at[spots[1]].set(largest)


def level_of(stream_key, shape, cuts, low, high):
    level, own = 1.0, jax.random.fold_in(stream_key, 6)
    for position, parts in cuts:
        heights = jnp.exp(jax.random.uniform(jax.random.fold_in(own, position), (parts,), jnp.float32, low / len(cuts), high / len(cuts)))
        level = level * jnp.repeat(heights, shape[position] // parts).reshape([-1 if axis == position else 1 for axis in range(len(shape))])
    return level


def bell_draw(rng, dims, deviation, limit, cuts=(), kind=jnp.bfloat16):
    array = deviation * jax.random.normal(rng, dims, jnp.float32)
    if cuts:
        array = array * level_of(rng, dims, cuts, -0.22, 0.18)
    return jnp.clip(array, -limit, limit).astype(kind)


def setup_inputs(seed: int = 0) -> dict:
    keys = jax.random.split(jax.random.key(seed), 20)
    tokens = bell_draw(keys[0], (SEQS, SEQ_LEN, D), 1.0, 6.0, ((0, 8),))
    lengths = draw_lengths(jax.random.fold_in(keys[19], 71), 0)
    timesteps = touch_ends(jax.random.randint(keys[2], (SEQS,), 0, 1000), jax.random.fold_in(keys[2], 1), 0, 999).astype(jnp.int32)
    cotangent = bell_draw(keys[3], (SEQS, SEQ_LEN, D), 1.0, 6.0, ((0, 8),), jnp.float32)
    proj_input = draw_proj_input(jax.random.fold_in(keys[19], 71), 0)
    proj_output = draw_proj_output(jax.random.fold_in(keys[19], 71), 0)
    proj_upward = draw_proj_upward(jax.random.fold_in(keys[19], 71), 0)
    proj_downward = draw_proj_downward(jax.random.fold_in(keys[19], 71), 0)
    norm_params = draw_norm_params(jax.random.fold_in(keys[19], 71), 0)
    input_mean = draw_input_mean(jax.random.fold_in(keys[19], 71), 0)
    input_square = jnp.clip(jnp.exp(math.log(0.49152) - 2.7080502 * jax.random.uniform(keys[10], (D, 3, HEADS * HEAD_DIM), jnp.float32) ** level_of(keys[10], (D, 3, HEADS * HEAD_DIM), ((2, 4),), -0.2, 0.2)), 0.032768, 0.49152)
    output_mean = draw_output_mean(jax.random.fold_in(keys[19], 71), 0)
    output_square = jnp.clip(jnp.exp(math.log(0.49152) - 2.7080502 * jax.random.uniform(keys[12], (HEADS * HEAD_DIM, D), jnp.float32) ** level_of(keys[12], (HEADS * HEAD_DIM, D), ((0, 4),), -0.2, 0.2)), 0.032768, 0.49152)
    upward_mean = draw_upward_mean(jax.random.fold_in(keys[19], 71), 0)
    upward_square = jnp.clip(jnp.exp(math.log(0.49152) - 2.7080502 * jax.random.uniform(keys[14], (D, FF), jnp.float32) ** level_of(keys[14], (D, FF), ((1, 4),), -0.2, 0.2)), 0.032768, 0.49152)
    downward_mean = draw_downward_mean(jax.random.fold_in(keys[19], 71), 0)
    downward_square = jnp.clip(jnp.exp(math.log(0.49152) - 2.7080502 * jax.random.uniform(keys[16], (FF, D), jnp.float32) ** level_of(keys[16], (FF, D), ((0, 4),), -0.2, 0.2)), 0.032768, 0.49152)
    norms_mean = draw_norms_mean(jax.random.fold_in(keys[19], 71), 0)
    norms_square = jnp.clip(jnp.exp(jax.random.uniform(keys[18], (4, D), jnp.float32, math.log(0.032768), math.log(0.49152))), 0.032768, 0.49152)
    return dict(tokens=tokens, lengths=lengths, timesteps=timesteps, cotangent=cotangent, proj_input=proj_input, proj_output=proj_output, proj_upward=proj_upward, proj_downward=proj_downward, norm_params=norm_params, input_mean=input_mean, input_square=input_square, output_mean=output_mean, output_square=output_square, upward_mean=upward_mean, upward_square=upward_square, downward_mean=downward_mean, downward_square=downward_square, norms_mean=norms_mean, norms_square=norms_square)


@jax.custom_vjp
def low(v):
    return lax.optimization_barrier(v.astype(jnp.bfloat16)).astype(jnp.float32)

@jax.custom_vjp
def low_back(v):
    return v

def low_keep(v):
    return (low(v), None)

def low_pass(kept, grad):
    return (grad,)

def back_keep(v):
    return (v, None)

def back_low(kept, grad):
    return (low(grad),)
low.defvjp(low_keep, low_pass)
low_back.defvjp(back_keep, back_low)
eps_norm = 1e-05
beta_one = 0.9
beta_two = 0.95
adam_eps = 1e-08
decay_weight = 0.1
clip_coeff = 0.03
rate_inproj = 0.07
rate_outproj = 0.3
rate_upproj = 0.07
rate_downproj = 0.05
rate_norms = 0.2

def layer_norm(hidden, gain, shift):
    centre = lax.optimization_barrier(jnp.mean(hidden, axis=-1, keepdims=True))
    offset = hidden - centre
    spread = lax.optimization_barrier(jnp.mean(offset * offset, axis=-1, keepdims=True))
    return offset * lax.rsqrt(spread + eps_norm) * gain + shift

def time_embed(steps_given, width):
    halfway = width // 2
    counter = jnp.arange(halfway, dtype=jnp.float32)
    frequency = jnp.exp(-math.log(10000.0) * counter / halfway)
    angles = steps_given.astype(jnp.float32)[:, None] * frequency[None, :]
    return jnp.concatenate([jnp.sin(angles), jnp.cos(angles)], axis=-1)

def adam_update(weight, gradient, mean_old, square_old, rate, decay_rate):
    mean_new = beta_one * mean_old + (1.0 - beta_one) * gradient
    square_new = beta_two * square_old + (1.0 - beta_two) * gradient * gradient
    direction = mean_new / (1.0 - beta_one ** STEP) / (jnp.sqrt(square_new / (1.0 - beta_two ** STEP)) + adam_eps)
    weight_new = weight - rate * (direction + decay_rate * weight)
    return (mean_new, square_new, weight_new)

def attend_group(operands):
    queries, keyset, valueset, live_keys = operands
    highest = lax.Precision.HIGHEST
    scores = jnp.einsum('sqhd,skhd->shqk', queries, keyset, precision=highest) * HEAD_DIM ** (-0.5)
    scores = jnp.where(live_keys[:, None, None, :] > 0, scores, -1000000000.0)
    scores = low_back(scores)
    softened = low(jax.nn.softmax(scores, axis=-1))
    return jnp.einsum('shqk,skhd->sqhd', softened, valueset, precision=highest)

def block_forward(start, live, proj_input, proj_output, proj_upward, proj_downward, norm_params):
    seq_total = start.shape[0]
    highest = lax.Precision.HIGHEST
    flat = start.reshape(seq_total * SEQ_LEN, D)
    weight_in = low(proj_input).reshape(D, 3 * HEADS * HEAD_DIM)
    weight_out = low(proj_output)
    weight_rise = low(proj_upward)
    weight_fall = low(proj_downward)
    normed_one = low(layer_norm(flat, norm_params[0], norm_params[1]))
    mixed = low_back(low(jnp.dot(normed_one, weight_in, precision=highest)))
    pieces = mixed.reshape(seq_total, SEQ_LEN, 3, HEADS, HEAD_DIM)
    per_group = min(seq_total, max(1, 4096 // SEQ_LEN))
    groups_all = seq_total // per_group

    def grouped(values):
        return values.reshape((groups_all, per_group) + values.shape[1:])
    context = lax.map(jax.checkpoint(attend_group), (grouped(pieces[:, :, 0]), grouped(pieces[:, :, 1]), grouped(pieces[:, :, 2]), grouped(live)))
    context = low_back(low(context.reshape(seq_total * SEQ_LEN, HEADS * HEAD_DIM)))
    attended = low_back(jnp.dot(context, weight_out, precision=highest))
    middle = flat + attended
    normed_two = low(layer_norm(middle, norm_params[2], norm_params[3]))
    upward = low_back(jnp.dot(normed_two, weight_rise, precision=highest))
    activated = low(jax.nn.gelu(upward, approximate=False))
    downward = low_back(jnp.dot(activated, weight_fall, precision=highest))
    return (middle + downward).reshape(seq_total, SEQ_LEN, D)

def reference(tokens, lengths, timesteps, cotangent, proj_input, proj_output, proj_upward, proj_downward, norm_params, input_mean, input_square, output_mean, output_square, upward_mean, upward_square, downward_mean, downward_square, norms_mean, norms_square):
    positions = jnp.arange(SEQ_LEN, dtype=jnp.int32)
    live = (positions[None, :] < lengths[:, None]).astype(jnp.float32)
    start = tokens.astype(jnp.float32) + time_embed(timesteps, D)[:, None, :]

    def forward(start_in, weight_a, weight_b, weight_c, weight_d, weight_e):
        return block_forward(start_in, live, weight_a, weight_b, weight_c, weight_d, weight_e)
    result, pullback = jax.vjp(forward, start, proj_input, proj_output, proj_upward, proj_downward, norm_params)
    gradients = pullback(cotangent * live[:, :, None])
    in_grad = gradients[0]
    grad_input, grad_output, grad_upward, grad_downward, grad_norms = gradients[1:]
    squares = jnp.sum(grad_input * grad_input) + jnp.sum(grad_output * grad_output) + jnp.sum(grad_upward * grad_upward) + jnp.sum(grad_downward * grad_downward) + jnp.sum(grad_norms * grad_norms)
    grad_norm = jnp.sqrt(squares)
    threshold = clip_coeff * D * math.sqrt(SEQS * SEQ_LEN)
    factor = jnp.minimum(1.0, threshold / grad_norm)
    in_m, in_v, in_w = adam_update(proj_input, grad_input * factor, input_mean, input_square, rate_inproj, decay_weight)
    out_m, out_v, out_w = adam_update(proj_output, grad_output * factor, output_mean, output_square, rate_outproj, decay_weight)
    up_m, up_v, up_w = adam_update(proj_upward, grad_upward * factor, upward_mean, upward_square, rate_upproj, decay_weight)
    down_m, down_v, down_w = adam_update(proj_downward, grad_downward * factor, downward_mean, downward_square, rate_downproj, decay_weight)
    norm_m, norm_v, norm_w = adam_update(norm_params, grad_norms * factor, norms_mean, norms_square, rate_norms, 0.0)
    return (result, in_grad, grad_norm, in_m, in_v, in_w, in_w.astype(jnp.bfloat16), out_m, out_v, out_w, out_w.astype(jnp.bfloat16), up_m, up_v, up_w, up_w.astype(jnp.bfloat16), down_m, down_v, down_w, down_w.astype(jnp.bfloat16), norm_m, norm_v, norm_w)
```

```python
import math

import jax
import jax.numpy as jnp
from jax import lax
from jax.experimental import pallas as pl
from jax.experimental.pallas import tpu as pltpu
from jax.sharding import PartitionSpec as P

HEAD_DIM = 64
STEP = 10


eps_norm = 1e-05
beta_one = 0.9
beta_two = 0.95
adam_eps = 1e-08
decay_weight = 0.1
clip_coeff = 0.03
rate_inproj = 0.07
rate_outproj = 0.3
rate_upproj = 0.07
rate_downproj = 0.05
rate_norms = 0.2


def time_embed(steps_given, width):
    halfway = width // 2
    counter = jnp.arange(halfway, dtype=jnp.float32)
    frequency = jnp.exp(-math.log(10000.0) * counter / halfway)
    angles = steps_given.astype(jnp.float32)[:, None] * frequency[None, :]
    return jnp.concatenate([jnp.sin(angles), jnp.cos(angles)], axis=-1)


def gelu_exact(values):
    return jax.nn.gelu(values, approximate=False)


def adam_update(weight, gradient, mean_old, square_old, rate, decay_rate):
    mean_new = beta_one * mean_old + (1.0 - beta_one) * gradient
    square_new = beta_two * square_old + (1.0 - beta_two) * gradient * gradient
    direction = (
        mean_new
        / (1.0 - beta_one**STEP)
        / (jnp.sqrt(square_new / (1.0 - beta_two**STEP)) + adam_eps)
    )
    weight_new = weight - rate * (direction + decay_rate * weight)
    return (mean_new, square_new, weight_new)


def masked_scores(queries, keyset, live_mask):
    scaling = queries.shape[-1] ** (-0.5)
    scores = (
        jnp.einsum("sqhd,skhd->shqk", queries, keyset, preferred_element_type=jnp.float32) * scaling
    )
    return jnp.where(live_mask[:, None, None, :] > 0, scores, -1000000000.0)


def attend_forward(queries, keyset, valueset, live_mask):
    scores = masked_scores(queries, keyset, live_mask)
    highest = jnp.max(scores, axis=-1, keepdims=True)
    summed = jnp.sum(jnp.exp(scores - highest), axis=-1, keepdims=True)
    logsum = highest + jnp.log(summed)
    softened = jnp.exp(scores - logsum).astype(jnp.bfloat16)
    context = jnp.einsum("shqk,skhd->sqhd", softened, valueset, preferred_element_type=jnp.float32)
    return (context.astype(jnp.bfloat16), logsum)


def attend_back(queries, keyset, valueset, live_mask, logsum, grad_context):
    scaling = queries.shape[-1] ** (-0.5)
    scores = masked_scores(queries, keyset, live_mask)
    softened = jnp.exp(scores - logsum)
    soft_half = softened.astype(jnp.bfloat16)
    grad_probs = jnp.einsum(
        "sqhd,skhd->shqk", grad_context, valueset, preferred_element_type=jnp.float32
    )
    grad_value = jnp.einsum(
        "shqk,sqhd->skhd", soft_half, grad_context, preferred_element_type=jnp.float32
    ).astype(jnp.bfloat16)
    inner_sum = jnp.sum(softened * grad_probs, axis=-1, keepdims=True)
    grad_scores = (softened * (grad_probs - inner_sum)).astype(jnp.bfloat16)
    grad_query = (
        jnp.einsum("shqk,skhd->sqhd", grad_scores, keyset, preferred_element_type=jnp.float32)
        * scaling
    ).astype(jnp.bfloat16)
    grad_key = (
        jnp.einsum("shqk,sqhd->skhd", grad_scores, queries, preferred_element_type=jnp.float32)
        * scaling
    ).astype(jnp.bfloat16)
    context = None
    context = jnp.einsum(
        "shqk,skhd->sqhd", soft_half, valueset, preferred_element_type=jnp.float32
    ).astype(jnp.bfloat16)
    return (grad_query, grad_key, grad_value, context)


def exchange(values, axis, pairs):
    return lax.ppermute(values, axis, pairs)


def swap_pairs(count, bit):
    return [(i, i ^ bit) for i in range(count)]


def pick(flag, first, second):
    return jnp.where(flag, first, second)


def foreign_shard(weight):
    dp_count, mp_count = lax.axis_size("dp"), lax.axis_size("mp")
    place = lax.axis_index("dp")
    low, high = place % 2, (place // 2) % 2
    quarter = weight.shape[0] // 4
    first = lax.dynamic_slice_in_dim(weight, low * quarter, quarter, 0)
    second = lax.dynamic_slice_in_dim(weight, (2 + high) * quarter, quarter, 0)
    across = swap_pairs(mp_count, 2)
    got_first = exchange(first, "mp", across)
    got_second = exchange(second, "mp", across)
    other_first = exchange(got_first, "dp", swap_pairs(dp_count, 1))
    other_second = exchange(got_second, "dp", swap_pairs(dp_count, 2))
    return assemble(low, high, got_first, other_first, got_second, other_second)


def assemble_kernel(place, got_first, other_first, got_second, other_second, out):
    rows = got_first.shape[0]
    for flag, begin, got, other in (
        (place[0], 0, got_first, other_first),
        (place[1], 2 * rows, got_second, other_second),
    ):
        got_at = pl.multiple_of(begin + flag * rows, 16)
        other_at = pl.multiple_of(begin + (1 - flag) * rows, 16)
        out[pl.ds(got_at, rows), :] = got[...].astype(out.dtype)
        out[pl.ds(other_at, rows), :] = other[...].astype(out.dtype)


def assemble(low, high, *pieces):
    rows, width = pieces[0].shape
    return pl.pallas_call(
        assemble_kernel,
        out_shape=jax.ShapeDtypeStruct((4 * rows, width), jnp.bfloat16),
        in_specs=[pl.BlockSpec(memory_space=pltpu.SMEM)]
        + [pl.BlockSpec(memory_space=pltpu.VMEM)] * 4,
        out_specs=pl.BlockSpec(memory_space=pltpu.VMEM),
        compiler_params=pltpu.CompilerParams(vmem_limit_bytes=32 * 1024 * 1024),
        name="assemble",
    )(jnp.stack([low, high]).astype(jnp.int32), *pieces)


def core_sum(partial):
    return partial + exchange(partial, "mp", swap_pairs(lax.axis_size("mp"), 1))


def dp_sum(values):
    dp_count = lax.axis_size("dp")
    if dp_count != 8:
        total = lax.psum(values, "dp")
        return total, jnp.sum(total * total) / dp_count
    place = lax.axis_index("dp")
    low, line = place % 2, place // 2
    inner = (line == 1) | (line == 2)
    beside = swap_pairs(8, 1)
    inward = [(0, 2), (1, 3), (6, 4), (7, 5)]
    outward = [(2, 0), (3, 1), (4, 6), (5, 7)]
    middle = [(2, 4), (4, 2), (3, 5), (5, 3)]
    beside_inner = [(2, 3), (3, 2), (4, 5), (5, 4)]
    rows = values.shape[0]
    half, quarter = rows // 2, rows // 4
    keep = lax.dynamic_slice_in_dim(values, low * quarter, quarter, 0)
    send = lax.dynamic_slice_in_dim(values, (1 - low) * quarter, quarter, 0)
    share = keep + exchange(send, "dp", beside)
    share = share + exchange(share, "dp", inward)
    share = share + exchange(share, "dp", middle)
    share = pick(inner, share, exchange(share, "dp", outward))
    squares = jnp.sum(share * share) / 4
    other = exchange(share, "dp", beside)
    upper = jnp.concatenate([pick(low == 0, share, other), pick(low == 0, other, share)], axis=0)
    block = values[half:]
    block = block + exchange(block, "dp", inward)
    side = line // 2
    keep = lax.dynamic_slice_in_dim(block, side * quarter, quarter, 0)
    send = lax.dynamic_slice_in_dim(block, (1 - side) * quarter, quarter, 0)
    share = keep + exchange(send, "dp", middle)
    share = share + exchange(share, "dp", beside_inner)
    squares = squares + jnp.where(inner, jnp.sum(share * share) / 2, 0.0)
    other = exchange(share, "dp", middle)
    block = jnp.concatenate([pick(side == 0, share, other), pick(side == 0, other, share)], axis=0)
    block = pick(inner, block, exchange(block, "dp", outward))
    return jnp.concatenate([upper, block], axis=0), squares


def norm_parts(hidden):
    centre = jnp.mean(hidden, axis=-1, keepdims=True)
    offset = hidden - centre
    spread = jnp.mean(offset * offset, axis=-1, keepdims=True)
    scale = lax.rsqrt(spread + eps_norm)
    return offset * scale, scale


def norm_back(grad, gain, normal, scale):
    scaled = grad * gain
    first = jnp.mean(scaled, axis=-1, keepdims=True)
    second = jnp.mean(scaled * normal, axis=-1, keepdims=True)
    return scale * (scaled - first - normal * second)


def dot_t(left, right):
    return lax.dot_general(left, right, (((1,), (1,)), ((), ())), preferred_element_type=jnp.float32)


def dot_n(left, right):
    return jnp.dot(left, right, preferred_element_type=jnp.float32)


def dot_over_rows(left, right):
    return lax.dot_general(left, right, (((0,), (0,)), ((), ())), preferred_element_type=jnp.float32)


def body(
    tokens,
    lengths,
    timesteps,
    cotangent,
    proj_input,
    proj_output,
    proj_upward,
    proj_downward,
    norm_params,
    input_mean,
    input_square,
    output_mean,
    output_square,
    upward_mean,
    upward_square,
    downward_mean,
    downward_square,
    norms_mean,
    norms_square,
):
    seq_count, seq_len, width = tokens.shape
    head_size = HEAD_DIM
    local = proj_output.shape[0]
    local_heads = local // head_size
    row_count = seq_count * seq_len
    mp_count = lax.axis_size("mp")
    half = jnp.bfloat16

    proj_input_t = jnp.transpose(proj_input, (1, 2, 0)).reshape(3 * local, width)
    with jax.named_scope("gather_weights"):
        attn_far = foreign_shard(jnp.concatenate([proj_input_t, proj_output], axis=0))
        up_far = foreign_shard(proj_upward)
        down_far = foreign_shard(proj_downward)
    in_far, out_far = attn_far[: 3 * local], attn_far[3 * local :]
    in_own, out_own = proj_input_t.astype(half), proj_output.astype(half)
    up_own, down_own = proj_upward.astype(half), proj_downward.astype(half)

    positions = lax.broadcasted_iota(jnp.int32, (seq_count, seq_len), 1)
    live_mask = (positions < lengths[:, None]).astype(jnp.float32)
    start = (tokens.astype(jnp.float32) + time_embed(timesteps, width)[:, None, :]).reshape(
        row_count, width
    )
    normal_one, scale_one = norm_parts(start)
    normed_one = (normal_one * norm_params[0] + norm_params[1]).astype(half)

    def front(weight_in):
        mixed = dot_t(normed_one, weight_in).astype(half)
        pieces = mixed.reshape(seq_count, seq_len, 3, local_heads, head_size)
        return pieces[:, :, 0], pieces[:, :, 1], pieces[:, :, 2]

    with jax.named_scope("attention_own"):
        queries, keyset, valueset = front(in_own)
        context, logsum = attend_forward(queries, keyset, valueset, live_mask)
        context = context.reshape(row_count, local)
        attended = dot_n(context, out_own)
    with jax.named_scope("attention_far"):
        far_context, unused = attend_forward(*front(in_far), live_mask)
        attended = attended + dot_n(far_context.reshape(row_count, local), out_far)
    middle = start + core_sum(attended)
    normal_two, scale_two = norm_parts(middle)
    normed_two = (normal_two * norm_params[2] + norm_params[3]).astype(half)
    grad_out = (cotangent * live_mask[:, :, None]).reshape(row_count, width)
    grad_down_in = grad_out.astype(half)

    def feed(weight_up, weight_down):
        upward = dot_n(normed_two, weight_up)
        activated = gelu_exact(upward).astype(half)
        grad_act = dot_t(grad_down_in, weight_down)
        unused_value, gelu_pull = jax.vjp(gelu_exact, upward)
        return activated, gelu_pull(grad_act)[0].astype(half)

    with jax.named_scope("feed_own"):
        activated, grad_rise = feed(up_own, down_own)
        grad_down_w = dot_over_rows(activated, grad_down_in)
        grad_up_w = dot_over_rows(normed_two, grad_rise)
        with jax.named_scope("sum_down"):
            grad_down_w, squares_down = dp_sum(grad_down_w)
        with jax.named_scope("sum_up"):
            grad_up_w, squares_up = dp_sum(grad_up_w)
        downward = dot_n(activated, down_own)
        entry_two = dot_t(grad_rise, up_own)
    with jax.named_scope("feed_far"):
        activated, grad_rise = feed(up_far, down_far)
        entry_two = entry_two + dot_t(grad_rise, up_far)
        downward = downward + dot_n(activated, down_far)
    entry_two = core_sum(entry_two)
    result = (middle + core_sum(downward)).reshape(seq_count, seq_len, width)
    grad_middle = grad_out + norm_back(entry_two, norm_params[2], normal_two, scale_two)
    grad_gain_two = jnp.sum(entry_two * normal_two, axis=0)
    grad_shift_two = jnp.sum(entry_two, axis=0)
    grad_attn = grad_middle.astype(half)
    with jax.named_scope("attention_back"):
        grad_context = dot_t(grad_attn, out_own).astype(half)
        grad_context = grad_context.reshape(seq_count, seq_len, local_heads, head_size)
        grad_query, grad_key, grad_value, unused = attend_back(
            queries, keyset, valueset, live_mask, logsum, grad_context
        )
        grad_out_w = dot_over_rows(context, grad_attn)
        grad_mixed = jnp.stack([grad_query, grad_key, grad_value], axis=2).reshape(
            row_count, 3 * local
        )
        grad_in_w = dot_over_rows(grad_mixed, normed_one)
        with jax.named_scope("sum_attn"):
            grad_attn_w, squares_attn = dp_sum(jnp.concatenate([grad_in_w, grad_out_w], axis=0))
        grad_in_w, grad_out_w = grad_attn_w[: 3 * local], grad_attn_w[3 * local :]
        entry_one = dot_n(grad_mixed, in_own)
    grad_gain_one = jnp.sum(entry_one * normal_one, axis=0)
    grad_shift_one = jnp.sum(entry_one, axis=0)
    with jax.named_scope("sum_entry_one"):
        side = lax.axis_index("mp") % 2
        piece = row_count // 2
        keep = lax.dynamic_slice_in_dim(entry_one, side * piece, piece, 0)
        send = lax.dynamic_slice_in_dim(entry_one, (1 - side) * piece, piece, 0)
        keep = keep + exchange(send, "mp", swap_pairs(mp_count, 1))
        keep = keep + exchange(keep, "mp", swap_pairs(mp_count, 2))
        other = exchange(keep, "mp", swap_pairs(mp_count, 1))
        entry_one = jnp.concatenate(
            [pick(side == 0, keep, other), pick(side == 0, other, keep)], axis=0
        )
    in_grad = grad_middle + norm_back(entry_one, norm_params[0], normal_one, scale_one)
    in_grad = in_grad.reshape(seq_count, seq_len, width)
    grad_norms = jnp.stack(
        [grad_gain_one, grad_shift_one, grad_gain_two / mp_count, grad_shift_two / mp_count]
    )
    grad_norms = lax.psum(grad_norms, ("dp", "mp"))
    squares = lax.psum(squares_down + squares_up + squares_attn, ("dp", "mp"))
    grad_norm = jnp.sqrt(squares + jnp.sum(grad_norms * grad_norms))
    threshold = clip_coeff * width * math.sqrt(lax.axis_size("dp") * row_count)
    factor = jnp.minimum(1.0, threshold / grad_norm)
    grad_in_w = jnp.transpose(grad_in_w.reshape(3, local, width), (2, 0, 1))
    in_m, in_v, in_w = adam_update(
        proj_input, grad_in_w * factor, input_mean, input_square, rate_inproj, decay_weight
    )
    out_m, out_v, out_w = adam_update(
        proj_output, grad_out_w * factor, output_mean, output_square, rate_outproj, decay_weight
    )
    up_m, up_v, up_w = adam_update(
        proj_upward, grad_up_w * factor, upward_mean, upward_square, rate_upproj, decay_weight
    )
    down_m, down_v, down_w = adam_update(
        proj_downward,
        grad_down_w * factor,
        downward_mean,
        downward_square,
        rate_downproj,
        decay_weight,
    )
    norm_m, norm_v, norm_w = adam_update(
        norm_params, grad_norms * factor, norms_mean, norms_square, rate_norms, 0.0
    )
    return (
        result,
        in_grad,
        grad_norm,
        in_m,
        in_v,
        in_w,
        in_w.astype(jnp.bfloat16),
        out_m,
        out_v,
        out_w,
        out_w.astype(jnp.bfloat16),
        up_m,
        up_v,
        up_w,
        up_w.astype(jnp.bfloat16),
        down_m,
        down_v,
        down_w,
        down_w.astype(jnp.bfloat16),
        norm_m,
        norm_v,
        norm_w,
    )


def solution(mesh):
    in_specs = (
        P("dp", None, None),
        P("dp"),
        P("dp"),
        P("dp", None, None),
        P(None, None, "mp"),
        P("mp", None),
        P(None, "mp"),
        P("mp", None),
        P(),
        P(None, None, "mp"),
        P(None, None, "mp"),
        P("mp", None),
        P("mp", None),
        P(None, "mp"),
        P(None, "mp"),
        P("mp", None),
        P("mp", None),
        P(),
        P(),
    )
    out_specs = (
        P("dp", None, None),
        P("dp", None, None),
        P(),
        P(None, None, "mp"),
        P(None, None, "mp"),
        P(None, None, "mp"),
        P(None, None, "mp"),
        P("mp", None),
        P("mp", None),
        P("mp", None),
        P("mp", None),
        P(None, "mp"),
        P(None, "mp"),
        P(None, "mp"),
        P(None, "mp"),
        P("mp", None),
        P("mp", None),
        P("mp", None),
        P("mp", None),
        P(),
        P(),
        P(),
    )
    return jax.shard_map(body, mesh=mesh, in_specs=in_specs, out_specs=out_specs, check_vma=False)
```

```python
import functools
import math

import jax
import jax.numpy as jnp
from jax import lax
from jax.experimental import pallas as pl
from jax.experimental.pallas import tpu as pltpu
from jax.sharding import PartitionSpec as P

HEAD_DIM = 64
STEP = 10


eps_norm = 1e-05
beta_one = 0.9
beta_two = 0.95
adam_eps = 1e-08
decay_weight = 0.1
clip_coeff = 0.03
rate_inproj = 0.07
rate_outproj = 0.3
rate_upproj = 0.07
rate_downproj = 0.05
rate_norms = 0.2
erf_upper = (
    0.00022905065861350646,
    0.0034082910107109506,
    0.050955695062380861,
    0.18520832239976145,
    1.128379143519084,
)
erf_lower = (
    -1.1791602954361697e-7,
    0.000023547966471313185,
    0.0010179625278914885,
    0.014070470171167667,
    0.11098505178285362,
    0.49746925110067538,
    1.0,
)

SEQS_STEP = 2


def time_embed(steps_given, width):
    halfway = width // 2
    counter = jnp.arange(halfway, dtype=jnp.float32)
    frequency = jnp.exp(-math.log(10000.0) * counter / halfway)
    angles = steps_given.astype(jnp.float32)[:, None] * frequency[None, :]
    return jnp.concatenate([jnp.sin(angles), jnp.cos(angles)], axis=-1)


def swap_pairs(count, bit):
    return [(i, i ^ bit) for i in range(count)]


def pick(flag, first, second):
    return jnp.where(flag, first, second)


def rows_dot(left, right):
    return jnp.dot(left, right, preferred_element_type=jnp.float32)


def last_dot(left, right):
    return lax.dot_general(left, right, (((1,), (1,)), ((), ())), preferred_element_type=jnp.float32)


def first_dot(left, right):
    return lax.dot_general(left, right, (((0,), (0,)), ((), ())), preferred_element_type=jnp.float32)


def norm_parts(hidden):
    centre = jnp.mean(hidden, axis=-1, keepdims=True)
    offset = hidden - centre
    spread = jnp.mean(offset * offset, axis=-1, keepdims=True)
    scale = lax.rsqrt(spread + eps_norm)
    return offset * scale, scale


def norm_back(grad, gain, normal, scale):
    scaled = grad * gain
    first = jnp.mean(scaled, axis=-1, keepdims=True)
    second = jnp.mean(scaled * normal, axis=-1, keepdims=True)
    return scale * (scaled - first - normal * second)


def flat_rows(values):
    return values.reshape(values.shape[0] * values.shape[1], values.shape[2])


def start_rows(tokens_ref, temb_ref):
    return flat_rows(tokens_ref[...].astype(jnp.float32) + temb_ref[...])


def grad_out_rows(lengths_ref, first_seq, cotangent_ref, block=None):
    seqs, seq_len, width = cotangent_ref.shape
    first = first_seq + (pl.program_id(0) if block is None else block) * seqs
    place = lax.broadcasted_iota(jnp.int32, (seq_len, width), 0)
    parts = [
        jnp.where(place < lengths_ref[first + s], cotangent_ref[s], 0.0) for s in range(seqs)
    ]
    return jnp.concatenate(parts, axis=0)


def head_masks(shape, heads):
    lanes = lax.broadcasted_iota(jnp.int32, shape, 1) // HEAD_DIM
    return [lanes == h for h in range(heads)]


def stack_heads(values, masks):
    return jnp.concatenate([jnp.where(m, values, jnp.zeros_like(values)) for m in masks], axis=0)


def merge_heads(values, masks):
    rows = values.shape[0] // len(masks)
    merged = jnp.zeros((rows, values.shape[1]), values.dtype)
    for h, mask in enumerate(masks):
        merged = jnp.where(mask, values[h * rows : (h + 1) * rows], merged)
    return merged


def soft_rows(stacked, keysets, lengths):
    scores = []
    for rows, keyset, length in zip(stacked, keysets, lengths):
        part = last_dot(rows, keyset) * HEAD_DIM ** (-0.5)
        live = lax.broadcasted_iota(jnp.int32, part.shape, 1) < length
        scores.append(jnp.where(live, part, -1000000000.0))
    scores = jnp.concatenate(scores, axis=0)
    raised = jnp.exp(scores - jnp.max(scores, axis=-1, keepdims=True))
    return raised * (1.0 / jnp.sum(raised, axis=-1, keepdims=True))


def split_seqs(values, seqs):
    rows = values.shape[0] // seqs
    return [values[s * rows : (s + 1) * rows] for s in range(seqs)]


def attend_block(lengths_ref, first_seq, normed, w_in, w_out, seqs, heads):
    pad = w_out.shape[0]
    mixed = rows_dot(normed, w_in[...]).astype(jnp.bfloat16)
    first = first_seq + pl.program_id(0) * seqs
    parts = split_seqs(mixed, seqs)
    masks = head_masks((parts[0].shape[0], pad), heads)
    soft = soft_rows(
        [stack_heads(part[:, :pad], masks) for part in parts],
        [part[:, pad : 2 * pad] for part in parts],
        [lengths_ref[first + s] for s in range(seqs)],
    ).astype(jnp.bfloat16)
    context = [
        merge_heads(rows_dot(probs, part[:, 2 * pad :]), masks)
        for probs, part in zip(split_seqs(soft, seqs), parts)
    ]
    context = jnp.concatenate(context, axis=0).astype(jnp.bfloat16)
    return mixed, context, rows_dot(context, w_out[...])


def front_own_kernel(
    heads, first_seq, lengths, tokens, temb, norms, w_in, w_out, mixed_out, normed_out, context_out, attended
):
    normal, unused = norm_parts(start_rows(tokens, temb))
    normed = (normal * norms[0:1] + norms[1:2]).astype(jnp.bfloat16)
    normed_out[...] = normed
    mixed, context, share = attend_block(
        lengths, first_seq, normed, w_in, w_out, tokens.shape[0], heads
    )
    mixed_out[...] = mixed
    context_out[...] = context
    attended[...] = share


def front_far_kernel(
    heads, seqs, first_seq, lengths, normed, w_in, w_out, own, attended, mixed_out
):
    mixed_out[...], unused, share = attend_block(
        lengths, first_seq, normed[...], w_in, w_out, seqs, heads
    )
    attended[...] = own[...] + share


def error_function(values):
    bounded = jnp.clip(values, -3.832506856900711, 3.832506856900711)
    square = bounded * bounded
    upper = jnp.full_like(square, erf_upper[0])
    for factor in erf_upper[1:]:
        upper = upper * square + factor
    lower = jnp.full_like(square, erf_lower[0])
    for factor in erf_lower[1:]:
        lower = lower * square + factor
    return bounded * upper / lower


def gelu_and_slope(values):
    scaled = values * math.sqrt(0.5)
    share = 0.5 + 0.5 * error_function(scaled)
    density = jnp.exp(-scaled * scaled) * (1.0 / math.sqrt(2.0 * math.pi))
    return values * share, share + values * density


def feed_block(normed, grad_down_in, up, up_t, down_t):
    upward = rows_dot(normed, up[...])
    activated, slope = gelu_and_slope(upward)
    grad_act = rows_dot(grad_down_in, down_t[...])
    grad_rise = (grad_act * slope).astype(jnp.bfloat16)
    return activated.astype(jnp.bfloat16), grad_rise, rows_dot(grad_rise, up_t[...])


def split_rows(flag, values, keep, send):
    rows = keep.shape[0]
    keep[...] = values[pl.ds(pl.multiple_of(flag * rows, 16), rows), :]
    send[...] = values[pl.ds(pl.multiple_of((1 - flag) * rows, 16), rows), :]


def feed_own_kernel(
    lengths,
    place,
    tokens,
    temb,
    attended_0,
    attended_1,
    received_0,
    received_1,
    cotangent,
    norms,
    up,
    up_t,
    down_t,
    middle_out,
    normed_out,
    grad_in_out,
    activated_out,
    entry,
    keep_down,
    send_down,
    keep_up,
    send_up,
    grad_down,
    grad_up,
):
    first = in_first_half()

    @pl.when(pl.program_id(0) == 0)
    def begin():
        grad_down[...] = jnp.zeros_like(grad_down)
        grad_up[...] = jnp.zeros_like(grad_up)

    attended = jnp.where(
        first, attended_0[...] + received_0[...], attended_1[...] + received_1[...]
    )
    middle = start_rows(tokens, temb) + attended
    middle_out[...] = middle
    normal, unused = norm_parts(middle)
    normed = (normal * norms[2:3] + norms[3:4]).astype(jnp.bfloat16)
    normed_out[...] = normed
    grad_down_in = grad_out_rows(lengths, 0, cotangent).astype(jnp.bfloat16)
    grad_in_out[...] = grad_down_in
    activated, grad_rise, share = feed_block(normed, grad_down_in, up, up_t, down_t)
    activated_out[...] = activated
    entry[...] = share
    grad_down[...] += first_dot(activated, grad_down_in)
    grad_up[...] += first_dot(normed, grad_rise)

    @pl.when(pl.program_id(0) == pl.num_programs(0) - 1)
    def write():
        split_rows(place[0], grad_down, keep_down, send_down)
        split_rows(place[1], grad_up, keep_up, send_up)


def feed_far_kernel(normed, grad_down_in, up, up_t, down_t, entry_own, activated_out, entry):
    activated, unused, share = feed_block(normed[...], grad_down_in[...], up, up_t, down_t)
    activated_out[...] = activated
    entry[...] = entry_own[...] + share


def in_first_half():
    return pl.program_id(0) < pl.num_programs(0) // 2


def down_kernel(own, far_0, far_1, down, down_far, out):
    far = jnp.where(in_first_half(), far_0[...], far_1[...])
    out[...] = rows_dot(own[...], down[...]) + rows_dot(far, down_far[...])


def result_kernel(middle, downward, received, result):
    result[...] = (middle[...] + (downward[...] + received[...])).reshape(result.shape)


def back_seqs(mixed, lengths, grad_context, heads, pad):
    seqs = len(lengths)
    parts = split_seqs(mixed, seqs)
    masks = head_masks((parts[0].shape[0], pad), heads)
    stacked = [stack_heads(part[:, :pad], masks) for part in parts]
    keysets = [part[:, pad : 2 * pad] for part in parts]
    soft = soft_rows(stacked, keysets, lengths)
    grad_stacked = [stack_heads(part, masks) for part in split_seqs(grad_context, seqs)]
    grad_probs = [last_dot(grad, part[:, 2 * pad :]) for grad, part in zip(grad_stacked, parts)]
    grad_probs = jnp.concatenate(grad_probs, axis=0)
    inner_sum = jnp.sum(soft * grad_probs, axis=-1, keepdims=True)
    grad_scores = split_seqs((soft * (grad_probs - inner_sum)).astype(jnp.bfloat16), seqs)
    probs = split_seqs(soft.astype(jnp.bfloat16), seqs)
    scaling = HEAD_DIM ** (-0.5)
    grads = []
    for s in range(seqs):
        grad_query = merge_heads(rows_dot(grad_scores[s], keysets[s]), masks) * scaling
        grad_key = first_dot(grad_scores[s], stacked[s]) * scaling
        grad_value = first_dot(probs[s], grad_stacked[s])
        grads.append(jnp.concatenate([grad_query, grad_key, grad_value], axis=1))
    return jnp.concatenate(grads, axis=0).astype(jnp.bfloat16)


def back_kernel(
    heads,
    first_seq,
    last,
    lengths,
    place,
    tokens,
    temb,
    cotangent,
    middle,
    entry,
    received,
    mixed,
    context,
    normed_one,
    norms,
    w_out_t,
    w_in_t,
    *rest,
):
    if last:
        old_in, old_out, old_norms = rest[:3]
        rest = rest[3:]
        pieces = rest[3:7]
    grad_middle_out, entry_out, grad_norms = rest[:3]
    grad_in, grad_out = rest[-2:]
    step = pl.program_id(0)
    seqs, seq_len, width = tokens.shape
    pad = context.shape[1]
    local = heads * HEAD_DIM

    @pl.when(step == 0)
    def begin():
        grad_in[...] = old_in[...] if last else jnp.zeros_like(grad_in)
        grad_out[...] = old_out[...] if last else jnp.zeros_like(grad_out)
        grad_norms[...] = old_norms[...] if last else jnp.zeros_like(grad_norms)

    entry_two = entry[...] + received[...]
    normal, scale = norm_parts(middle[...])
    grad_middle = grad_out_rows(lengths, first_seq, cotangent) + norm_back(
        entry_two, norms[2:3], normal, scale
    )
    grad_middle_out[...] = grad_middle
    grad_norms[2:3] += jnp.sum(entry_two * normal, axis=0, keepdims=True)
    grad_norms[3:4] += jnp.sum(entry_two, axis=0, keepdims=True)
    grad_attn = grad_middle.astype(jnp.bfloat16)
    grad_context = rows_dot(grad_attn, w_out_t[...]).astype(jnp.bfloat16)
    grad_out[...] += first_dot(context[...], grad_attn)
    found = [lengths[first_seq + step * seqs + s] for s in range(seqs)]
    grad_mixed = back_seqs(mixed[...], found, grad_context, heads, pad)
    grad_in[...] += first_dot(grad_mixed, normed_one[...])
    entry_one = rows_dot(grad_mixed, w_in_t[...])
    entry_out[...] = entry_one
    normal_one, unused = norm_parts(start_rows(tokens, temb))
    grad_norms[0:1] += jnp.sum(entry_one * normal_one, axis=0, keepdims=True)
    grad_norms[1:2] += jnp.sum(entry_one, axis=0, keepdims=True)

    if last:

        @pl.when(step == pl.num_programs(0) - 1)
        def write():
            parts = [grad_in.at[part * pad : part * pad + local] for part in range(3)]
            parts.append(grad_out.at[:local])
            for flag, pair, outs in (
                (place[0], parts[:2], pieces[:2]),
                (place[1], parts[2:], pieces[2:]),
            ):

                @pl.when(flag == 0)
                def straight():
                    outs[0][...] = pair[0][...]
                    outs[1][...] = pair[1][...]

                @pl.when(flag != 0)
                def crossed():
                    outs[0][...] = pair[1][...]
                    outs[1][...] = pair[0][...]


def back_far_kernel(
    heads, seqs, first_seq, lengths, grad_middle, mixed, entry, w_out_t, w_in_t, total
):
    pad = w_out_t.shape[1]
    grad_attn = grad_middle[...].astype(jnp.bfloat16)
    grad_context = rows_dot(grad_attn, w_out_t[...]).astype(jnp.bfloat16)
    first = first_seq + pl.program_id(0) * seqs
    found = [lengths[first + s] for s in range(seqs)]
    grad_mixed = back_seqs(mixed[...], found, grad_context, heads, pad)
    total[...] = entry[...] + rows_dot(grad_mixed, w_in_t[...])


def add_kernel(left, right, total):
    total[...] = left[...] + right[...]


def share_kernel(place, keep_a, got_a, keep_b, got_b, keep_a2, send_a2, keep_b2, send_b2, sums):
    rows = keep_a.shape[0]
    sums[:rows] = keep_a[...] + got_a[...]
    sums[rows:] = keep_b[...] + got_b[...]
    split_rows(place[1], sums.at[:rows], keep_a2, send_a2)
    split_rows(place[0], sums.at[rows:], keep_b2, send_b2)


def pair_kernel(keep_a, got_a, keep_b, got_b, both):
    rows = keep_a.shape[0]
    both[:rows] = keep_a[...] + got_a[...]
    both[rows : 2 * rows] = keep_b[...] + got_b[...]


def pair_small_kernel(mp_copies, keep_a, got_a, keep_b, got_b, norms, both):
    pair_kernel(keep_a, got_a, keep_b, got_b, both)
    rows = keep_a.shape[0]
    gains = lax.broadcasted_iota(jnp.int32, norms.shape, 0) < 2
    both[2 * rows :] = jnp.zeros((8, both.shape[1]), jnp.float32)
    both[2 * rows : 2 * rows + 4] = norms[...] * jnp.where(gains, 1.0, 1.0 / mp_copies)


def all_squares(values):
    columns = jnp.sum(values * values, axis=0, keepdims=True)
    return jnp.sum(columns, axis=1, keepdims=True)


def total_kernel(both, got, total_a, total_b, squares):
    rows = total_a.shape[0]
    total = both[...] + got[...]
    total_a[...] = total[:rows]
    total_b[...] = total[rows:]
    squares[...] = jnp.broadcast_to(all_squares(total), squares.shape)


def total_small_kernel(both, got, squares, *rest):
    total_a, total_b, small = rest[-3:]
    rows = (both.shape[0] - 8) // 2
    total_a[:rows] = both[:rows] + got[:rows]
    total_b[:rows] = both[rows : 2 * rows] + got[rows : 2 * rows]
    found = squares[:1, :1] + all_squares(total_a[:rows]) + all_squares(total_b[:rows])
    norms = both[2 * rows :] + got[2 * rows :]
    fifth = lax.broadcasted_iota(jnp.int32, norms.shape, 0) == 4
    small[...] = jnp.where(fifth, found, norms)
    total_a[rows:] = small[...]
    total_b[rows:] = small[...]


def place_rows(flag, own, got, out):
    rows = out.shape[0] // 2
    out[pl.ds(pl.multiple_of(flag * rows, 16), rows), :] = own[:rows]
    out[pl.ds(pl.multiple_of((1 - flag) * rows, 16), rows), :] = got[:rows]


def merge_kernel(place, own_a, got_a, own_b, got_b, out_a, out_b):
    place_rows(place[1], own_a, got_a, out_a)
    place_rows(place[0], own_b, got_b, out_b)


def merge_small_kernel(place, own_a, got_a, own_b, got_b, diagonal, out_a, out_b, small):
    merge_kernel(place, own_a, got_a, own_b, got_b, out_a, out_b)
    rows = own_a.shape[0] - 8
    small[...] = (own_a[rows:] + got_a[rows:]) + (got_b[rows:] + diagonal[...])


def clip_factor(small, threshold):
    squares = small[4:5, :1] + all_squares(small[:4])
    norm = jnp.sqrt(squares)
    return norm, jnp.minimum(1.0, threshold / norm)


def adam_step(weight, gradient, mean_old, square_old, rate, decay, outs):
    mean_new = beta_one * mean_old + (1.0 - beta_one) * gradient
    square_new = beta_two * square_old + (1.0 - beta_two) * gradient * gradient
    lower = jnp.sqrt(square_new * (1.0 / (1.0 - beta_two**STEP))) + adam_eps
    direction = mean_new * (1.0 / (1.0 - beta_one**STEP)) / lower
    weight_new = weight - rate * (direction + decay * weight)
    outs[0][...] = mean_new
    outs[1][...] = square_new
    outs[2][...] = weight_new
    if len(outs) > 3:
        outs[3][...] = weight_new.astype(outs[3].dtype)


def adam_kernel(threshold, flag, rate, place, small, own, got, weight, mean, square, *outs):
    unused, factor = clip_factor(small, threshold)
    mine = pl.program_id(0) // (pl.num_programs(0) // 2) == place[flag]
    gradient = jnp.where(mine, own[...], got[...]) * factor
    adam_step(weight[...], gradient, mean[...], square[...], rate, decay_weight, outs)


def adam_attn_kernel(
    threshold,
    place,
    small,
    own_a,
    got_a,
    own_b,
    got_b,
    in_weight,
    in_mean,
    in_square,
    out_weight,
    out_mean,
    out_square,
    norm_weight,
    norm_mean,
    norm_square,
    *outs,
):
    norm, factor = clip_factor(small, threshold)
    step = pl.program_id(0)

    @pl.when(step < 3)
    def inside():
        pick_a = jnp.where(step == place[0], own_a[...], got_a[...])
        pick_b = jnp.where(place[1] == 0, own_b[...], got_b[...])
        gradient = jnp.where(step < 2, pick_a, pick_b) * factor
        values = in_weight[...], gradient, in_mean[...], in_square[...]
        adam_step(*values, rate_inproj, decay_weight, outs[:4])

    @pl.when(step == 3)
    def outside():
        gradient = jnp.where(place[1] == 1, own_b[...], got_b[...]) * factor
        values = out_weight[...], gradient, out_mean[...], out_square[...]
        adam_step(*values, rate_outproj, decay_weight, outs[4:8])
        gradient = small[:4] * factor
        values = norm_weight[...], gradient, norm_mean[...], norm_square[...]
        adam_step(*values, rate_norms, 0.0, outs[8:11])
        outs[11][...] = jnp.broadcast_to(norm, outs[11].shape)


def finish_kernel(
    tokens, temb, middle_0, middle_1, entry_0, entry_1, got_0, got_1, norms, in_grad
):
    first = in_first_half()
    grad_middle = jnp.where(first, middle_0[...], middle_1[...])
    entry = jnp.where(first, entry_0[...], entry_1[...]) + jnp.where(first, got_0[...], got_1[...])
    normal, scale = norm_parts(start_rows(tokens, temb))
    total = grad_middle + norm_back(entry, norms[0:1], normal, scale)
    in_grad[...] = total.reshape(in_grad.shape)


def attn_weights_kernel(w_in, w_out, in_n, in_t, out_n, out_t):
    local = w_out.shape[0]
    pad = out_n.shape[0]
    half = jnp.bfloat16
    in_n[...] = jnp.zeros_like(in_n)
    in_t[...] = jnp.zeros_like(in_t)
    out_n[...] = jnp.zeros_like(out_n)
    out_t[...] = jnp.zeros_like(out_t)
    for part in range(3):
        piece = w_in[part * local : (part + 1) * local, :]
        in_t[part * pad : part * pad + local, :] = piece.astype(half)
        in_n[:, part * pad : part * pad + local] = piece.T.astype(half)
    out_n[:local, :] = w_out[...].astype(half)
    out_t[:, :local] = w_out[...].T.astype(half)


def attn_far_kernel(
    piece, own, beside, line, upper, lower, in_n, in_t, out_n, out_t, rows
):
    local = own.shape[0]
    pad = out_n.shape[0]
    half = jnp.bfloat16
    index = piece[0]
    rows[...] = jnp.zeros_like(rows)
    rows[index, :local] = own[...].astype(half)
    rows[index ^ 1, :local] = beside[...].astype(half)
    rows[index ^ 2, :local] = line[...].astype(half)
    rows[index ^ 3, : local // 2] = upper[...].astype(half)
    rows[index ^ 3, local // 2 : local] = lower[...].astype(half)
    for part in range(3):
        in_t[part * pad : (part + 1) * pad] = rows[part]
        in_n[:, part * pad : (part + 1) * pad] = rows[part].T
    out_n[...] = rows[3]
    out_t[...] = rows[3].T


def diagonal_kernel(beside, line, upper, lower):
    rows = upper.shape[0]
    upper[...] = line[:rows]
    lower[...] = beside[rows:]


def touch_kernel(*refs):
    refs[-1][...] = jnp.zeros_like(refs[-1])


def feed_weights_kernel(up, down, up_n, up_t, down_n, down_t):
    half = jnp.bfloat16
    for weight, straight, turned in ((up, up_n, up_t), (down, down_n, down_t)):
        value = weight[...].astype(half)
        straight[...] = value
        turned[...] = value.T


def feed_far_weights_kernel(piece, own, beside, line, upper, lower, *outs):
    half = jnp.bfloat16
    index = piece[0]
    rows = own.shape[0] // 2
    for which in range(2):
        straight, turned = outs[2 * which : 2 * which + 2]
        part = slice(which * rows, (which + 1) * rows)
        for place, got in ((index, own), (index ^ 1, beside), (index ^ 2, line)):
            straight[pl.ds(pl.multiple_of(place * rows, 16), rows), :] = got[part].astype(half)
        last = (upper, lower)[which]
        at = pl.multiple_of((index ^ 3) * rows, 16)
        straight[pl.ds(at, rows), :] = last[...].astype(half)
        turned[...] = straight[...].T


SCALARS = pl.BlockSpec(memory_space=pltpu.SMEM)
ANYWHERE = pl.BlockSpec(memory_space=pl.ANY)
WHOLE = pl.BlockSpec(memory_space=pltpu.VMEM)


def array(shape, dtype=jnp.float32):
    return jax.ShapeDtypeStruct(shape, dtype)


STAGE_COST = 10**12
class Chain:
    def __init__(self):
        self.token = None

    def __call__(
        self,
        kernel,
        args,
        in_specs,
        out_specs,
        out_shape,
        grid=(),
        scratch=(),
        scalars=(),
        vmem=20,
        ends_stage=False,
    ):
        args, in_specs, count = list(args), list(in_specs), len(args) + len(scalars)
        run = kernel
        if self.token is not None:
            args.append(self.token)
            in_specs.append(ANYWHERE)

            def run(*refs):
                return kernel(*refs[:count], *refs[count + 1 :])

        results = pl.pallas_call(
            run,
            grid_spec=pltpu.PrefetchScalarGridSpec(
                num_scalar_prefetch=len(scalars),
                grid=grid,
                in_specs=in_specs,
                out_specs=out_specs,
                scratch_shapes=list(scratch),
            ),
            out_shape=out_shape,
            compiler_params=pltpu.CompilerParams(vmem_limit_bytes=vmem * 1024 * 1024),
            cost_estimate=pl.CostEstimate(
                flops=10**12 if ends_stage else 1, bytes_accessed=1, transcendentals=0
            ),
            name=getattr(kernel, "func", kernel).__name__,
        )(*scalars, *args)
        leaves = jax.tree.leaves(results)
        self.token = min(leaves, key=lambda leaf: leaf.size * leaf.dtype.itemsize)
        return results


def body(
    tokens,
    lengths,
    timesteps,
    cotangent,
    proj_input,
    proj_output,
    proj_upward,
    proj_downward,
    norm_params,
    input_mean,
    input_square,
    output_mean,
    output_square,
    upward_mean,
    upward_square,
    downward_mean,
    downward_square,
    norms_mean,
    norms_square,
):
    seq_count, seq_len, width = tokens.shape
    local = proj_output.shape[0]
    hidden = proj_downward.shape[0]
    heads = local // HEAD_DIM
    rows = seq_count * seq_len
    dp_count, mp_count = lax.axis_size("dp"), lax.axis_size("mp")
    by_pairs = dp_count == 8
    pad = -(-local // 128) * 128
    half = jnp.bfloat16
    seqs = SEQS_STEP
    step_rows = seqs * seq_len
    steps = seq_count // seqs
    half_steps = steps // 2
    half_seqs = seq_count // 2
    half_rows = rows // 2
    more = 2 * seqs
    more_rows = more * seq_len
    more_steps = half_steps // 2
    quarter = hidden // 4
    threshold = clip_coeff * width * math.sqrt(dp_count * rows)
    own_place = lax.axis_index("dp")
    low, high = own_place % 2, (own_place // 2) % 2
    place = jnp.stack([low, high]).astype(jnp.int32)
    piece = (own_place % 4).astype(jnp.int32)[None]
    chain = Chain()

    def across(values):
        return lax.ppermute(values, "mp", swap_pairs(mp_count, 2))

    def core(values):
        return lax.ppermute(values, "mp", swap_pairs(mp_count, 1))

    def beside(values):
        return lax.ppermute(values, "dp", swap_pairs(dp_count, 1))

    def line(values):
        return lax.ppermute(values, "dp", swap_pairs(dp_count, 2))

    def far_line(values):
        return lax.ppermute(values, "dp", swap_pairs(dp_count, 4))

    def corner(values):
        return lax.ppermute(values, "dp", swap_pairs(dp_count, 3))

    def blocks(columns, offset=0, count=step_rows):
        return pl.BlockSpec((count, columns), lambda i, *_: (i + offset, 0))

    def near_blocks(columns):
        return pl.BlockSpec(
            (step_rows, columns), lambda i, *_: (jnp.minimum(i, half_steps - 1), 0)
        )

    def away_blocks(columns):
        return pl.BlockSpec(
            (step_rows, columns), lambda i, *_: (jnp.maximum(i - half_steps, 0), 0)
        )

    def fixed(*shape):
        return pl.BlockSpec(shape, lambda *_: (0,) * len(shape))

    def seq_blocks(middle, offset=0, count=seqs):
        return pl.BlockSpec((count, middle, width), lambda i, *_: (i + offset, 0, 0))

    wide = blocks(width)
    more_wide = blocks(width, 0, more_rows)
    norm_block = fixed(*norm_params.shape)
    temb = time_embed(timesteps, width)[:, None, :]
    input_t = jnp.transpose(proj_input, (1, 2, 0)).reshape(3 * local, width)

    def mine_of_four(parts):
        return pick(high == 0, pick(low == 0, *parts[:2]), pick(low == 0, *parts[2:]))

    def diagonal(beside_got, line_got, ends_stage):
        shapes = [array((beside_got.shape[0] // 2, width))] * 2
        upper, lower = chain(
            diagonal_kernel,
            (beside_got, line_got),
            [WHOLE] * 2,
            [WHOLE] * 2,
            shapes,
            ends_stage=ends_stage,
        )
        return beside(upper), line(lower)

    attn_parts = [input_t[i * local : (i + 1) * local] for i in range(3)] + [proj_output]
    feed_parts = [
        jnp.concatenate([w[i * quarter : (i + 1) * quarter] for w in (proj_upward, proj_downward)])
        for i in range(4)
    ]
    attn_got = across(mine_of_four(attn_parts))
    in_n, in_t, out_n, out_t = chain(
        attn_weights_kernel,
        (input_t, proj_output),
        [WHOLE] * 2,
        [WHOLE] * 4,
        [array((width, 3 * pad), half), array((3 * pad, width), half)]
        + [array((pad, width), half), array((width, pad), half)],
    )
    feed_got = across(mine_of_four(feed_parts))

    def front(part):
        start = part * more_steps
        return chain(
            functools.partial(front_own_kernel, heads, part * half_seqs),
            (tokens, temb, norm_params, in_n, out_n),
            [seq_blocks(seq_len, start, more), seq_blocks(1, start, more), norm_block]
            + [fixed(width, 3 * pad), fixed(pad, width)],
            [blocks(columns, 0, more_rows) for columns in (3 * pad, width, pad, width)],
            [array((half_rows, 3 * pad), half), array((half_rows, width), half)]
            + [array((half_rows, pad), half), array((half_rows, width))],
            grid=(more_steps,),
            scalars=(lengths,),
        )

    fronts = [front(0)]
    attn_y, attn_z = beside(attn_got), line(attn_got)
    chain(touch_kernel, (attn_got,), [ANYWHERE], WHOLE, array((8, 128)), ends_stage=True)
    fronts.append(front(1))
    attn_upper, attn_lower = diagonal(attn_y, attn_z, False)
    up_n, up_t, down_n, down_t = chain(
        feed_weights_kernel,
        (proj_upward, proj_downward),
        [WHOLE] * 2,
        [WHOLE] * 4,
        [array((width, hidden), half), array((hidden, width), half)]
        + [array((hidden, width), half), array((width, hidden), half)],
    )
    far_in, far_in_t, far_out, far_out_t = chain(
        attn_far_kernel,
        (attn_got, attn_y, attn_z, attn_upper, attn_lower),
        [WHOLE] * 5,
        [WHOLE] * 4,
        [array((width, 3 * pad), half), array((3 * pad, width), half)]
        + [array((pad, width), half), array((width, pad), half)],
        scratch=[pltpu.VMEM((4, pad, width), half)],
        scalars=(piece,),
        ends_stage=True,
    )
    feed_y, feed_z = beside(feed_got), line(feed_got)

    def far_front(part):
        unused, normed, unused_too, own = fronts[part]
        attended, mixed = chain(
            functools.partial(front_far_kernel, heads, more, part * half_seqs),
            (normed, far_in, far_out, own),
            [more_wide, fixed(width, 3 * pad), fixed(pad, width), more_wide],
            [more_wide, blocks(3 * pad, 0, more_rows)],
            [array((half_rows, width)), array((half_rows, 3 * pad), half)],
            grid=(more_steps,),
            scalars=(lengths,),
        )
        return attended, core(attended), mixed

    attended_0, attended_got_0, far_mixed_0 = far_front(0)
    attended_1, attended_got_1, far_mixed_1 = far_front(1)
    far_mixed = far_mixed_0, far_mixed_1
    feed_upper, feed_lower = diagonal(feed_y, feed_z, True)

    shared = [array((rows, width))] + [array((rows, width), half)] * 2
    shared += [array((rows, hidden), half), array((rows, width))]
    halves = [array((hidden // 2, width))] * 2 + [array((width // 2, hidden))] * 2
    middle, normed_two, grad_down_in, activated, entry, *grads = chain(
        feed_own_kernel,
        (tokens, temb, attended_0, attended_1, attended_got_0, attended_got_1)
        + (cotangent, norm_params, up_n, up_t, down_t),
        [seq_blocks(seq_len), seq_blocks(1)]
        + [near_blocks(width), away_blocks(width)] * 2
        + [seq_blocks(seq_len), norm_block]
        + [fixed(width, hidden), fixed(hidden, width), fixed(width, hidden)],
        [wide, wide, wide, blocks(hidden), wide] + [fixed(*shape.shape) for shape in halves],
        shared + halves,
        grid=(steps,),
        scratch=[pltpu.VMEM((hidden, width), jnp.float32), pltpu.VMEM((width, hidden), jnp.float32)],
        scalars=(lengths, place),
        vmem=40,
    )

    def send_pair(pair):
        keep_a, send_a, keep_b, send_b = pair
        return keep_a, beside(send_a), keep_b, line(send_b)

    def share_pair(pair, ends_stage):
        if not by_pairs:
            return pair
        size = array((pair[0].shape[0] // 2, width))
        keep_a, send_a, keep_b, send_b = chain(
            share_kernel,
            pair,
            [WHOLE] * 4,
            [WHOLE] * 4,
            [size] * 4,
            scratch=[pltpu.VMEM((4 * size.shape[0], width), jnp.float32)],
            scalars=(place,),
            ends_stage=ends_stage,
        )
        return keep_a, line(send_a), keep_b, beside(send_b)

    def merge_pair(pair, extra, kernel, *more_args):
        size = array((2 * (pair[0].shape[0] - extra), width))
        small = [array((extra, width))] if extra else []
        first, second, *rest = chain(
            kernel,
            (*pair, *more_args),
            [WHOLE] * (4 + len(more_args)),
            [WHOLE] * (2 + len(small)),
            [size] * 2 + small,
            scalars=(place,),
        )
        return (first, beside(first), second, line(second)), *rest

    def sum_plainly(pair):
        keep_a, send_a, keep_b, send_b = pair
        totals = []
        for flag, keep, send in ((low, keep_a, send_a), (high, keep_b, send_b)):
            whole = pick(flag == 0, jnp.concatenate([keep, send]), jnp.concatenate([send, keep]))
            total = lax.psum(whole, "dp")
            count = total.shape[0] // 2
            totals += [lax.dynamic_slice_in_dim(total, f * count, count) for f in (flag, 1 - flag)]
        return totals, sum(jnp.sum(total * total) for total in totals) / dp_count

    if by_pairs:
        grads = send_pair(grads)
    up_far_n, up_far_t, down_far_n, down_far_t = chain(
        feed_far_weights_kernel,
        (feed_got, feed_y, feed_z, feed_upper, feed_lower),
        [WHOLE] * 5,
        [WHOLE] * 4,
        [array((width, hidden), half), array((hidden, width), half)]
        + [array((hidden, width), half), array((width, hidden), half)],
        scalars=(piece,),
        ends_stage=True,
    )

    def far(part):
        offset = part * more_steps
        own = blocks(width, offset, more_rows)
        act, total = chain(
            feed_far_kernel,
            (normed_two, grad_down_in, up_far_n, up_far_t, down_far_t, entry),
            [own, own, fixed(width, hidden), fixed(hidden, width), fixed(width, hidden), own],
            [blocks(hidden, 0, more_rows), more_wide],
            [array((half_rows, hidden), half), array((half_rows, width))],
            grid=(more_steps,),
            vmem=24,
        )
        return act, total, core(total)

    far_0, far_1 = far(0), far(1)
    grads = share_pair(grads, True)

    def back(part, feed, before):
        start = part * half_steps
        mixed, normed_one, context, unused = fronts[part]
        shapes = [(3 * pad, width), (pad, width), norm_params.shape]
        last = before is not None
        ends = [(local, width)] * 4 if last else shapes[:2]
        return chain(
            functools.partial(back_kernel, heads, part * half_seqs, last),
            (tokens, temb, cotangent, middle, feed[1], feed[2], mixed, context, normed_one)
            + (norm_params, out_t, in_t)
            + (before if last else ()),
            [seq_blocks(seq_len, start), seq_blocks(1, start), seq_blocks(seq_len, start)]
            + [blocks(width, start), wide, wide, blocks(3 * pad), blocks(pad), wide]
            + [norm_block, fixed(width, pad), fixed(3 * pad, width)]
            + ([fixed(*shape) for shape in shapes] if last else []),
            [wide, wide, norm_block] + [fixed(*shape) for shape in ends],
            [array((half_rows, width))] * 2
            + [array(norm_params.shape)]
            + [array(shape) for shape in ends],
            grid=(half_steps,),
            scratch=[pltpu.VMEM(shape, jnp.float32) for shape in shapes[:2]] if last else (),
            scalars=(lengths, place),
            vmem=32,
        )

    grad_middle_0, entry_one_0, norms_0, in_0, out_0 = back(0, far_0, None)
    if by_pairs:
        both = chain(
            pair_kernel,
            grads,
            [WHOLE] * 4,
            WHOLE,
            array((2 * grads[0].shape[0], width)),
            ends_stage=True,
        )
        both_got = far_line(both)
    grad_middle_1, entry_one_1, grad_norms, *attn_grads = back(1, far_1, (in_0, out_0, norms_0))
    if by_pairs:
        attn_grads = send_pair(attn_grads)

    def back_far(part, grad_middle, own):
        total = chain(
            functools.partial(back_far_kernel, heads, more, part * half_seqs),
            (grad_middle, far_mixed[part], own, far_out_t, far_in_t),
            [more_wide, blocks(3 * pad, 0, more_rows), more_wide]
            + [fixed(width, pad), fixed(3 * pad, width)],
            more_wide,
            array((half_rows, width)),
            grid=(more_steps,),
            scalars=(lengths,),
        )
        return total, core(total)

    first_half = back_far(0, grad_middle_0, entry_one_0)
    second_half = back_far(1, grad_middle_1, entry_one_1)
    downward = chain(
        down_kernel,
        (activated, far_0[0], far_1[0], down_n, down_far_n),
        [blocks(hidden), near_blocks(hidden), away_blocks(hidden)] + [fixed(hidden, width)] * 2,
        wide,
        array((rows, width)),
        grid=(steps,),
    )
    downward_got = core(downward)
    if by_pairs:
        size = array((both.shape[0] // 2, width))
        first, second, squares = chain(
            total_kernel,
            (both, both_got),
            [WHOLE] * 2,
            [WHOLE] * 3,
            [size, size, array((8, 128))],
        )
        grads = first, line(first), second, beside(second)
        attn_grads = share_pair(attn_grads, True)
        (grads,) = merge_pair(grads, 0, merge_kernel)
        attn_both = chain(
            functools.partial(pair_small_kernel, mp_count),
            (*attn_grads, grad_norms),
            [WHOLE] * 5,
            WHOLE,
            array((2 * attn_grads[0].shape[0] + 8, width)),
        )
        attn_both_got = far_line(attn_both)
    result = chain(
        result_kernel,
        (middle, downward, downward_got),
        [wide] * 3,
        seq_blocks(seq_len),
        array(tokens.shape),
        grid=(steps,),
    )
    in_grad = chain(
        finish_kernel,
        (tokens, temb, grad_middle_0, grad_middle_1, first_half[0], second_half[0])
        + (first_half[1], second_half[1], norm_params),
        [seq_blocks(seq_len), seq_blocks(1)]
        + [near_blocks(width), away_blocks(width)] * 3
        + [norm_block],
        seq_blocks(seq_len),
        array(tokens.shape),
        grid=(steps,),
    )
    if by_pairs:
        size = array((attn_both.shape[0] // 2 + 4, width))
        first, second, small = chain(
            total_small_kernel,
            (attn_both, attn_both_got, squares, grads[1], grads[3]),
            [WHOLE] * 3 + [ANYWHERE] * 2,
            [WHOLE] * 3,
            [size, size, array((8, width))],
        )
        attn_grads = first, line(first), second, beside(second)
        attn_grads, small = merge_pair(attn_grads, 8, merge_small_kernel, corner(small))
        for move in (core, across):
            small = chain(
                add_kernel, (small, move(small)), [WHOLE] * 2, WHOLE, array(small.shape)
            )
    else:
        grads, squares = sum_plainly(grads)
        attn_grads, attn_squares = sum_plainly(attn_grads)
        shares = jnp.array([1.0, 1.0, 1.0 / mp_count, 1.0 / mp_count], jnp.float32)
        found = jnp.broadcast_to(squares + attn_squares, (4, width))
        small = jnp.concatenate([grad_norms * shares[:, None], found])
        small = lax.psum(small, ("dp", "mp"))

    def adam(flag, rate, own, got, weight, mean, square):
        count = weight.shape[0] // 4
        block = pl.BlockSpec((count, width), lambda i, *_: (i, 0))
        part = pl.BlockSpec((count, width), lambda i, *_: (lax.rem(i, 2), 0))
        return chain(
            functools.partial(adam_kernel, threshold, flag, rate),
            (small, own, got, weight, mean, square),
            [fixed(8, width), part, part] + [block] * 3,
            [block] * 4,
            [array(weight.shape)] * 3 + [array(weight.shape, half)],
            grid=(4,),
            scalars=(place,),
        )

    def turned(values):
        return jnp.transpose(values, (1, 2, 0)).reshape(3 * local, width)

    down_state = adam(
        0, rate_downproj, *grads[:2], proj_downward, downward_mean, downward_square
    )
    up_state = adam(1, rate_upproj, *grads[2:], proj_upward, upward_mean, upward_square)
    block = pl.BlockSpec((local, width), lambda i, *_: (jnp.minimum(i, 2), 0))
    one = fixed(local, width)
    states = chain(
        functools.partial(adam_attn_kernel, threshold),
        (small, *attn_grads)
        + (input_t, turned(input_mean), turned(input_square))
        + (proj_output, output_mean, output_square, norm_params, norms_mean, norms_square),
        [fixed(8, width)] + [one] * 4 + [block] * 3 + [one] * 3 + [norm_block] * 3,
        [block] * 4 + [one] * 4 + [norm_block] * 3 + [fixed(8, 128)],
        [array(input_t.shape)] * 3
        + [array(input_t.shape, half)]
        + [array(proj_output.shape)] * 3
        + [array(proj_output.shape, half)]
        + [array(norm_params.shape)] * 3
        + [array((8, 128))],
        grid=(4,),
        scalars=(place,),
        vmem=24,
    )
    in_state = [jnp.transpose(s.reshape(3, local, width), (2, 0, 1)) for s in states[:4]]
    grad_norm = states[11][0, 0]
    return (
        result,
        in_grad,
        grad_norm,
        *in_state,
        *states[4:8],
        *up_state,
        *down_state,
        *states[8:11],
    )


def solution(mesh):
    in_specs = (
        P("dp", None, None),
        P("dp"),
        P("dp"),
        P("dp", None, None),
        P(None, None, "mp"),
        P("mp", None),
        P(None, "mp"),
        P("mp", None),
        P(),
        P(None, None, "mp"),
        P(None, None, "mp"),
        P("mp", None),
        P("mp", None),
        P(None, "mp"),
        P(None, "mp"),
        P("mp", None),
        P("mp", None),
        P(),
        P(),
    )
    out_specs = (
        P("dp", None, None),
        P("dp", None, None),
        P(),
        P(None, None, "mp"),
        P(None, None, "mp"),
        P(None, None, "mp"),
        P(None, None, "mp"),
        P("mp", None),
        P("mp", None),
        P("mp", None),
        P("mp", None),
        P(None, "mp"),
        P(None, "mp"),
        P(None, "mp"),
        P(None, "mp"),
        P("mp", None),
        P("mp", None),
        P("mp", None),
        P("mp", None),
        P(),
        P(),
        P(),
    )
    return jax.shard_map(body, mesh=mesh, in_specs=in_specs, out_specs=out_specs, check_vma=False)
```

```python
import functools
import math

import jax
import jax.numpy as jnp
from jax import lax
from jax.experimental import pallas as pl
from jax.experimental.pallas import tpu as pltpu
from jax.sharding import PartitionSpec as P

HEAD_DIM = 64
STEP = 10


eps_norm = 1e-05
beta_one = 0.9
beta_two = 0.95
adam_eps = 1e-08
decay_weight = 0.1
clip_coeff = 0.03
rate_inproj = 0.07
rate_outproj = 0.3
rate_upproj = 0.07
rate_downproj = 0.05
rate_norms = 0.2
erf_upper = (
    0.00022905065861350646,
    0.0034082910107109506,
    0.050955695062380861,
    0.18520832239976145,
    1.128379143519084,
)
erf_lower = (
    -1.1791602954361697e-7,
    0.000023547966471313185,
    0.0010179625278914885,
    0.014070470171167667,
    0.11098505178285362,
    0.49746925110067538,
    1.0,
)

SEQS_STEP = 2


def time_embed(steps_given, width):
    halfway = width // 2
    counter = jnp.arange(halfway, dtype=jnp.float32)
    frequency = jnp.exp(-math.log(10000.0) * counter / halfway)
    angles = steps_given.astype(jnp.float32)[:, None] * frequency[None, :]
    return jnp.concatenate([jnp.sin(angles), jnp.cos(angles)], axis=-1)


def swap_pairs(count, bit):
    return [(i, i ^ bit) for i in range(count)]


def pick(flag, first, second):
    return jnp.where(flag, first, second)


def rows_dot(left, right):
    return jnp.dot(left, right, preferred_element_type=jnp.float32)


def last_dot(left, right):
    return lax.dot_general(left, right, (((1,), (1,)), ((), ())), preferred_element_type=jnp.float32)


def first_dot(left, right):
    return lax.dot_general(left, right, (((0,), (0,)), ((), ())), preferred_element_type=jnp.float32)


def norm_parts(hidden):
    centre = jnp.mean(hidden, axis=-1, keepdims=True)
    offset = hidden - centre
    spread = jnp.mean(offset * offset, axis=-1, keepdims=True)
    scale = lax.rsqrt(spread + eps_norm)
    return offset * scale, scale


def norm_back(grad, gain, normal, scale):
    scaled = grad * gain
    first = jnp.mean(scaled, axis=-1, keepdims=True)
    second = jnp.mean(scaled * normal, axis=-1, keepdims=True)
    return scale * (scaled - first - normal * second)


def flat_rows(values):
    return values.reshape(values.shape[0] * values.shape[1], values.shape[2])


def start_rows(tokens_ref, temb_ref):
    return flat_rows(tokens_ref[...].astype(jnp.float32) + temb_ref[...])


def grad_out_rows(lengths_ref, first_seq, cotangent_ref, block=None):
    seqs, seq_len, width = cotangent_ref.shape
    first = first_seq + (pl.program_id(0) if block is None else block) * seqs
    place = lax.broadcasted_iota(jnp.int32, (seq_len, width), 0)
    parts = [
        jnp.where(place < lengths_ref[first + s], cotangent_ref[s], 0.0) for s in range(seqs)
    ]
    return jnp.concatenate(parts, axis=0)


def head_masks(shape, heads):
    lanes = lax.broadcasted_iota(jnp.int32, shape, 1) // HEAD_DIM
    return [lanes == h for h in range(heads)]


def stack_heads(values, masks):
    return jnp.concatenate([jnp.where(m, values, jnp.zeros_like(values)) for m in masks], axis=0)


def merge_heads(values, masks):
    rows = values.shape[0] // len(masks)
    merged = jnp.zeros((rows, values.shape[1]), values.dtype)
    for h, mask in enumerate(masks):
        merged = jnp.where(mask, values[h * rows : (h + 1) * rows], merged)
    return merged


def soft_rows(stacked, keysets, lengths):
    scores = []
    for rows, keyset, length in zip(stacked, keysets, lengths):
        part = last_dot(rows, keyset) * HEAD_DIM ** (-0.5)
        live = lax.broadcasted_iota(jnp.int32, part.shape, 1) < length
        scores.append(jnp.where(live, part, -1000000000.0))
    scores = jnp.concatenate(scores, axis=0)
    raised = jnp.exp(scores - jnp.max(scores, axis=-1, keepdims=True))
    return raised * (1.0 / jnp.sum(raised, axis=-1, keepdims=True))


def split_seqs(values, seqs):
    rows = values.shape[0] // seqs
    return [values[s * rows : (s + 1) * rows] for s in range(seqs)]


def attend_block(lengths_ref, first_seq, normed, w_in, w_out, seqs, heads):
    pad = w_out.shape[0]
    mixed = rows_dot(normed, w_in[...]).astype(jnp.bfloat16)
    first = first_seq + pl.program_id(0) * seqs
    parts = split_seqs(mixed, seqs)
    masks = head_masks((parts[0].shape[0], pad), heads)
    soft = soft_rows(
        [stack_heads(part[:, :pad], masks) for part in parts],
        [part[:, pad : 2 * pad] for part in parts],
        [lengths_ref[first + s] for s in range(seqs)],
    ).astype(jnp.bfloat16)
    context = [
        merge_heads(rows_dot(probs, part[:, 2 * pad :]), masks)
        for probs, part in zip(split_seqs(soft, seqs), parts)
    ]
    context = jnp.concatenate(context, axis=0).astype(jnp.bfloat16)
    return mixed, context, rows_dot(context, w_out[...])


def front_own_kernel(
    heads, first_seq, lengths, tokens, temb, norms, w_in, w_out, mixed_out, normed_out, context_out, attended
):
    normal, unused = norm_parts(start_rows(tokens, temb))
    normed = (normal * norms[0:1] + norms[1:2]).astype(jnp.bfloat16)
    normed_out[...] = normed
    mixed, context, share = attend_block(
        lengths, first_seq, normed, w_in, w_out, tokens.shape[0], heads
    )
    mixed_out[...] = mixed
    context_out[...] = context
    attended[...] = share


def front_far_kernel(
    heads, seqs, first_seq, lengths, normed, w_in, w_out, own, attended, mixed_out
):
    mixed_out[...], unused, share = attend_block(
        lengths, first_seq, normed[...], w_in, w_out, seqs, heads
    )
    attended[...] = own[...] + share


def error_function(values):
    bounded = jnp.clip(values, -3.832506856900711, 3.832506856900711)
    square = bounded * bounded
    upper = jnp.full_like(square, erf_upper[0])
    for factor in erf_upper[1:]:
        upper = upper * square + factor
    lower = jnp.full_like(square, erf_lower[0])
    for factor in erf_lower[1:]:
        lower = lower * square + factor
    return bounded * upper / lower


def gelu_and_slope(values):
    scaled = values * math.sqrt(0.5)
    share = 0.5 + 0.5 * error_function(scaled)
    density = jnp.exp(-scaled * scaled) * (1.0 / math.sqrt(2.0 * math.pi))
    return values * share, share + values * density


def feed_block(normed, grad_down_in, up, up_t, down_t):
    upward = rows_dot(normed, up[...])
    activated, slope = gelu_and_slope(upward)
    grad_act = rows_dot(grad_down_in, down_t[...])
    grad_rise = (grad_act * slope).astype(jnp.bfloat16)
    return activated.astype(jnp.bfloat16), grad_rise, rows_dot(grad_rise, up_t[...])


def split_rows(flag, values, keep, send):
    rows = keep.shape[0]
    keep[...] = values[pl.ds(pl.multiple_of(flag * rows, 16), rows), :]
    send[...] = values[pl.ds(pl.multiple_of((1 - flag) * rows, 16), rows), :]


def feed_own_kernel(
    lengths,
    place,
    tokens,
    temb,
    attended_0,
    attended_1,
    received_0,
    received_1,
    cotangent,
    norms,
    up,
    up_t,
    down_t,
    middle_out,
    normed_out,
    grad_in_out,
    activated_out,
    entry,
    keep_down,
    send_down,
    keep_up,
    send_up,
    grad_down,
    grad_up,
):
    first = in_first_half()

    @pl.when(pl.program_id(0) == 0)
    def begin():
        grad_down[...] = jnp.zeros_like(grad_down)
        grad_up[...] = jnp.zeros_like(grad_up)

    attended = jnp.where(
        first, attended_0[...] + received_0[...], attended_1[...] + received_1[...]
    )
    middle = start_rows(tokens, temb) + attended
    middle_out[...] = middle
    normal, unused = norm_parts(middle)
    normed = (normal * norms[2:3] + norms[3:4]).astype(jnp.bfloat16)
    normed_out[...] = normed
    grad_down_in = grad_out_rows(lengths, 0, cotangent).astype(jnp.bfloat16)
    grad_in_out[...] = grad_down_in
    activated, grad_rise, share = feed_block(normed, grad_down_in, up, up_t, down_t)
    activated_out[...] = activated
    entry[...] = share
    grad_down[...] += first_dot(activated, grad_down_in)
    grad_up[...] += first_dot(normed, grad_rise)

    @pl.when(pl.program_id(0) == pl.num_programs(0) - 1)
    def write():
        split_rows(place[0], grad_down, keep_down, send_down)
        split_rows(place[1], grad_up, keep_up, send_up)


def feed_far_kernel(normed, grad_down_in, up, up_t, down_t, entry_own, activated_out, entry):
    activated, unused, share = feed_block(normed[...], grad_down_in[...], up, up_t, down_t)
    activated_out[...] = activated
    entry[...] = entry_own[...] + share


def in_first_half():
    return pl.program_id(0) < pl.num_programs(0) // 2


def result_kernel(middle, downward, received, result):
    result[...] = (middle[...] + (downward[0] + received[0])).reshape(result.shape)


def back_seqs(mixed, lengths, grad_context, heads, pad):
    seqs = len(lengths)
    parts = split_seqs(mixed, seqs)
    masks = head_masks((parts[0].shape[0], pad), heads)
    stacked = [stack_heads(part[:, :pad], masks) for part in parts]
    keysets = [part[:, pad : 2 * pad] for part in parts]
    soft = soft_rows(stacked, keysets, lengths)
    grad_stacked = [stack_heads(part, masks) for part in split_seqs(grad_context, seqs)]
    grad_probs = [last_dot(grad, part[:, 2 * pad :]) for grad, part in zip(grad_stacked, parts)]
    grad_probs = jnp.concatenate(grad_probs, axis=0)
    inner_sum = jnp.sum(soft * grad_probs, axis=-1, keepdims=True)
    grad_scores = split_seqs((soft * (grad_probs - inner_sum)).astype(jnp.bfloat16), seqs)
    probs = split_seqs(soft.astype(jnp.bfloat16), seqs)
    scaling = HEAD_DIM ** (-0.5)
    grads = []
    for s in range(seqs):
        grad_query = merge_heads(rows_dot(grad_scores[s], keysets[s]), masks) * scaling
        grad_key = first_dot(grad_scores[s], stacked[s]) * scaling
        grad_value = first_dot(probs[s], grad_stacked[s])
        grads.append(jnp.concatenate([grad_query, grad_key, grad_value], axis=1))
    return jnp.concatenate(grads, axis=0).astype(jnp.bfloat16)


def back_kernel(
    heads,
    first_seq,
    last,
    lengths,
    place,
    cotangent,
    middle,
    entry,
    received,
    mixed,
    context,
    normed_one,
    norms,
    w_out_t,
    *rest,
):
    if last:
        old_in, old_out, old_norms = rest[:3]
        rest = rest[3:]
        pieces = rest[3:7]
    grad_middle_out, grad_mixed_out, grad_norms = rest[:3]
    grad_in, grad_out = rest[-2:]
    step = pl.program_id(0)
    seqs, seq_len, width = cotangent.shape
    pad = context.shape[1]
    local = heads * HEAD_DIM

    @pl.when(step == 0)
    def begin():
        grad_in[...] = old_in[...] if last else jnp.zeros_like(grad_in)
        grad_out[...] = old_out[...] if last else jnp.zeros_like(grad_out)
        grad_norms[...] = old_norms[...] if last else jnp.zeros_like(grad_norms)

    entry_two = entry[...] + received[...]
    normal, scale = norm_parts(middle[...])
    grad_middle = grad_out_rows(lengths, first_seq, cotangent) + norm_back(
        entry_two, norms[2:3], normal, scale
    )
    grad_middle_out[...] = grad_middle
    grad_norms[2:3] += jnp.sum(entry_two * normal, axis=0, keepdims=True)
    grad_norms[3:4] += jnp.sum(entry_two, axis=0, keepdims=True)
    grad_attn = grad_middle.astype(jnp.bfloat16)
    grad_context = rows_dot(grad_attn, w_out_t[...]).astype(jnp.bfloat16)
    grad_out[...] += first_dot(context[...], grad_attn)
    found = [lengths[first_seq + step * seqs + s] for s in range(seqs)]
    grad_mixed = back_seqs(mixed[...], found, grad_context, heads, pad)
    grad_mixed_out[...] = grad_mixed
    grad_in[...] += first_dot(grad_mixed, normed_one[...])

    if last:

        @pl.when(step == pl.num_programs(0) - 1)
        def write():
            parts = [grad_in.at[part * pad : part * pad + local] for part in range(3)]
            parts.append(grad_out.at[:local])
            for flag, pair, outs in (
                (place[0], parts[:2], pieces[:2]),
                (place[1], parts[2:], pieces[2:]),
            ):

                @pl.when(flag == 0)
                def straight():
                    outs[0][...] = pair[0][...]
                    outs[1][...] = pair[1][...]

                @pl.when(flag != 0)
                def crossed():
                    outs[0][...] = pair[1][...]
                    outs[1][...] = pair[0][...]


def back_far_kernel(
    heads,
    lengths,
    tokens,
    temb,
    middle_0,
    middle_1,
    mixed_0,
    mixed_1,
    own_0,
    own_1,
    w_out_t,
    w_in_t,
    own_in_t,
    act,
    far_act_0,
    far_act_1,
    down,
    down_far,
    shares,
    grad_norms,
):
    @pl.when(pl.program_id(0) == 0)
    def begin():
        grad_norms[...] = jnp.zeros_like(grad_norms)

    first = in_first_half()
    seqs = tokens.shape[0]
    pad = w_out_t.shape[1]
    own = rows_dot(jnp.where(first, own_0[...], own_1[...]), own_in_t[...])
    normal, unused = norm_parts(start_rows(tokens, temb))
    grad_norms[0:1] += jnp.sum(own * normal, axis=0, keepdims=True)
    grad_norms[1:2] += jnp.sum(own, axis=0, keepdims=True)
    grad_attn = jnp.where(first, middle_0[...], middle_1[...]).astype(jnp.bfloat16)
    grad_context = rows_dot(grad_attn, w_out_t[...]).astype(jnp.bfloat16)
    found = [lengths[pl.program_id(0) * seqs + s] for s in range(seqs)]
    mixed = jnp.where(first, mixed_0[...], mixed_1[...])
    grad_mixed = back_seqs(mixed, found, grad_context, heads, pad)
    shares[0] = own + rows_dot(grad_mixed, w_in_t[...])
    far_act = jnp.where(first, far_act_0[...], far_act_1[...])
    shares[1] = rows_dot(act[...], down[...]) + rows_dot(far_act, down_far[...])


def add_kernel(left, right, total):
    total[...] = left[...] + right[...]


def share_kernel(place, keep_a, got_a, keep_b, got_b, keep_a2, send_a2, keep_b2, send_b2, sums):
    rows = keep_a.shape[0]
    sums[:rows] = keep_a[...] + got_a[...]
    sums[rows:] = keep_b[...] + got_b[...]
    split_rows(place[1], sums.at[:rows], keep_a2, send_a2)
    split_rows(place[0], sums.at[rows:], keep_b2, send_b2)


def pair_kernel(keep_a, got_a, keep_b, got_b, both):
    rows = keep_a.shape[0]
    both[:rows] = keep_a[...] + got_a[...]
    both[rows : 2 * rows] = keep_b[...] + got_b[...]


def pair_small_kernel(mp_copies, keep_a, got_a, keep_b, got_b, norms_one, norms_two, both):
    pair_kernel(keep_a, got_a, keep_b, got_b, both)
    rows = keep_a.shape[0]
    both[2 * rows :] = jnp.zeros((8, both.shape[1]), jnp.float32)
    both[2 * rows : 2 * rows + 4] = norms_one[...] + norms_two[...] * (1.0 / mp_copies)


def all_squares(values):
    columns = jnp.sum(values * values, axis=0, keepdims=True)
    return jnp.sum(columns, axis=1, keepdims=True)


def total_kernel(both, got, total_a, total_b, squares):
    rows = total_a.shape[0]
    total = both[...] + got[...]
    total_a[...] = total[:rows]
    total_b[...] = total[rows:]
    squares[...] = jnp.broadcast_to(all_squares(total), squares.shape)


def total_small_kernel(both, got, squares, *rest):
    total_a, total_b, small = rest[-3:]
    rows = (both.shape[0] - 8) // 2
    total_a[:rows] = both[:rows] + got[:rows]
    total_b[:rows] = both[rows : 2 * rows] + got[rows : 2 * rows]
    found = squares[:1, :1] + all_squares(total_a[:rows]) + all_squares(total_b[:rows])
    norms = both[2 * rows :] + got[2 * rows :]
    fifth = lax.broadcasted_iota(jnp.int32, norms.shape, 0) == 4
    small[...] = jnp.where(fifth, found, norms)
    total_a[rows:] = small[...]
    total_b[rows:] = small[...]


def place_rows(flag, own, got, out):
    rows = out.shape[0] // 2
    out[pl.ds(pl.multiple_of(flag * rows, 16), rows), :] = own[:rows]
    out[pl.ds(pl.multiple_of((1 - flag) * rows, 16), rows), :] = got[:rows]


def merge_kernel(place, own_a, got_a, own_b, got_b, out_a, out_b):
    place_rows(place[1], own_a, got_a, out_a)
    place_rows(place[0], own_b, got_b, out_b)


def merge_after_kernel(place, own_a, got_a, own_b, got_b, after_a, after_b, out_a, out_b):
    merge_kernel(place, own_a, got_a, own_b, got_b, out_a, out_b)


def merge_small_kernel(place, own_a, got_a, own_b, got_b, diagonal, out_a, out_b, small):
    merge_kernel(place, own_a, got_a, own_b, got_b, out_a, out_b)
    rows = own_a.shape[0] - 8
    small[...] = (own_a[rows:] + got_a[rows:]) + (got_b[rows:] + diagonal[...])


def clip_factor(small, threshold):
    squares = small[4:5, :1] + all_squares(small[:4])
    norm = jnp.sqrt(squares)
    return norm, jnp.minimum(1.0, threshold / norm)


def adam_step(weight, gradient, mean_old, square_old, rate, decay, outs):
    mean_new = beta_one * mean_old + (1.0 - beta_one) * gradient
    square_new = beta_two * square_old + (1.0 - beta_two) * gradient * gradient
    lower = jnp.sqrt(square_new * (1.0 / (1.0 - beta_two**STEP))) + adam_eps
    direction = mean_new * (1.0 / (1.0 - beta_one**STEP)) / lower
    weight_new = weight - rate * (direction + decay * weight)
    outs[0][...] = mean_new
    outs[1][...] = square_new
    outs[2][...] = weight_new
    if len(outs) > 3:
        outs[3][...] = weight_new.astype(outs[3].dtype)


def adam_feed_kernel(threshold, place, small, *refs):
    unused, factor = clip_factor(small, threshold)
    late = pl.program_id(0) // (pl.num_programs(0) // 2)
    for which, rate in enumerate((rate_downproj, rate_upproj)):
        own, got, weight, mean, square = refs[5 * which : 5 * which + 5]
        outs = refs[10 + 4 * which : 14 + 4 * which]
        gradient = jnp.where(late == place[which], own[...], got[...]) * factor
        adam_step(weight[...], gradient, mean[...], square[...], rate, decay_weight, outs)


def adam_attn_kernel(
    threshold,
    place,
    small,
    own_a,
    got_a,
    own_b,
    got_b,
    in_weight,
    in_mean,
    in_square,
    out_weight,
    out_mean,
    out_square,
    norm_weight,
    norm_mean,
    norm_square,
    *outs,
):
    norm, factor = clip_factor(small, threshold)
    step = pl.program_id(0)

    @pl.when(step < 3)
    def inside():
        pick_a = jnp.where(step == place[0], own_a[...], got_a[...])
        pick_b = jnp.where(place[1] == 0, own_b[...], got_b[...])
        gradient = jnp.where(step < 2, pick_a, pick_b) * factor
        values = in_weight[...], gradient, in_mean[...], in_square[...]
        adam_step(*values, rate_inproj, decay_weight, outs[:4])

    @pl.when(step == 3)
    def outside():
        gradient = jnp.where(place[1] == 1, own_b[...], got_b[...]) * factor
        values = out_weight[...], gradient, out_mean[...], out_square[...]
        adam_step(*values, rate_outproj, decay_weight, outs[4:8])
        gradient = small[:4] * factor
        values = norm_weight[...], gradient, norm_mean[...], norm_square[...]
        adam_step(*values, rate_norms, 0.0, outs[8:11])
        outs[11][...] = jnp.broadcast_to(norm, outs[11].shape)


def finish_kernel(tokens, temb, middle_0, middle_1, entry_one, received, norms, in_grad):
    grad_middle = jnp.where(in_first_half(), middle_0[...], middle_1[...])
    entry = entry_one[0] + received[0]
    normal, scale = norm_parts(start_rows(tokens, temb))
    total = grad_middle + norm_back(entry, norms[0:1], normal, scale)
    in_grad[...] = total.reshape(in_grad.shape)


def attn_weights_kernel(w_in, w_out, in_n, in_t, out_n, out_t):
    local = w_out.shape[0]
    pad = out_n.shape[0]
    half = jnp.bfloat16
    in_n[...] = jnp.zeros_like(in_n)
    in_t[...] = jnp.zeros_like(in_t)
    out_n[...] = jnp.zeros_like(out_n)
    out_t[...] = jnp.zeros_like(out_t)
    for part in range(3):
        piece = w_in[part * local : (part + 1) * local, :]
        in_t[part * pad : part * pad + local, :] = piece.astype(half)
        in_n[:, part * pad : part * pad + local] = piece.T.astype(half)
    out_n[:local, :] = w_out[...].astype(half)
    out_t[:, :local] = w_out[...].T.astype(half)


def attn_far_kernel(piece, own, beside, line, corner, in_n, in_t, out_n, out_t, rows):
    local = own.shape[0]
    pad = out_n.shape[0]
    half = jnp.bfloat16
    index = piece[0]
    rows[...] = jnp.zeros_like(rows)
    rows[index, :local] = own[...].astype(half)
    rows[index ^ 1, :local] = beside[...].astype(half)
    rows[index ^ 2, :local] = line[...].astype(half)
    rows[index ^ 3, :local] = corner[...].astype(half)
    for part in range(3):
        in_t[part * pad : (part + 1) * pad] = rows[part]
        in_n[:, part * pad : (part + 1) * pad] = rows[part].T
    out_n[...] = rows[3]
    out_t[...] = rows[3].T


def send_attn_kernel(piece, inside, inside_corner, outside, own, corner):
    for index, block, out in ((piece[0], inside, own), (piece[0] ^ 3, inside_corner, corner)):

        @pl.when(index < 3)
        def from_input():
            out[...] = block[...]

        @pl.when(index == 3)
        def from_output():
            out[...] = outside[...]


def send_feed_kernel(piece, up, down, up_corner, down_corner, own, corner):
    rows = up.shape[0]
    own[:rows] = up[...]
    own[rows:] = down[...]
    corner[:rows] = up_corner[...]
    corner[rows:] = down_corner[...]


def touch_kernel(*refs):
    refs[-1][...] = jnp.zeros_like(refs[-1])


def feed_weights_kernel(up, down, up_n, up_t, down_n, down_t):
    half = jnp.bfloat16
    for weight, straight, turned in ((up, up_n, up_t), (down, down_n, down_t)):
        value = weight[...].astype(half)
        straight[...] = value
        turned[...] = value.T


def feed_far_weights_kernel(piece, own, beside, line, corner, *outs):
    half = jnp.bfloat16
    index = piece[0]
    rows = own.shape[0] // 2
    pieces = (index, own), (index ^ 1, beside), (index ^ 2, line), (index ^ 3, corner)
    for which in range(2):
        straight, turned = outs[2 * which : 2 * which + 2]
        part = slice(which * rows, (which + 1) * rows)
        for place, got in pieces:
            straight[pl.ds(pl.multiple_of(place * rows, 16), rows), :] = got[part].astype(half)
        turned[...] = straight[...].T


SCALARS = pl.BlockSpec(memory_space=pltpu.SMEM)
ANYWHERE = pl.BlockSpec(memory_space=pl.ANY)
WHOLE = pl.BlockSpec(memory_space=pltpu.VMEM)


def array(shape, dtype=jnp.float32):
    return jax.ShapeDtypeStruct(shape, dtype)


STAGE_COST = 10**12
class Chain:
    def __init__(self):
        self.token = None

    def __call__(
        self,
        kernel,
        args,
        in_specs,
        out_specs,
        out_shape,
        grid=(),
        scratch=(),
        scalars=(),
        vmem=20,
        ends_stage=False,
    ):
        args, in_specs, count = list(args), list(in_specs), len(args) + len(scalars)
        run = kernel
        if self.token is not None:
            args.append(self.token)
            in_specs.append(ANYWHERE)

            def run(*refs):
                return kernel(*refs[:count], *refs[count + 1 :])

        results = pl.pallas_call(
            run,
            grid_spec=pltpu.PrefetchScalarGridSpec(
                num_scalar_prefetch=len(scalars),
                grid=grid,
                in_specs=in_specs,
                out_specs=out_specs,
                scratch_shapes=list(scratch),
            ),
            out_shape=out_shape,
            compiler_params=pltpu.CompilerParams(vmem_limit_bytes=vmem * 1024 * 1024),
            cost_estimate=pl.CostEstimate(
                flops=10**12 if ends_stage else 1, bytes_accessed=1, transcendentals=0
            ),
            name=getattr(kernel, "func", kernel).__name__,
        )(*scalars, *args)
        leaves = jax.tree.leaves(results)
        self.token = min(leaves, key=lambda leaf: leaf.size * leaf.dtype.itemsize)
        return results


def body(
    tokens,
    lengths,
    timesteps,
    cotangent,
    proj_input,
    proj_output,
    proj_upward,
    proj_downward,
    norm_params,
    input_mean,
    input_square,
    output_mean,
    output_square,
    upward_mean,
    upward_square,
    downward_mean,
    downward_square,
    norms_mean,
    norms_square,
):
    seq_count, seq_len, width = tokens.shape
    local = proj_output.shape[0]
    hidden = proj_downward.shape[0]
    heads = local // HEAD_DIM
    rows = seq_count * seq_len
    dp_count, mp_count = lax.axis_size("dp"), lax.axis_size("mp")
    by_pairs = dp_count == 8
    pad = -(-local // 128) * 128
    half = jnp.bfloat16
    seqs = SEQS_STEP
    step_rows = seqs * seq_len
    steps = seq_count // seqs
    half_steps = steps // 2
    half_seqs = seq_count // 2
    half_rows = rows // 2
    more = 2 * seqs
    more_rows = more * seq_len
    more_steps = half_steps // 2
    quarter = hidden // 4
    threshold = clip_coeff * width * math.sqrt(dp_count * rows)
    own_place = lax.axis_index("dp")
    low, high = own_place % 2, (own_place // 2) % 2
    place = jnp.stack([low, high]).astype(jnp.int32)
    piece = (own_place % 4).astype(jnp.int32)[None]
    chain = Chain()

    def across(values):
        return lax.ppermute(values, "mp", swap_pairs(mp_count, 2))

    def core(values):
        return lax.ppermute(values, "mp", swap_pairs(mp_count, 1))

    def beside(values):
        return lax.ppermute(values, "dp", swap_pairs(dp_count, 1))

    def line(values):
        return lax.ppermute(values, "dp", swap_pairs(dp_count, 2))

    def far_line(values):
        return lax.ppermute(values, "dp", swap_pairs(dp_count, 4))

    def corner(values):
        return lax.ppermute(values, "dp", swap_pairs(dp_count, 3))

    def blocks(columns, offset=0, count=step_rows):
        return pl.BlockSpec((count, columns), lambda i, *_: (i + offset, 0))

    def near_blocks(columns):
        return pl.BlockSpec(
            (step_rows, columns), lambda i, *_: (jnp.minimum(i, half_steps - 1), 0)
        )

    def away_blocks(columns):
        return pl.BlockSpec(
            (step_rows, columns), lambda i, *_: (jnp.maximum(i - half_steps, 0), 0)
        )

    def fixed(*shape):
        return pl.BlockSpec(shape, lambda *_: (0,) * len(shape))

    def seq_blocks(middle, offset=0, count=seqs):
        return pl.BlockSpec((count, middle, width), lambda i, *_: (i + offset, 0, 0))

    wide = blocks(width)
    more_wide = blocks(width, 0, more_rows)
    norm_block = fixed(*norm_params.shape)
    temb = time_embed(timesteps, width)[:, None, :]
    input_t = jnp.transpose(proj_input, (1, 2, 0)).reshape(3 * local, width)

    def piece_block(count, flip, most=3):
        def index(i, piece):
            return (jnp.minimum(piece[0] ^ flip, most), 0)

        return pl.BlockSpec((count, width), index)

    attn_sends = chain(
        send_attn_kernel,
        (input_t, input_t, proj_output),
        [piece_block(local, 0, 2), piece_block(local, 3, 2), fixed(local, width)],
        [fixed(local, width)] * 2,
        [array((local, width))] * 2,
        grid=(1,),
        scalars=(piece,),
    )
    attn_got, attn_corner = [across(values) for values in attn_sends]
    in_n, in_t, out_n, out_t = chain(
        attn_weights_kernel,
        (input_t, proj_output),
        [WHOLE] * 2,
        [WHOLE] * 4,
        [array((width, 3 * pad), half), array((3 * pad, width), half)]
        + [array((pad, width), half), array((width, pad), half)],
    )

    def front(part):
        start = part * more_steps
        return chain(
            functools.partial(front_own_kernel, heads, part * half_seqs),
            (tokens, temb, norm_params, in_n, out_n),
            [seq_blocks(seq_len, start, more), seq_blocks(1, start, more), norm_block]
            + [fixed(width, 3 * pad), fixed(pad, width)],
            [blocks(columns, 0, more_rows) for columns in (3 * pad, width, pad, width)],
            [array((half_rows, 3 * pad), half), array((half_rows, width), half)]
            + [array((half_rows, pad), half), array((half_rows, width))],
            grid=(more_steps,),
            scalars=(lengths,),
        )

    fronts = [front(0)]
    attn_y, attn_z = beside(attn_got), line(attn_got)
    chain(touch_kernel, (attn_got,), [ANYWHERE], WHOLE, array((8, 128)), ends_stage=True)
    feed_sends = chain(
        send_feed_kernel,
        (proj_upward, proj_downward, proj_upward, proj_downward),
        [piece_block(quarter, 0)] * 2 + [piece_block(quarter, 3)] * 2,
        [fixed(2 * quarter, width)] * 2,
        [array((2 * quarter, width))] * 2,
        grid=(1,),
        scalars=(piece,),
    )
    feed_got, feed_corner = [across(values) for values in feed_sends]
    fronts.append(front(1))
    up_n, up_t, down_n, down_t = chain(
        feed_weights_kernel,
        (proj_upward, proj_downward),
        [WHOLE] * 2,
        [WHOLE] * 4,
        [array((width, hidden), half), array((hidden, width), half)]
        + [array((hidden, width), half), array((width, hidden), half)],
    )
    far_in, far_in_t, far_out, far_out_t = chain(
        attn_far_kernel,
        (attn_got, attn_y, attn_z, attn_corner),
        [WHOLE] * 4,
        [WHOLE] * 4,
        [array((width, 3 * pad), half), array((3 * pad, width), half)]
        + [array((pad, width), half), array((width, pad), half)],
        scratch=[pltpu.VMEM((4, pad, width), half)],
        scalars=(piece,),
        ends_stage=True,
    )

    def far_front(part):
        unused, normed, unused_too, own = fronts[part]
        attended, mixed = chain(
            functools.partial(front_far_kernel, heads, more, part * half_seqs),
            (normed, far_in, far_out, own),
            [more_wide, fixed(width, 3 * pad), fixed(pad, width), more_wide],
            [more_wide, blocks(3 * pad, 0, more_rows)],
            [array((half_rows, width)), array((half_rows, 3 * pad), half)],
            grid=(more_steps,),
            scalars=(lengths,),
        )
        return attended, core(attended), mixed

    attended_0, attended_got_0, far_mixed_0 = far_front(0)
    attended_1, attended_got_1, far_mixed_1 = far_front(1)
    far_mixed = far_mixed_0, far_mixed_1
    feed_y, feed_z = beside(feed_got), line(feed_got)
    chain(touch_kernel, (feed_got,), [ANYWHERE], WHOLE, array((8, 128)), ends_stage=True)

    shared = [array((rows, width))] + [array((rows, width), half)] * 2
    shared += [array((rows, hidden), half), array((rows, width))]
    halves = [array((hidden // 2, width))] * 2 + [array((width // 2, hidden))] * 2
    middle, normed_two, grad_down_in, activated, entry, *grads = chain(
        feed_own_kernel,
        (tokens, temb, attended_0, attended_1, attended_got_0, attended_got_1)
        + (cotangent, norm_params, up_n, up_t, down_t),
        [seq_blocks(seq_len), seq_blocks(1)]
        + [near_blocks(width), away_blocks(width)] * 2
        + [seq_blocks(seq_len), norm_block]
        + [fixed(width, hidden), fixed(hidden, width), fixed(width, hidden)],
        [wide, wide, wide, blocks(hidden), wide] + [fixed(*shape.shape) for shape in halves],
        shared + halves,
        grid=(steps,),
        scratch=[pltpu.VMEM((hidden, width), jnp.float32), pltpu.VMEM((width, hidden), jnp.float32)],
        scalars=(lengths, place),
        vmem=40,
    )

    def send_pair(pair):
        keep_a, send_a, keep_b, send_b = pair
        return keep_a, beside(send_a), keep_b, line(send_b)

    def share_pair(pair, ends_stage):
        if not by_pairs:
            return pair
        size = array((pair[0].shape[0] // 2, width))
        keep_a, send_a, keep_b, send_b = chain(
            share_kernel,
            pair,
            [WHOLE] * 4,
            [WHOLE] * 4,
            [size] * 4,
            scratch=[pltpu.VMEM((4 * size.shape[0], width), jnp.float32)],
            scalars=(place,),
            ends_stage=ends_stage,
        )
        return keep_a, line(send_a), keep_b, beside(send_b)

    def merge_pair(pair, extra, kernel, more_args, spec):
        size = array((2 * (pair[0].shape[0] - extra), width))
        small = [array((extra, width))] if extra else []
        first, second, *rest = chain(
            kernel,
            (*pair, *more_args),
            [WHOLE] * 4 + [spec] * len(more_args),
            [WHOLE] * (2 + len(small)),
            [size] * 2 + small,
            scalars=(place,),
        )
        return (first, beside(first), second, line(second)), *rest

    def sum_plainly(pair):
        keep_a, send_a, keep_b, send_b = pair
        totals = []
        for flag, keep, send in ((low, keep_a, send_a), (high, keep_b, send_b)):
            whole = pick(flag == 0, jnp.concatenate([keep, send]), jnp.concatenate([send, keep]))
            total = lax.psum(whole, "dp")
            count = total.shape[0] // 2
            totals += [lax.dynamic_slice_in_dim(total, f * count, count) for f in (flag, 1 - flag)]
        return totals, sum(jnp.sum(total * total) for total in totals) / dp_count

    if by_pairs:
        grads = send_pair(grads)
    up_far_n, up_far_t, down_far_n, down_far_t = chain(
        feed_far_weights_kernel,
        (feed_got, feed_y, feed_z, feed_corner),
        [WHOLE] * 4,
        [WHOLE] * 4,
        [array((width, hidden), half), array((hidden, width), half)]
        + [array((hidden, width), half), array((width, hidden), half)],
        scalars=(piece,),
        ends_stage=True,
    )

    def far(part):
        offset = part * more_steps
        own = blocks(width, offset, more_rows)
        act, total = chain(
            feed_far_kernel,
            (normed_two, grad_down_in, up_far_n, up_far_t, down_far_t, entry),
            [own, own, fixed(width, hidden), fixed(hidden, width), fixed(width, hidden), own],
            [blocks(hidden, 0, more_rows), more_wide],
            [array((half_rows, hidden), half), array((half_rows, width))],
            grid=(more_steps,),
            vmem=24,
        )
        return act, total, core(total)

    far_0, far_1 = far(0), far(1)
    grads = share_pair(grads, True)

    def back(part, feed, before):
        start = part * half_steps
        mixed, normed_one, context, unused = fronts[part]
        shapes = [(3 * pad, width), (pad, width), norm_params.shape]
        last = before is not None
        ends = [(local, width)] * 4 if last else shapes[:2]
        return chain(
            functools.partial(back_kernel, heads, part * half_seqs, last),
            (cotangent, middle, feed[1], feed[2], mixed, context, normed_one, norm_params, out_t)
            + (before if last else ()),
            [seq_blocks(seq_len, start), blocks(width, start), wide, wide]
            + [blocks(3 * pad), blocks(pad), wide, norm_block, fixed(width, pad)]
            + ([fixed(*shape) for shape in shapes] if last else []),
            [wide, blocks(3 * pad), norm_block] + [fixed(*shape) for shape in ends],
            [array((half_rows, width)), array((half_rows, 3 * pad), half)]
            + [array(norm_params.shape)]
            + [array(shape) for shape in ends],
            grid=(half_steps,),
            scratch=[pltpu.VMEM(shape, jnp.float32) for shape in shapes[:2]] if last else (),
            scalars=(lengths, place),
            vmem=32,
        )

    grad_middle_0, grad_mixed_0, norms_0, in_0, out_0 = back(0, far_0, None)
    if by_pairs:
        both = chain(
            pair_kernel,
            grads,
            [WHOLE] * 4,
            WHOLE,
            array((2 * grads[0].shape[0], width)),
            ends_stage=True,
        )
        both_got = far_line(both)
    grad_middle_1, grad_mixed_1, norms_two, *attn_grads = back(1, far_1, (in_0, out_0, norms_0))
    if by_pairs:
        attn_grads = send_pair(attn_grads)

    def more_halves(columns):
        return [
            pl.BlockSpec((more_rows, columns), lambda i, *_: (jnp.minimum(i, more_steps - 1), 0)),
            pl.BlockSpec((more_rows, columns), lambda i, *_: (jnp.maximum(i - more_steps, 0), 0)),
        ]

    shares, norms_one = chain(
        functools.partial(back_far_kernel, heads),
        (tokens, temb, grad_middle_0, grad_middle_1, *far_mixed, grad_mixed_0, grad_mixed_1)
        + (far_out_t, far_in_t, in_t, activated, far_0[0], far_1[0], down_n, down_far_n),
        [seq_blocks(seq_len, 0, more), seq_blocks(1, 0, more)]
        + more_halves(width)
        + more_halves(3 * pad) * 2
        + [fixed(width, pad), fixed(3 * pad, width), fixed(3 * pad, width)]
        + [blocks(hidden, 0, more_rows)]
        + more_halves(hidden)
        + [fixed(hidden, width)] * 2,
        [pl.BlockSpec((2, more_rows, width), lambda i, *_: (0, i, 0)), norm_block],
        [array((2, rows, width)), array(norm_params.shape)],
        grid=(2 * more_steps,),
        scalars=(lengths,),
        vmem=52,
    )
    shares_got = core(shares)

    def share_blocks(which):
        return pl.BlockSpec((1, step_rows, width), lambda i, *_: (which, i, 0))

    if by_pairs:
        size = array((both.shape[0] // 2, width))
        first, second, squares = chain(
            total_kernel,
            (both, both_got),
            [WHOLE] * 2,
            [WHOLE] * 3,
            [size, size, array((8, 128))],
        )
        grads = first, line(first), second, beside(second)
        attn_grads = share_pair(attn_grads, True)
        (grads,) = merge_pair(grads, 0, merge_after_kernel, attn_grads[1::2], ANYWHERE)
        attn_both = chain(
            functools.partial(pair_small_kernel, mp_count),
            (*attn_grads, norms_one, norms_two),
            [WHOLE] * 6,
            WHOLE,
            array((2 * attn_grads[0].shape[0] + 8, width)),
        )
        attn_both_got = far_line(attn_both)
    result = chain(
        result_kernel,
        (middle, shares, shares_got),
        [wide, share_blocks(1), share_blocks(1)],
        seq_blocks(seq_len),
        array(tokens.shape),
        grid=(steps,),
    )
    in_grad = chain(
        finish_kernel,
        (tokens, temb, grad_middle_0, grad_middle_1, shares, shares_got, norm_params),
        [seq_blocks(seq_len), seq_blocks(1), near_blocks(width), away_blocks(width)]
        + [share_blocks(0), share_blocks(0), norm_block],
        seq_blocks(seq_len),
        array(tokens.shape),
        grid=(steps,),
    )
    if by_pairs:
        size = array((attn_both.shape[0] // 2 + 4, width))
        first, second, small = chain(
            total_small_kernel,
            (attn_both, attn_both_got, squares, grads[1], grads[3]),
            [WHOLE] * 3 + [ANYWHERE] * 2,
            [WHOLE] * 3,
            [size, size, array((8, width))],
        )
        attn_grads = first, line(first), second, beside(second)
        attn_grads, small = merge_pair(
            attn_grads, 8, merge_small_kernel, (corner(small),), WHOLE
        )
        for move in (core, across):
            small = chain(
                add_kernel, (small, move(small)), [WHOLE] * 2, WHOLE, array(small.shape)
            )
    else:
        grads, squares = sum_plainly(grads)
        attn_grads, attn_squares = sum_plainly(attn_grads)
        found = jnp.broadcast_to(squares + attn_squares, (4, width))
        small = jnp.concatenate([norms_one + norms_two / mp_count, found])
        small = lax.psum(small, ("dp", "mp"))

    def turned(values):
        return jnp.transpose(values, (1, 2, 0)).reshape(3 * local, width)

    weights = proj_downward, proj_upward
    moments = (downward_mean, downward_square), (upward_mean, upward_square)
    args, specs, outs, shapes = [small], [fixed(8, width)], [], []
    for which, weight in enumerate(weights):
        count = weight.shape[0] // 4
        block = pl.BlockSpec((count, width), lambda i, *_: (i, 0))
        part = pl.BlockSpec((count, width), lambda i, *_: (lax.rem(i, 2), 0))
        args += [*grads[2 * which : 2 * which + 2], weight, *moments[which]]
        specs += [part] * 2 + [block] * 3
        outs += [block] * 4
        shapes += [array(weight.shape)] * 3 + [array(weight.shape, half)]
    feed_states = chain(
        functools.partial(adam_feed_kernel, threshold),
        args,
        specs,
        outs,
        shapes,
        grid=(4,),
        scalars=(place,),
        vmem=32,
    )
    block = pl.BlockSpec((local, width), lambda i, *_: (jnp.minimum(i, 2), 0))
    one = fixed(local, width)
    states = chain(
        functools.partial(adam_attn_kernel, threshold),
        (small, *attn_grads)
        + (input_t, turned(input_mean), turned(input_square))
        + (proj_output, output_mean, output_square, norm_params, norms_mean, norms_square),
        [fixed(8, width)] + [one] * 4 + [block] * 3 + [one] * 3 + [norm_block] * 3,
        [block] * 4 + [one] * 4 + [norm_block] * 3 + [fixed(8, 128)],
        [array(input_t.shape)] * 3
        + [array(input_t.shape, half)]
        + [array(proj_output.shape)] * 3
        + [array(proj_output.shape, half)]
        + [array(norm_params.shape)] * 3
        + [array((8, 128))],
        grid=(4,),
        scalars=(place,),
        vmem=24,
    )
    in_state = [jnp.transpose(s.reshape(3, local, width), (2, 0, 1)) for s in states[:4]]
    grad_norm = states[11][0, 0]
    return (
        result,
        in_grad,
        grad_norm,
        *in_state,
        *states[4:8],
        *feed_states[4:],
        *feed_states[:4],
        *states[8:11],
    )


def solution(mesh):
    in_specs = (
        P("dp", None, None),
        P("dp"),
        P("dp"),
        P("dp", None, None),
        P(None, None, "mp"),
        P("mp", None),
        P(None, "mp"),
        P("mp", None),
        P(),
        P(None, None, "mp"),
        P(None, None, "mp"),
        P("mp", None),
        P("mp", None),
        P(None, "mp"),
        P(None, "mp"),
        P("mp", None),
        P("mp", None),
        P(),
        P(),
    )
    out_specs = (
        P("dp", None, None),
        P("dp", None, None),
        P(),
        P(None, None, "mp"),
        P(None, None, "mp"),
        P(None, None, "mp"),
        P(None, None, "mp"),
        P("mp", None),
        P("mp", None),
        P("mp", None),
        P("mp", None),
        P(None, "mp"),
        P(None, "mp"),
        P(None, "mp"),
        P(None, "mp"),
        P("mp", None),
        P("mp", None),
        P("mp", None),
        P("mp", None),
        P(),
        P(),
        P(),
    )
    return jax.shard_map(body, mesh=mesh, in_specs=in_specs, out_specs=out_specs, check_vma=False)
```

```python
import functools
import math

import jax
import jax.numpy as jnp
from jax import lax
from jax.experimental import pallas as pl
from jax.experimental.pallas import tpu as pltpu
from jax.sharding import PartitionSpec as P

HEAD_DIM = 64
STEP = 10


eps_norm = 1e-05
beta_one = 0.9
beta_two = 0.95
adam_eps = 1e-08
decay_weight = 0.1
clip_coeff = 0.03
rate_inproj = 0.07
rate_outproj = 0.3
rate_upproj = 0.07
rate_downproj = 0.05
rate_norms = 0.2
erf_upper = (
    0.00022905065861350646,
    0.0034082910107109506,
    0.050955695062380861,
    0.18520832239976145,
    1.128379143519084,
)
erf_lower = (
    -1.1791602954361697e-7,
    0.000023547966471313185,
    0.0010179625278914885,
    0.014070470171167667,
    0.11098505178285362,
    0.49746925110067538,
    1.0,
)

SEQS_STEP = 2


def time_embed(steps_given, width):
    halfway = width // 2
    counter = jnp.arange(halfway, dtype=jnp.float32)
    frequency = jnp.exp(-math.log(10000.0) * counter / halfway)
    angles = steps_given.astype(jnp.float32)[:, None] * frequency[None, :]
    return jnp.concatenate([jnp.sin(angles), jnp.cos(angles)], axis=-1)


def swap_pairs(count, bit):
    return [(i, i ^ bit) for i in range(count)]


def pick(flag, first, second):
    return jnp.where(flag, first, second)


def rows_dot(left, right):
    return jnp.dot(left, right, preferred_element_type=jnp.float32)


def last_dot(left, right):
    return lax.dot_general(left, right, (((1,), (1,)), ((), ())), preferred_element_type=jnp.float32)


def first_dot(left, right):
    return lax.dot_general(left, right, (((0,), (0,)), ((), ())), preferred_element_type=jnp.float32)


def norm_parts(hidden):
    centre = jnp.mean(hidden, axis=-1, keepdims=True)
    offset = hidden - centre
    spread = jnp.mean(offset * offset, axis=-1, keepdims=True)
    scale = lax.rsqrt(spread + eps_norm)
    return offset * scale, scale


def norm_back(grad, gain, normal, scale):
    scaled = grad * gain
    first = jnp.mean(scaled, axis=-1, keepdims=True)
    second = jnp.mean(scaled * normal, axis=-1, keepdims=True)
    return scale * (scaled - first - normal * second)


def flat_rows(values):
    return values.reshape(values.shape[0] * values.shape[1], values.shape[2])


def start_rows(tokens_ref, temb_ref):
    return flat_rows(tokens_ref[...].astype(jnp.float32) + temb_ref[...])


def grad_out_rows(lengths_ref, first_seq, cotangent_ref, block=None):
    seqs, seq_len, width = cotangent_ref.shape
    first = first_seq + (pl.program_id(0) if block is None else block) * seqs
    place = lax.broadcasted_iota(jnp.int32, (seq_len, width), 0)
    parts = [
        jnp.where(place < lengths_ref[first + s], cotangent_ref[s], 0.0) for s in range(seqs)
    ]
    return jnp.concatenate(parts, axis=0)


def head_masks(shape, heads):
    lanes = lax.broadcasted_iota(jnp.int32, shape, 1) // HEAD_DIM
    return [lanes == h for h in range(heads)]


def stack_heads(values, masks):
    return jnp.concatenate([jnp.where(m, values, jnp.zeros_like(values)) for m in masks], axis=0)


def merge_heads(values, masks):
    rows = values.shape[0] // len(masks)
    merged = jnp.zeros((rows, values.shape[1]), values.dtype)
    for h, mask in enumerate(masks):
        merged = jnp.where(mask, values[h * rows : (h + 1) * rows], merged)
    return merged


def soft_rows(stacked, keysets, lengths):
    scores = []
    for rows, keyset, length in zip(stacked, keysets, lengths):
        part = last_dot(rows, keyset) * HEAD_DIM ** (-0.5)
        live = lax.broadcasted_iota(jnp.int32, part.shape, 1) < length
        scores.append(jnp.where(live, part, -1000000000.0))
    scores = jnp.concatenate(scores, axis=0)
    raised = jnp.exp(scores - jnp.max(scores, axis=-1, keepdims=True))
    return raised * (1.0 / jnp.sum(raised, axis=-1, keepdims=True))


def split_seqs(values, seqs):
    rows = values.shape[0] // seqs
    return [values[s * rows : (s + 1) * rows] for s in range(seqs)]


def attend_block(lengths_ref, first_seq, normed, w_in, w_out, seqs, heads):
    pad = w_out.shape[0]
    mixed = rows_dot(normed, w_in[...]).astype(jnp.bfloat16)
    first = first_seq + pl.program_id(0) * seqs
    parts = split_seqs(mixed, seqs)
    masks = head_masks((parts[0].shape[0], pad), heads)
    soft = soft_rows(
        [stack_heads(part[:, :pad], masks) for part in parts],
        [part[:, pad : 2 * pad] for part in parts],
        [lengths_ref[first + s] for s in range(seqs)],
    ).astype(jnp.bfloat16)
    context = [
        merge_heads(rows_dot(probs, part[:, 2 * pad :]), masks)
        for probs, part in zip(split_seqs(soft, seqs), parts)
    ]
    context = jnp.concatenate(context, axis=0).astype(jnp.bfloat16)
    return mixed, context, rows_dot(context, w_out[...])


def front_own_kernel(
    heads, first_seq, lengths, tokens, temb, norms, w_in, w_out, mixed_out, normed_out, context_out, attended
):
    normal, unused = norm_parts(start_rows(tokens, temb))
    normed = (normal * norms[0:1] + norms[1:2]).astype(jnp.bfloat16)
    normed_out[...] = normed
    mixed, context, share = attend_block(
        lengths, first_seq, normed, w_in, w_out, tokens.shape[0], heads
    )
    mixed_out[...] = mixed
    context_out[...] = context
    attended[...] = share


def front_far_kernel(
    heads, seqs, first_seq, lengths, normed, w_in, w_out, own, attended, mixed_out
):
    mixed_out[...], unused, share = attend_block(
        lengths, first_seq, normed[...], w_in, w_out, seqs, heads
    )
    attended[...] = own[...] + share


def error_function(values):
    bounded = jnp.clip(values, -3.832506856900711, 3.832506856900711)
    square = bounded * bounded
    upper = jnp.full_like(square, erf_upper[0])
    for factor in erf_upper[1:]:
        upper = upper * square + factor
    lower = jnp.full_like(square, erf_lower[0])
    for factor in erf_lower[1:]:
        lower = lower * square + factor
    return bounded * upper / lower


def gelu_and_slope(values):
    scaled = values * math.sqrt(0.5)
    share = 0.5 + 0.5 * error_function(scaled)
    density = jnp.exp(-scaled * scaled) * (1.0 / math.sqrt(2.0 * math.pi))
    return values * share, share + values * density


def feed_block(normed, grad_down_in, up, up_t, down_t):
    upward = rows_dot(normed, up[...])
    activated, slope = gelu_and_slope(upward)
    grad_act = rows_dot(grad_down_in, down_t[...])
    grad_rise = (grad_act * slope).astype(jnp.bfloat16)
    return activated.astype(jnp.bfloat16), grad_rise, rows_dot(grad_rise, up_t[...])


def split_rows(flag, values, keep, send):
    rows = keep.shape[0]
    keep[...] = values[pl.ds(pl.multiple_of(flag * rows, 16), rows), :]
    send[...] = values[pl.ds(pl.multiple_of((1 - flag) * rows, 16), rows), :]


def feed_own_kernel(
    lengths,
    place,
    tokens,
    temb,
    attended_0,
    attended_1,
    received_0,
    received_1,
    cotangent,
    norms,
    up,
    up_t,
    down_t,
    middle_out,
    normed_out,
    grad_in_out,
    activated_out,
    entry,
    keep_down,
    send_down,
    keep_up,
    send_up,
    grad_down,
    grad_up,
):
    first = in_first_half()

    @pl.when(pl.program_id(0) == 0)
    def begin():
        grad_down[...] = jnp.zeros_like(grad_down)
        grad_up[...] = jnp.zeros_like(grad_up)

    attended = jnp.where(
        first, attended_0[...] + received_0[...], attended_1[...] + received_1[...]
    )
    middle = start_rows(tokens, temb) + attended
    middle_out[...] = middle
    normal, unused = norm_parts(middle)
    normed = (normal * norms[2:3] + norms[3:4]).astype(jnp.bfloat16)
    normed_out[...] = normed
    grad_down_in = grad_out_rows(lengths, 0, cotangent).astype(jnp.bfloat16)
    grad_in_out[...] = grad_down_in
    activated, grad_rise, share = feed_block(normed, grad_down_in, up, up_t, down_t)
    activated_out[...] = activated
    entry[...] = share
    grad_down[...] += first_dot(activated, grad_down_in)
    grad_up[...] += first_dot(normed, grad_rise)

    @pl.when(pl.program_id(0) == pl.num_programs(0) - 1)
    def write():
        split_rows(place[0], grad_down, keep_down, send_down)
        split_rows(place[1], grad_up, keep_up, send_up)


def feed_far_kernel(normed, grad_down_in, up, up_t, down_t, entry_own, activated_out, entry):
    activated, unused, share = feed_block(normed[...], grad_down_in[...], up, up_t, down_t)
    activated_out[...] = activated
    entry[...] = entry_own[...] + share


def in_first_half():
    return pl.program_id(0) < pl.num_programs(0) // 2


def result_kernel(middle, downward, received, result):
    result[...] = (middle[...] + (downward[0] + received[0])).reshape(result.shape)


def back_seqs(mixed, lengths, grad_context, heads, pad):
    seqs = len(lengths)
    parts = split_seqs(mixed, seqs)
    masks = head_masks((parts[0].shape[0], pad), heads)
    stacked = [stack_heads(part[:, :pad], masks) for part in parts]
    keysets = [part[:, pad : 2 * pad] for part in parts]
    soft = soft_rows(stacked, keysets, lengths)
    grad_stacked = [stack_heads(part, masks) for part in split_seqs(grad_context, seqs)]
    grad_probs = [last_dot(grad, part[:, 2 * pad :]) for grad, part in zip(grad_stacked, parts)]
    grad_probs = jnp.concatenate(grad_probs, axis=0)
    inner_sum = jnp.sum(soft * grad_probs, axis=-1, keepdims=True)
    grad_scores = split_seqs((soft * (grad_probs - inner_sum)).astype(jnp.bfloat16), seqs)
    probs = split_seqs(soft.astype(jnp.bfloat16), seqs)
    scaling = HEAD_DIM ** (-0.5)
    grads = []
    for s in range(seqs):
        grad_query = merge_heads(rows_dot(grad_scores[s], keysets[s]), masks) * scaling
        grad_key = first_dot(grad_scores[s], stacked[s]) * scaling
        grad_value = first_dot(probs[s], grad_stacked[s])
        grads.append(jnp.concatenate([grad_query, grad_key, grad_value], axis=1))
    return jnp.concatenate(grads, axis=0).astype(jnp.bfloat16)


def back_kernel(
    heads,
    first_seq,
    last,
    lengths,
    place,
    cotangent,
    middle,
    entry,
    received,
    mixed,
    context,
    normed_one,
    norms,
    w_out_t,
    *rest,
):
    if last:
        old_in, old_out, old_norms = rest[:3]
        rest = rest[3:]
        pieces = rest[3:7]
    grad_middle_out, grad_mixed_out, grad_norms = rest[:3]
    grad_in, grad_out = rest[-2:]
    step = pl.program_id(0)
    seqs, seq_len, width = cotangent.shape
    pad = context.shape[1]
    local = heads * HEAD_DIM

    @pl.when(step == 0)
    def begin():
        grad_in[...] = old_in[...] if last else jnp.zeros_like(grad_in)
        grad_out[...] = old_out[...] if last else jnp.zeros_like(grad_out)
        grad_norms[...] = old_norms[...] if last else jnp.zeros_like(grad_norms)

    entry_two = entry[...] + received[...]
    normal, scale = norm_parts(middle[...])
    grad_middle = grad_out_rows(lengths, first_seq, cotangent) + norm_back(
        entry_two, norms[2:3], normal, scale
    )
    grad_middle_out[...] = grad_middle
    grad_norms[2:3] += jnp.sum(entry_two * normal, axis=0, keepdims=True)
    grad_norms[3:4] += jnp.sum(entry_two, axis=0, keepdims=True)
    grad_attn = grad_middle.astype(jnp.bfloat16)
    grad_context = rows_dot(grad_attn, w_out_t[...]).astype(jnp.bfloat16)
    grad_out[...] += first_dot(context[...], grad_attn)
    found = [lengths[first_seq + step * seqs + s] for s in range(seqs)]
    grad_mixed = back_seqs(mixed[...], found, grad_context, heads, pad)
    grad_mixed_out[...] = grad_mixed
    grad_in[...] += first_dot(grad_mixed, normed_one[...])

    if last:

        @pl.when(step == pl.num_programs(0) - 1)
        def write():
            parts = [grad_in.at[part * pad : part * pad + local] for part in range(3)]
            parts.append(grad_out.at[:local])
            for flag, pair, outs in (
                (place[0], parts[:2], pieces[:2]),
                (place[1], parts[2:], pieces[2:]),
            ):

                @pl.when(flag == 0)
                def straight():
                    outs[0][...] = pair[0][...]
                    outs[1][...] = pair[1][...]

                @pl.when(flag != 0)
                def crossed():
                    outs[0][...] = pair[1][...]
                    outs[1][...] = pair[0][...]


def back_far_kernel(
    heads,
    lengths,
    tokens,
    temb,
    middle_0,
    middle_1,
    mixed_0,
    mixed_1,
    own_0,
    own_1,
    w_out_t,
    w_in_t,
    own_in_t,
    act,
    far_act_0,
    far_act_1,
    down,
    down_far,
    shares,
    grad_norms,
):
    @pl.when(pl.program_id(0) == 0)
    def begin():
        grad_norms[...] = jnp.zeros_like(grad_norms)

    first = in_first_half()
    seqs = tokens.shape[0]
    pad = w_out_t.shape[1]
    own = rows_dot(jnp.where(first, own_0[...], own_1[...]), own_in_t[...])
    normal, unused = norm_parts(start_rows(tokens, temb))
    grad_norms[0:1] += jnp.sum(own * normal, axis=0, keepdims=True)
    grad_norms[1:2] += jnp.sum(own, axis=0, keepdims=True)
    grad_attn = jnp.where(first, middle_0[...], middle_1[...]).astype(jnp.bfloat16)
    grad_context = rows_dot(grad_attn, w_out_t[...]).astype(jnp.bfloat16)
    found = [lengths[pl.program_id(0) * seqs + s] for s in range(seqs)]
    mixed = jnp.where(first, mixed_0[...], mixed_1[...])
    grad_mixed = back_seqs(mixed, found, grad_context, heads, pad)
    shares[0] = own + rows_dot(grad_mixed, w_in_t[...])
    far_act = jnp.where(first, far_act_0[...], far_act_1[...])
    shares[1] = rows_dot(act[...], down[...]) + rows_dot(far_act, down_far[...])


def add_kernel(left, right, total):
    total[...] = left[...] + right[...]


def share_kernel(place, keep_a, got_a, keep_b, got_b, keep_a2, send_a2, keep_b2, send_b2, sums):
    rows = keep_a.shape[0]
    sums[:rows] = keep_a[...] + got_a[...]
    sums[rows:] = keep_b[...] + got_b[...]
    split_rows(place[1], sums.at[:rows], keep_a2, send_a2)
    split_rows(place[0], sums.at[rows:], keep_b2, send_b2)


def pair_kernel(keep_a, got_a, keep_b, got_b, both):
    rows = keep_a.shape[0]
    both[:rows] = keep_a[...] + got_a[...]
    both[rows : 2 * rows] = keep_b[...] + got_b[...]


def pair_small_kernel(mp_copies, keep_a, got_a, keep_b, got_b, norms_one, norms_two, both):
    pair_kernel(keep_a, got_a, keep_b, got_b, both)
    rows = keep_a.shape[0]
    both[2 * rows :] = jnp.zeros((8, both.shape[1]), jnp.float32)
    both[2 * rows : 2 * rows + 4] = norms_one[...] + norms_two[...] * (1.0 / mp_copies)


def all_squares(values):
    columns = jnp.sum(values * values, axis=0, keepdims=True)
    return jnp.sum(columns, axis=1, keepdims=True)


def total_kernel(both, got, total_a, total_b, squares):
    rows = total_a.shape[0]
    total = both[...] + got[...]
    total_a[...] = total[:rows]
    total_b[...] = total[rows:]
    squares[...] = jnp.broadcast_to(all_squares(total), squares.shape)


def total_small_kernel(both, got, squares, *rest):
    total_a, total_b, small = rest[-3:]
    rows = (both.shape[0] - 8) // 2
    total_a[:rows] = both[:rows] + got[:rows]
    total_b[:rows] = both[rows : 2 * rows] + got[rows : 2 * rows]
    found = squares[:1, :1] + all_squares(total_a[:rows]) + all_squares(total_b[:rows])
    norms = both[2 * rows :] + got[2 * rows :]
    fifth = lax.broadcasted_iota(jnp.int32, norms.shape, 0) == 4
    small[...] = jnp.where(fifth, found, norms)
    total_a[rows:] = small[...]
    total_b[rows:] = small[...]


def place_rows(flag, own, got, out):
    rows = out.shape[0] // 2
    out[pl.ds(pl.multiple_of(flag * rows, 16), rows), :] = own[:rows]
    out[pl.ds(pl.multiple_of((1 - flag) * rows, 16), rows), :] = got[:rows]


def merge_kernel(place, own_a, got_a, own_b, got_b, out_a, out_b):
    place_rows(place[1], own_a, got_a, out_a)
    place_rows(place[0], own_b, got_b, out_b)


def merge_after_kernel(place, own_a, got_a, own_b, got_b, after_a, after_b, out_a, out_b):
    merge_kernel(place, own_a, got_a, own_b, got_b, out_a, out_b)


def small_kernel(own_a, got_a, got_b, diagonal, small):
    rows = own_a.shape[0] - 8
    small[...] = (own_a[rows:] + got_a[rows:]) + (got_b[rows:] + diagonal[...])


def clip_factor(small, threshold):
    squares = small[4:5, :1] + all_squares(small[:4])
    norm = jnp.sqrt(squares)
    return norm, jnp.minimum(1.0, threshold / norm)


def adam_step(weight, gradient, mean_old, square_old, rate, decay, outs):
    mean_new = beta_one * mean_old + (1.0 - beta_one) * gradient
    square_new = beta_two * square_old + (1.0 - beta_two) * gradient * gradient
    lower = jnp.sqrt(square_new * (1.0 / (1.0 - beta_two**STEP))) + adam_eps
    direction = mean_new * (1.0 / (1.0 - beta_one**STEP)) / lower
    weight_new = weight - rate * (direction + decay * weight)
    outs[0][...] = mean_new
    outs[1][...] = square_new
    outs[2][...] = weight_new
    if len(outs) > 3:
        outs[3][...] = weight_new.astype(outs[3].dtype)


def adam_feed_kernel(threshold, place, small, *refs):
    unused, factor = clip_factor(small, threshold)
    late = pl.program_id(0) // (pl.num_programs(0) // 2)
    for which, rate in enumerate((rate_downproj, rate_upproj)):
        own, got, weight, mean, square = refs[5 * which : 5 * which + 5]
        outs = refs[10 + 4 * which : 14 + 4 * which]
        gradient = jnp.where(late == place[which], own[...], got[...]) * factor
        adam_step(weight[...], gradient, mean[...], square[...], rate, decay_weight, outs)


def adam_attn_kernel(
    threshold,
    place,
    small,
    own_a,
    got_a,
    own_b,
    got_b,
    in_weight,
    in_mean,
    in_square,
    out_weight,
    out_mean,
    out_square,
    norm_weight,
    norm_mean,
    norm_square,
    *outs,
):
    norm, factor = clip_factor(small, threshold)
    step = pl.program_id(0)

    @pl.when(step < 3)
    def inside():
        pick_a = jnp.where(step == place[0], own_a[...], got_a[...])
        pick_b = jnp.where(place[1] == 0, own_b[...], got_b[...])
        gradient = jnp.where(step < 2, pick_a, pick_b) * factor
        values = in_weight[...], gradient, in_mean[...], in_square[...]
        adam_step(*values, rate_inproj, decay_weight, outs[:4])

    @pl.when(step == 3)
    def outside():
        gradient = jnp.where(place[1] == 1, own_b[...], got_b[...]) * factor
        values = out_weight[...], gradient, out_mean[...], out_square[...]
        adam_step(*values, rate_outproj, decay_weight, outs[4:8])
        gradient = small[:4] * factor
        values = norm_weight[...], gradient, norm_mean[...], norm_square[...]
        adam_step(*values, rate_norms, 0.0, outs[8:11])
        outs[11][...] = jnp.broadcast_to(norm, outs[11].shape)


def finish_kernel(tokens, temb, middle_0, middle_1, entry_one, received, norms, in_grad):
    grad_middle = jnp.where(in_first_half(), middle_0[...], middle_1[...])
    entry = entry_one[0] + received[0]
    normal, scale = norm_parts(start_rows(tokens, temb))
    total = grad_middle + norm_back(entry, norms[0:1], normal, scale)
    in_grad[...] = total.reshape(in_grad.shape)


def attn_weights_kernel(w_in, w_out, in_n, in_t, out_n, out_t):
    local = w_out.shape[0]
    pad = out_n.shape[0]
    half = jnp.bfloat16
    in_n[...] = jnp.zeros_like(in_n)
    in_t[...] = jnp.zeros_like(in_t)
    out_n[...] = jnp.zeros_like(out_n)
    out_t[...] = jnp.zeros_like(out_t)
    for part in range(3):
        piece = w_in[part * local : (part + 1) * local, :]
        in_t[part * pad : part * pad + local, :] = piece.astype(half)
        in_n[:, part * pad : part * pad + local] = piece.T.astype(half)
    out_n[:local, :] = w_out[...].astype(half)
    out_t[:, :local] = w_out[...].T.astype(half)


def attn_far_kernel(piece, own, beside, line, corner, in_n, in_t, out_n, out_t, rows):
    local = own.shape[0]
    pad = out_n.shape[0]
    half = jnp.bfloat16
    index = piece[0]
    rows[...] = jnp.zeros_like(rows)
    rows[index, :local] = own[...].astype(half)
    rows[index ^ 1, :local] = beside[...].astype(half)
    rows[index ^ 2, :local] = line[...].astype(half)
    rows[index ^ 3, :local] = corner[...].astype(half)
    for part in range(3):
        in_t[part * pad : (part + 1) * pad] = rows[part]
        in_n[:, part * pad : (part + 1) * pad] = rows[part].T
    out_n[...] = rows[3]
    out_t[...] = rows[3].T


def send_attn_kernel(piece, inside, inside_corner, outside, own, corner):
    for index, block, out in ((piece[0], inside, own), (piece[0] ^ 3, inside_corner, corner)):

        @pl.when(index < 3)
        def from_input():
            out[...] = block[...]

        @pl.when(index == 3)
        def from_output():
            out[...] = outside[...]


def send_feed_kernel(piece, up, down, up_corner, down_corner, own, corner):
    rows = up.shape[0]
    own[:rows] = up[...]
    own[rows:] = down[...]
    corner[:rows] = up_corner[...]
    corner[rows:] = down_corner[...]


def touch_kernel(*refs):
    refs[-1][...] = jnp.zeros_like(refs[-1])


def feed_weights_kernel(up, down, up_n, up_t, down_n, down_t):
    half = jnp.bfloat16
    for weight, straight, turned in ((up, up_n, up_t), (down, down_n, down_t)):
        value = weight[...].astype(half)
        straight[...] = value
        turned[...] = value.T


def feed_far_weights_kernel(piece, own, beside, line, corner, *outs):
    half = jnp.bfloat16
    index = piece[0]
    rows = own.shape[0] // 2
    pieces = (index, own), (index ^ 1, beside), (index ^ 2, line), (index ^ 3, corner)
    for which in range(2):
        straight, turned = outs[2 * which : 2 * which + 2]
        part = slice(which * rows, (which + 1) * rows)
        for place, got in pieces:
            straight[pl.ds(pl.multiple_of(place * rows, 16), rows), :] = got[part].astype(half)
        turned[...] = straight[...].T


SCALARS = pl.BlockSpec(memory_space=pltpu.SMEM)
ANYWHERE = pl.BlockSpec(memory_space=pl.ANY)
WHOLE = pl.BlockSpec(memory_space=pltpu.VMEM)


def array(shape, dtype=jnp.float32):
    return jax.ShapeDtypeStruct(shape, dtype)


STAGE_COST = 10**12
class Chain:
    def __init__(self):
        self.token = None

    def __call__(
        self,
        kernel,
        args,
        in_specs,
        out_specs,
        out_shape,
        grid=(),
        scratch=(),
        scalars=(),
        vmem=20,
        ends_stage=False,
    ):
        args, in_specs, count = list(args), list(in_specs), len(args) + len(scalars)
        run = kernel
        if self.token is not None:
            args.append(self.token)
            in_specs.append(ANYWHERE)

            def run(*refs):
                return kernel(*refs[:count], *refs[count + 1 :])

        results = pl.pallas_call(
            run,
            grid_spec=pltpu.PrefetchScalarGridSpec(
                num_scalar_prefetch=len(scalars),
                grid=grid,
                in_specs=in_specs,
                out_specs=out_specs,
                scratch_shapes=list(scratch),
            ),
            out_shape=out_shape,
            compiler_params=pltpu.CompilerParams(vmem_limit_bytes=vmem * 1024 * 1024),
            cost_estimate=pl.CostEstimate(
                flops=10**12 if ends_stage else 1, bytes_accessed=1, transcendentals=0
            ),
            name=getattr(kernel, "func", kernel).__name__,
        )(*scalars, *args)
        leaves = jax.tree.leaves(results)
        self.token = min(leaves, key=lambda leaf: leaf.size * leaf.dtype.itemsize)
        return results


def body(
    tokens,
    lengths,
    timesteps,
    cotangent,
    proj_input,
    proj_output,
    proj_upward,
    proj_downward,
    norm_params,
    input_mean,
    input_square,
    output_mean,
    output_square,
    upward_mean,
    upward_square,
    downward_mean,
    downward_square,
    norms_mean,
    norms_square,
):
    seq_count, seq_len, width = tokens.shape
    local = proj_output.shape[0]
    hidden = proj_downward.shape[0]
    heads = local // HEAD_DIM
    rows = seq_count * seq_len
    dp_count, mp_count = lax.axis_size("dp"), lax.axis_size("mp")
    by_pairs = dp_count == 8
    pad = -(-local // 128) * 128
    half = jnp.bfloat16
    seqs = SEQS_STEP
    step_rows = seqs * seq_len
    steps = seq_count // seqs
    half_steps = steps // 2
    half_seqs = seq_count // 2
    half_rows = rows // 2
    more = 2 * seqs
    more_rows = more * seq_len
    more_steps = half_steps // 2
    quarter = hidden // 4
    threshold = clip_coeff * width * math.sqrt(dp_count * rows)
    own_place = lax.axis_index("dp")
    low, high = own_place % 2, (own_place // 2) % 2
    place = jnp.stack([low, high]).astype(jnp.int32)
    piece = (own_place % 4).astype(jnp.int32)[None]
    chain = Chain()

    def across(values):
        return lax.ppermute(values, "mp", swap_pairs(mp_count, 2))

    def core(values):
        return lax.ppermute(values, "mp", swap_pairs(mp_count, 1))

    def beside(values):
        return lax.ppermute(values, "dp", swap_pairs(dp_count, 1))

    def line(values):
        return lax.ppermute(values, "dp", swap_pairs(dp_count, 2))

    def far_line(values):
        return lax.ppermute(values, "dp", swap_pairs(dp_count, 4))

    def corner(values):
        return lax.ppermute(values, "dp", swap_pairs(dp_count, 3))

    def blocks(columns, offset=0, count=step_rows):
        return pl.BlockSpec((count, columns), lambda i, *_: (i + offset, 0))

    def near_blocks(columns):
        return pl.BlockSpec(
            (step_rows, columns), lambda i, *_: (jnp.minimum(i, half_steps - 1), 0)
        )

    def away_blocks(columns):
        return pl.BlockSpec(
            (step_rows, columns), lambda i, *_: (jnp.maximum(i - half_steps, 0), 0)
        )

    def fixed(*shape):
        return pl.BlockSpec(shape, lambda *_: (0,) * len(shape))

    def seq_blocks(middle, offset=0, count=seqs):
        return pl.BlockSpec((count, middle, width), lambda i, *_: (i + offset, 0, 0))

    wide = blocks(width)
    more_wide = blocks(width, 0, more_rows)
    norm_block = fixed(*norm_params.shape)
    temb = time_embed(timesteps, width)[:, None, :]
    input_t = jnp.transpose(proj_input, (1, 2, 0)).reshape(3 * local, width)

    def piece_block(count, flip, most=3):
        def index(i, piece):
            return (jnp.minimum(piece[0] ^ flip, most), 0)

        return pl.BlockSpec((count, width), index)

    attn_sends = chain(
        send_attn_kernel,
        (input_t, input_t, proj_output),
        [piece_block(local, 0, 2), piece_block(local, 3, 2), fixed(local, width)],
        [fixed(local, width)] * 2,
        [array((local, width))] * 2,
        grid=(1,),
        scalars=(piece,),
        vmem=60,
    )
    attn_got, attn_corner = [across(values) for values in attn_sends]
    in_n, in_t, out_n, out_t = chain(
        attn_weights_kernel,
        (input_t, proj_output),
        [WHOLE] * 2,
        [WHOLE] * 4,
        [array((width, 3 * pad), half), array((3 * pad, width), half)]
        + [array((pad, width), half), array((width, pad), half)],
    )

    def front(part):
        start = part * more_steps
        return chain(
            functools.partial(front_own_kernel, heads, part * half_seqs),
            (tokens, temb, norm_params, in_n, out_n),
            [seq_blocks(seq_len, start, more), seq_blocks(1, start, more), norm_block]
            + [fixed(width, 3 * pad), fixed(pad, width)],
            [blocks(columns, 0, more_rows) for columns in (3 * pad, width, pad, width)],
            [array((half_rows, 3 * pad), half), array((half_rows, width), half)]
            + [array((half_rows, pad), half), array((half_rows, width))],
            grid=(more_steps,),
            scalars=(lengths,),
            ends_stage=part == 1,
        )

    fronts = [front(0)]
    feed_sends = chain(
        send_feed_kernel,
        (proj_upward, proj_downward, proj_upward, proj_downward),
        [piece_block(quarter, 0)] * 2 + [piece_block(quarter, 3)] * 2,
        [fixed(2 * quarter, width)] * 2,
        [array((2 * quarter, width))] * 2,
        grid=(1,),
        scalars=(piece,),
    )
    attn_y, attn_z = beside(attn_got), line(attn_got)
    chain(touch_kernel, (attn_got,), [ANYWHERE], WHOLE, array((8, 128)), ends_stage=True)
    feed_got, feed_corner = [across(values) for values in feed_sends]
    fronts.append(front(1))
    up_n, up_t, down_n, down_t = chain(
        feed_weights_kernel,
        (proj_upward, proj_downward),
        [WHOLE] * 2,
        [WHOLE] * 4,
        [array((width, hidden), half), array((hidden, width), half)]
        + [array((hidden, width), half), array((width, hidden), half)],
    )
    far_in, far_in_t, far_out, far_out_t = chain(
        attn_far_kernel,
        (attn_got, attn_y, attn_z, attn_corner),
        [WHOLE] * 4,
        [WHOLE] * 4,
        [array((width, 3 * pad), half), array((3 * pad, width), half)]
        + [array((pad, width), half), array((width, pad), half)],
        scratch=[pltpu.VMEM((4, pad, width), half)],
        scalars=(piece,),
        ends_stage=True,
    )

    def far_front(part):
        unused, normed, unused_too, own = fronts[part]
        attended, mixed = chain(
            functools.partial(front_far_kernel, heads, more, part * half_seqs),
            (normed, far_in, far_out, own),
            [more_wide, fixed(width, 3 * pad), fixed(pad, width), more_wide],
            [more_wide, blocks(3 * pad, 0, more_rows)],
            [array((half_rows, width)), array((half_rows, 3 * pad), half)],
            grid=(more_steps,),
            scalars=(lengths,),
        )
        return attended, core(attended), mixed

    attended_0, attended_got_0, far_mixed_0 = far_front(0)
    attended_1, attended_got_1, far_mixed_1 = far_front(1)
    far_mixed = far_mixed_0, far_mixed_1
    feed_y, feed_z = beside(feed_got), line(feed_got)
    chain(touch_kernel, (feed_got,), [ANYWHERE], WHOLE, array((8, 128)), ends_stage=True)

    shared = [array((rows, width))] + [array((rows, width), half)] * 2
    shared += [array((rows, hidden), half), array((rows, width))]
    halves = [array((hidden // 2, width))] * 2 + [array((width // 2, hidden))] * 2
    middle, normed_two, grad_down_in, activated, entry, *grads = chain(
        feed_own_kernel,
        (tokens, temb, attended_0, attended_1, attended_got_0, attended_got_1)
        + (cotangent, norm_params, up_n, up_t, down_t),
        [seq_blocks(seq_len), seq_blocks(1)]
        + [near_blocks(width), away_blocks(width)] * 2
        + [seq_blocks(seq_len), norm_block]
        + [fixed(width, hidden), fixed(hidden, width), fixed(width, hidden)],
        [wide, wide, wide, blocks(hidden), wide] + [fixed(*shape.shape) for shape in halves],
        shared + halves,
        grid=(steps,),
        scratch=[pltpu.VMEM((hidden, width), jnp.float32), pltpu.VMEM((width, hidden), jnp.float32)],
        scalars=(lengths, place),
        vmem=40,
    )

    def send_pair(pair):
        keep_a, send_a, keep_b, send_b = pair
        return keep_a, beside(send_a), keep_b, line(send_b)

    def share_pair(pair, ends_stage):
        if not by_pairs:
            return pair
        size = array((pair[0].shape[0] // 2, width))
        keep_a, send_a, keep_b, send_b = chain(
            share_kernel,
            pair,
            [WHOLE] * 4,
            [WHOLE] * 4,
            [size] * 4,
            scratch=[pltpu.VMEM((4 * size.shape[0], width), jnp.float32)],
            scalars=(place,),
            ends_stage=ends_stage,
        )
        return keep_a, line(send_a), keep_b, beside(send_b)

    def merge_pair(pair, extra, kernel, after):
        size = array((2 * (pair[0].shape[0] - extra), width))
        first, second = chain(
            kernel,
            (*pair, *after),
            [WHOLE] * 4 + [ANYWHERE] * len(after),
            [WHOLE] * 2,
            [size] * 2,
            scalars=(place,),
        )
        return first, beside(first), second, line(second)

    def sum_plainly(pair):
        keep_a, send_a, keep_b, send_b = pair
        totals = []
        for flag, keep, send in ((low, keep_a, send_a), (high, keep_b, send_b)):
            whole = pick(flag == 0, jnp.concatenate([keep, send]), jnp.concatenate([send, keep]))
            total = lax.psum(whole, "dp")
            count = total.shape[0] // 2
            totals += [lax.dynamic_slice_in_dim(total, f * count, count) for f in (flag, 1 - flag)]
        return totals, sum(jnp.sum(total * total) for total in totals) / dp_count

    if by_pairs:
        grads = send_pair(grads)
    up_far_n, up_far_t, down_far_n, down_far_t = chain(
        feed_far_weights_kernel,
        (feed_got, feed_y, feed_z, feed_corner),
        [WHOLE] * 4,
        [WHOLE] * 4,
        [array((width, hidden), half), array((hidden, width), half)]
        + [array((hidden, width), half), array((width, hidden), half)],
        scalars=(piece,),
        ends_stage=True,
    )

    def far(part):
        offset = part * more_steps
        own = blocks(width, offset, more_rows)
        act, total = chain(
            feed_far_kernel,
            (normed_two, grad_down_in, up_far_n, up_far_t, down_far_t, entry),
            [own, own, fixed(width, hidden), fixed(hidden, width), fixed(width, hidden), own],
            [blocks(hidden, 0, more_rows), more_wide],
            [array((half_rows, hidden), half), array((half_rows, width))],
            grid=(more_steps,),
            vmem=24,
        )
        return act, total, core(total)

    far_0, far_1 = far(0), far(1)
    grads = share_pair(grads, True)

    def back(part, feed, before):
        start = part * half_steps
        mixed, normed_one, context, unused = fronts[part]
        shapes = [(3 * pad, width), (pad, width), norm_params.shape]
        last = before is not None
        ends = [(local, width)] * 4 if last else shapes[:2]
        return chain(
            functools.partial(back_kernel, heads, part * half_seqs, last),
            (cotangent, middle, feed[1], feed[2], mixed, context, normed_one, norm_params, out_t)
            + (before if last else ()),
            [seq_blocks(seq_len, start), blocks(width, start), wide, wide]
            + [blocks(3 * pad), blocks(pad), wide, norm_block, fixed(width, pad)]
            + ([fixed(*shape) for shape in shapes] if last else []),
            [wide, blocks(3 * pad), norm_block] + [fixed(*shape) for shape in ends],
            [array((half_rows, width)), array((half_rows, 3 * pad), half)]
            + [array(norm_params.shape)]
            + [array(shape) for shape in ends],
            grid=(half_steps,),
            scratch=[pltpu.VMEM(shape, jnp.float32) for shape in shapes[:2]] if last else (),
            scalars=(lengths, place),
            vmem=32,
        )

    grad_middle_0, grad_mixed_0, norms_0, in_0, out_0 = back(0, far_0, None)
    if by_pairs:
        both = chain(
            pair_kernel,
            grads,
            [WHOLE] * 4,
            WHOLE,
            array((2 * grads[0].shape[0], width)),
            ends_stage=True,
        )
        both_got = far_line(both)
    grad_middle_1, grad_mixed_1, norms_two, *attn_grads = back(1, far_1, (in_0, out_0, norms_0))
    if by_pairs:
        attn_grads = send_pair(attn_grads)

    def more_halves(columns):
        return [
            pl.BlockSpec((more_rows, columns), lambda i, *_: (jnp.minimum(i, more_steps - 1), 0)),
            pl.BlockSpec((more_rows, columns), lambda i, *_: (jnp.maximum(i - more_steps, 0), 0)),
        ]

    shares, norms_one = chain(
        functools.partial(back_far_kernel, heads),
        (tokens, temb, grad_middle_0, grad_middle_1, *far_mixed, grad_mixed_0, grad_mixed_1)
        + (far_out_t, far_in_t, in_t, activated, far_0[0], far_1[0], down_n, down_far_n),
        [seq_blocks(seq_len, 0, more), seq_blocks(1, 0, more)]
        + more_halves(width)
        + more_halves(3 * pad) * 2
        + [fixed(width, pad), fixed(3 * pad, width), fixed(3 * pad, width)]
        + [blocks(hidden, 0, more_rows)]
        + more_halves(hidden)
        + [fixed(hidden, width)] * 2,
        [pl.BlockSpec((2, more_rows, width), lambda i, *_: (0, i, 0)), norm_block],
        [array((2, rows, width)), array(norm_params.shape)],
        grid=(2 * more_steps,),
        scalars=(lengths,),
        vmem=52,
    )
    shares_got = core(shares)

    def share_blocks(which):
        return pl.BlockSpec((1, step_rows, width), lambda i, *_: (which, i, 0))

    if by_pairs:
        size = array((both.shape[0] // 2, width))
        first, second, squares = chain(
            total_kernel,
            (both, both_got),
            [WHOLE] * 2,
            [WHOLE] * 3,
            [size, size, array((8, 128))],
        )
        grads = first, line(first), second, beside(second)
        attn_grads = share_pair(attn_grads, True)
        grads = merge_pair(grads, 0, merge_after_kernel, attn_grads[1::2])
        attn_both = chain(
            functools.partial(pair_small_kernel, mp_count),
            (*attn_grads, norms_one, norms_two),
            [WHOLE] * 6,
            WHOLE,
            array((2 * attn_grads[0].shape[0] + 8, width)),
        )
        attn_both_got = far_line(attn_both)
    result = chain(
        result_kernel,
        (middle, shares, shares_got),
        [wide, share_blocks(1), share_blocks(1)],
        seq_blocks(seq_len),
        array(tokens.shape),
        grid=(steps,),
    )
    in_grad = chain(
        finish_kernel,
        (tokens, temb, grad_middle_0, grad_middle_1, shares, shares_got, norm_params),
        [seq_blocks(seq_len), seq_blocks(1), near_blocks(width), away_blocks(width)]
        + [share_blocks(0), share_blocks(0), norm_block],
        seq_blocks(seq_len),
        array(tokens.shape),
        grid=(steps,),
    )
    if by_pairs:
        size = array((attn_both.shape[0] // 2 + 4, width))
        first, second, small = chain(
            total_small_kernel,
            (attn_both, attn_both_got, squares, grads[1], grads[3]),
            [WHOLE] * 3 + [ANYWHERE] * 2,
            [WHOLE] * 3,
            [size, size, array((8, width))],
        )
        attn_grads = first, line(first), second, beside(second)
        small = chain(
            small_kernel,
            (*attn_grads[:2], attn_grads[3], corner(small)),
            [WHOLE] * 4,
            WHOLE,
            array(small.shape),
        )
        small_got = core(small)
        small = chain(add_kernel, (small, small_got), [WHOLE] * 2, WHOLE, array(small.shape))
        small_got = across(small)
        attn_grads = merge_pair(attn_grads, 8, merge_kernel, ())
        small = chain(add_kernel, (small, small_got), [WHOLE] * 2, WHOLE, array(small.shape))
    else:
        grads, squares = sum_plainly(grads)
        attn_grads, attn_squares = sum_plainly(attn_grads)
        found = jnp.broadcast_to(squares + attn_squares, (4, width))
        small = jnp.concatenate([norms_one + norms_two / mp_count, found])
        small = lax.psum(small, ("dp", "mp"))

    def turned(values):
        return jnp.transpose(values, (1, 2, 0)).reshape(3 * local, width)

    weights = proj_downward, proj_upward
    moments = (downward_mean, downward_square), (upward_mean, upward_square)
    args, specs, outs, shapes = [small], [fixed(8, width)], [], []
    for which, weight in enumerate(weights):
        count = weight.shape[0] // 4
        block = pl.BlockSpec((count, width), lambda i, *_: (i, 0))
        part = pl.BlockSpec((count, width), lambda i, *_: (lax.rem(i, 2), 0))
        args += [*grads[2 * which : 2 * which + 2], weight, *moments[which]]
        specs += [part] * 2 + [block] * 3
        outs += [block] * 4
        shapes += [array(weight.shape)] * 3 + [array(weight.shape, half)]
    feed_states = chain(
        functools.partial(adam_feed_kernel, threshold),
        args,
        specs,
        outs,
        shapes,
        grid=(4,),
        scalars=(place,),
        vmem=32,
    )
    block = pl.BlockSpec((local, width), lambda i, *_: (jnp.minimum(i, 2), 0))
    one = fixed(local, width)
    states = chain(
        functools.partial(adam_attn_kernel, threshold),
        (small, *attn_grads)
        + (input_t, turned(input_mean), turned(input_square))
        + (proj_output, output_mean, output_square, norm_params, norms_mean, norms_square),
        [fixed(8, width)] + [one] * 4 + [block] * 3 + [one] * 3 + [norm_block] * 3,
        [block] * 4 + [one] * 4 + [norm_block] * 3 + [fixed(8, 128)],
        [array(input_t.shape)] * 3
        + [array(input_t.shape, half)]
        + [array(proj_output.shape)] * 3
        + [array(proj_output.shape, half)]
        + [array(norm_params.shape)] * 3
        + [array((8, 128))],
        grid=(4,),
        scalars=(place,),
        vmem=24,
    )
    in_state = [jnp.transpose(s.reshape(3, local, width), (2, 0, 1)) for s in states[:4]]
    grad_norm = states[11][0, 0]
    return (
        result,
        in_grad,
        grad_norm,
        *in_state,
        *states[4:8],
        *feed_states[4:],
        *feed_states[:4],
        *states[8:11],
    )


def solution(mesh):
    in_specs = (
        P("dp", None, None),
        P("dp"),
        P("dp"),
        P("dp", None, None),
        P(None, None, "mp"),
        P("mp", None),
        P(None, "mp"),
        P("mp", None),
        P(),
        P(None, None, "mp"),
        P(None, None, "mp"),
        P("mp", None),
        P("mp", None),
        P(None, "mp"),
        P(None, "mp"),
        P("mp", None),
        P("mp", None),
        P(),
        P(),
    )
    out_specs = (
        P("dp", None, None),
        P("dp", None, None),
        P(),
        P(None, None, "mp"),
        P(None, None, "mp"),
        P(None, None, "mp"),
        P(None, None, "mp"),
        P("mp", None),
        P("mp", None),
        P("mp", None),
        P("mp", None),
        P(None, "mp"),
        P(None, "mp"),
        P(None, "mp"),
        P(None, "mp"),
        P("mp", None),
        P("mp", None),
        P("mp", None),
        P("mp", None),
        P(),
        P(),
        P(),
    )
    return jax.shard_map(body, mesh=mesh, in_specs=in_specs, out_specs=out_specs, check_vma=False)
```

```python
import functools
import math

import jax
import jax.numpy as jnp
from jax import lax
from jax.experimental import pallas as pl
from jax.experimental.pallas import tpu as pltpu
from jax.sharding import PartitionSpec as P

HEAD_DIM = 64
STEP = 10


eps_norm = 1e-05
beta_one = 0.9
beta_two = 0.95
adam_eps = 1e-08
decay_weight = 0.1
clip_coeff = 0.03
rate_inproj = 0.07
rate_outproj = 0.3
rate_upproj = 0.07
rate_downproj = 0.05
rate_norms = 0.2
erf_upper = (
    0.00022905065861350646,
    0.0034082910107109506,
    0.050955695062380861,
    0.18520832239976145,
    1.128379143519084,
)
erf_lower = (
    -1.1791602954361697e-7,
    0.000023547966471313185,
    0.0010179625278914885,
    0.014070470171167667,
    0.11098505178285362,
    0.49746925110067538,
    1.0,
)

SEQS_STEP = 2


def time_embed(steps_given, width):
    halfway = width // 2
    counter = jnp.arange(halfway, dtype=jnp.float32)
    frequency = jnp.exp(-math.log(10000.0) * counter / halfway)
    angles = steps_given.astype(jnp.float32)[:, None] * frequency[None, :]
    return jnp.concatenate([jnp.sin(angles), jnp.cos(angles)], axis=-1)


def swap_pairs(count, bit):
    return [(i, i ^ bit) for i in range(count)]


def pick(flag, first, second):
    return jnp.where(flag, first, second)


def rows_dot(left, right):
    return jnp.dot(left, right, preferred_element_type=jnp.float32)


def last_dot(left, right):
    return lax.dot_general(left, right, (((1,), (1,)), ((), ())), preferred_element_type=jnp.float32)


def first_dot(left, right):
    return lax.dot_general(left, right, (((0,), (0,)), ((), ())), preferred_element_type=jnp.float32)


def norm_parts(hidden):
    centre = jnp.mean(hidden, axis=-1, keepdims=True)
    offset = hidden - centre
    spread = jnp.mean(offset * offset, axis=-1, keepdims=True)
    scale = lax.rsqrt(spread + eps_norm)
    return offset * scale, scale


def norm_back(grad, gain, normal, scale):
    scaled = grad * gain
    first = jnp.mean(scaled, axis=-1, keepdims=True)
    second = jnp.mean(scaled * normal, axis=-1, keepdims=True)
    return scale * (scaled - first - normal * second)


def flat_rows(values):
    return values.reshape(values.shape[0] * values.shape[1], values.shape[2])


def start_rows(tokens_ref, temb_ref):
    return flat_rows(tokens_ref[...].astype(jnp.float32) + temb_ref[...])


def grad_out_rows(lengths_ref, first_seq, cotangent_ref, block=None):
    seqs, seq_len, width = cotangent_ref.shape
    first = first_seq + (pl.program_id(0) if block is None else block) * seqs
    place = lax.broadcasted_iota(jnp.int32, (seq_len, width), 0)
    parts = [
        jnp.where(place < lengths_ref[first + s], cotangent_ref[s], 0.0) for s in range(seqs)
    ]
    return jnp.concatenate(parts, axis=0)


def head_masks(shape, heads):
    lanes = lax.broadcasted_iota(jnp.int32, shape, 1) // HEAD_DIM
    return [lanes == h for h in range(heads)]


def stack_heads(values, masks):
    return jnp.concatenate([jnp.where(m, values, jnp.zeros_like(values)) for m in masks], axis=0)


def merge_heads(values, masks):
    rows = values.shape[0] // len(masks)
    merged = jnp.zeros((rows, values.shape[1]), values.dtype)
    for h, mask in enumerate(masks):
        merged = jnp.where(mask, values[h * rows : (h + 1) * rows], merged)
    return merged


def soft_rows(stacked, keysets, lengths):
    scores = []
    for rows, keyset, length in zip(stacked, keysets, lengths):
        part = last_dot(rows, keyset) * HEAD_DIM ** (-0.5)
        live = lax.broadcasted_iota(jnp.int32, part.shape, 1) < length
        scores.append(jnp.where(live, part, -1000000000.0))
    scores = jnp.concatenate(scores, axis=0)
    raised = jnp.exp(scores - jnp.max(scores, axis=-1, keepdims=True))
    return raised * (1.0 / jnp.sum(raised, axis=-1, keepdims=True))


def split_seqs(values, seqs):
    rows = values.shape[0] // seqs
    return [values[s * rows : (s + 1) * rows] for s in range(seqs)]


def attend_block(lengths_ref, first_seq, normed, w_in, w_out, seqs, heads):
    pad = w_out.shape[0]
    mixed = rows_dot(normed, w_in[...]).astype(jnp.bfloat16)
    first = first_seq + pl.program_id(0) * seqs
    parts = split_seqs(mixed, seqs)
    masks = head_masks((parts[0].shape[0], pad), heads)
    soft = soft_rows(
        [stack_heads(part[:, :pad], masks) for part in parts],
        [part[:, pad : 2 * pad] for part in parts],
        [lengths_ref[first + s] for s in range(seqs)],
    ).astype(jnp.bfloat16)
    context = [
        merge_heads(rows_dot(probs, part[:, 2 * pad :]), masks)
        for probs, part in zip(split_seqs(soft, seqs), parts)
    ]
    context = jnp.concatenate(context, axis=0).astype(jnp.bfloat16)
    return mixed, context, rows_dot(context, w_out[...])


def front_own_kernel(
    heads, first_seq, lengths, tokens, temb, norms, w_in, w_out, mixed_out, normed_out, context_out, attended
):
    normal, unused = norm_parts(start_rows(tokens, temb))
    normed = (normal * norms[0:1] + norms[1:2]).astype(jnp.bfloat16)
    normed_out[...] = normed
    mixed, context, share = attend_block(
        lengths, first_seq, normed, w_in, w_out, tokens.shape[0], heads
    )
    mixed_out[...] = mixed
    context_out[...] = context
    attended[...] = share


def front_far_kernel(
    heads, seqs, first_seq, lengths, normed, w_in, w_out, own, attended, mixed_out
):
    mixed_out[...], unused, share = attend_block(
        lengths, first_seq, normed[...], w_in, w_out, seqs, heads
    )
    attended[...] = own[...] + share


def error_function(values):
    bounded = jnp.clip(values, -3.832506856900711, 3.832506856900711)
    square = bounded * bounded
    upper = jnp.full_like(square, erf_upper[0])
    for factor in erf_upper[1:]:
        upper = upper * square + factor
    lower = jnp.full_like(square, erf_lower[0])
    for factor in erf_lower[1:]:
        lower = lower * square + factor
    return bounded * upper / lower


def gelu_and_slope(values):
    scaled = values * math.sqrt(0.5)
    share = 0.5 + 0.5 * error_function(scaled)
    density = jnp.exp(-scaled * scaled) * (1.0 / math.sqrt(2.0 * math.pi))
    return values * share, share + values * density


def feed_block(normed, grad_down_in, up, up_t, down_t):
    upward = rows_dot(normed, up[...])
    activated, slope = gelu_and_slope(upward)
    grad_act = rows_dot(grad_down_in, down_t[...])
    grad_rise = (grad_act * slope).astype(jnp.bfloat16)
    return activated.astype(jnp.bfloat16), grad_rise, rows_dot(grad_rise, up_t[...])


def split_rows(flag, values, keep, send):
    rows = keep.shape[0]
    keep[...] = values[pl.ds(pl.multiple_of(flag * rows, 16), rows), :]
    send[...] = values[pl.ds(pl.multiple_of((1 - flag) * rows, 16), rows), :]


def feed_own_kernel(
    lengths,
    place,
    tokens,
    temb,
    attended_0,
    attended_1,
    received_0,
    received_1,
    cotangent,
    norms,
    up,
    up_t,
    down_t,
    middle_out,
    normed_out,
    grad_in_out,
    activated_out,
    entry,
    keep_down,
    send_down,
    keep_up,
    send_up,
    grad_down,
    grad_up,
):
    first = in_first_half()

    @pl.when(pl.program_id(0) == 0)
    def begin():
        grad_down[...] = jnp.zeros_like(grad_down)
        grad_up[...] = jnp.zeros_like(grad_up)

    attended = jnp.where(
        first, attended_0[...] + received_0[...], attended_1[...] + received_1[...]
    )
    middle = start_rows(tokens, temb) + attended
    middle_out[...] = middle
    normal, unused = norm_parts(middle)
    normed = (normal * norms[2:3] + norms[3:4]).astype(jnp.bfloat16)
    normed_out[...] = normed
    grad_down_in = grad_out_rows(lengths, 0, cotangent).astype(jnp.bfloat16)
    grad_in_out[...] = grad_down_in
    activated, grad_rise, share = feed_block(normed, grad_down_in, up, up_t, down_t)
    activated_out[...] = activated
    entry[...] = share
    grad_down[...] += first_dot(activated, grad_down_in)
    grad_up[...] += first_dot(normed, grad_rise)

    @pl.when(pl.program_id(0) == pl.num_programs(0) - 1)
    def write():
        split_rows(place[0], grad_down, keep_down, send_down)
        split_rows(place[1], grad_up, keep_up, send_up)


def feed_far_kernel(normed, grad_down_in, up, up_t, down_t, entry_own, activated_out, entry):
    activated, unused, share = feed_block(normed[...], grad_down_in[...], up, up_t, down_t)
    activated_out[...] = activated
    entry[...] = entry_own[...] + share


def in_first_half():
    return pl.program_id(0) < pl.num_programs(0) // 2


def result_kernel(middle, downward, received, result):
    result[...] = (middle[...] + (downward[0] + received[0])).reshape(result.shape)


def back_seqs(mixed, lengths, grad_context, heads, pad):
    seqs = len(lengths)
    parts = split_seqs(mixed, seqs)
    masks = head_masks((parts[0].shape[0], pad), heads)
    stacked = [stack_heads(part[:, :pad], masks) for part in parts]
    keysets = [part[:, pad : 2 * pad] for part in parts]
    soft = soft_rows(stacked, keysets, lengths)
    grad_stacked = [stack_heads(part, masks) for part in split_seqs(grad_context, seqs)]
    grad_probs = [last_dot(grad, part[:, 2 * pad :]) for grad, part in zip(grad_stacked, parts)]
    grad_probs = jnp.concatenate(grad_probs, axis=0)
    inner_sum = jnp.sum(soft * grad_probs, axis=-1, keepdims=True)
    grad_scores = split_seqs((soft * (grad_probs - inner_sum)).astype(jnp.bfloat16), seqs)
    probs = split_seqs(soft.astype(jnp.bfloat16), seqs)
    scaling = HEAD_DIM ** (-0.5)
    grads = []
    for s in range(seqs):
        grad_query = merge_heads(rows_dot(grad_scores[s], keysets[s]), masks) * scaling
        grad_key = first_dot(grad_scores[s], stacked[s]) * scaling
        grad_value = first_dot(probs[s], grad_stacked[s])
        grads.append(jnp.concatenate([grad_query, grad_key, grad_value], axis=1))
    return jnp.concatenate(grads, axis=0).astype(jnp.bfloat16)


def back_kernel(
    heads,
    first_seq,
    last,
    lengths,
    place,
    cotangent,
    middle,
    entry,
    received,
    mixed,
    context,
    normed_one,
    norms,
    w_out_t,
    *rest,
):
    if last:
        old_in, old_out, old_norms = rest[:3]
        rest = rest[3:]
        pieces = rest[3:7]
    grad_middle_out, grad_mixed_out, grad_norms = rest[:3]
    grad_in, grad_out = rest[-2:]
    step = pl.program_id(0)
    seqs, seq_len, width = cotangent.shape
    pad = context.shape[1]
    local = heads * HEAD_DIM

    @pl.when(step == 0)
    def begin():
        grad_in[...] = old_in[...] if last else jnp.zeros_like(grad_in)
        grad_out[...] = old_out[...] if last else jnp.zeros_like(grad_out)
        grad_norms[...] = old_norms[...] if last else jnp.zeros_like(grad_norms)

    entry_two = entry[...] + received[...]
    normal, scale = norm_parts(middle[...])
    grad_middle = grad_out_rows(lengths, first_seq, cotangent) + norm_back(
        entry_two, norms[2:3], normal, scale
    )
    grad_middle_out[...] = grad_middle
    grad_norms[2:3] += jnp.sum(entry_two * normal, axis=0, keepdims=True)
    grad_norms[3:4] += jnp.sum(entry_two, axis=0, keepdims=True)
    grad_attn = grad_middle.astype(jnp.bfloat16)
    grad_context = rows_dot(grad_attn, w_out_t[...]).astype(jnp.bfloat16)
    grad_out[...] += first_dot(context[...], grad_attn)
    found = [lengths[first_seq + step * seqs + s] for s in range(seqs)]
    grad_mixed = back_seqs(mixed[...], found, grad_context, heads, pad)
    grad_mixed_out[...] = grad_mixed
    grad_in[...] += first_dot(grad_mixed, normed_one[...])

    if last:

        @pl.when(step == pl.num_programs(0) - 1)
        def write():
            parts = [grad_in.at[part * pad : part * pad + local] for part in range(3)]
            parts.append(grad_out.at[:local])
            for flag, pair, outs in (
                (place[0], parts[:2], pieces[:2]),
                (place[1], parts[2:], pieces[2:]),
            ):

                @pl.when(flag == 0)
                def straight():
                    outs[0][...] = pair[0][...]
                    outs[1][...] = pair[1][...]

                @pl.when(flag != 0)
                def crossed():
                    outs[0][...] = pair[1][...]
                    outs[1][...] = pair[0][...]


def back_far_kernel(
    heads,
    lengths,
    tokens,
    temb,
    middle_0,
    middle_1,
    mixed_0,
    mixed_1,
    own_0,
    own_1,
    w_out_t,
    w_in_t,
    own_in_t,
    act,
    far_act_0,
    far_act_1,
    down,
    down_far,
    shares,
    grad_norms,
):
    @pl.when(pl.program_id(0) == 0)
    def begin():
        grad_norms[...] = jnp.zeros_like(grad_norms)

    first = in_first_half()
    seqs = tokens.shape[0]
    pad = w_out_t.shape[1]
    own = rows_dot(jnp.where(first, own_0[...], own_1[...]), own_in_t[...])
    normal, unused = norm_parts(start_rows(tokens, temb))
    grad_norms[0:1] += jnp.sum(own * normal, axis=0, keepdims=True)
    grad_norms[1:2] += jnp.sum(own, axis=0, keepdims=True)
    grad_attn = jnp.where(first, middle_0[...], middle_1[...]).astype(jnp.bfloat16)
    grad_context = rows_dot(grad_attn, w_out_t[...]).astype(jnp.bfloat16)
    found = [lengths[pl.program_id(0) * seqs + s] for s in range(seqs)]
    mixed = jnp.where(first, mixed_0[...], mixed_1[...])
    grad_mixed = back_seqs(mixed, found, grad_context, heads, pad)
    shares[0] = own + rows_dot(grad_mixed, w_in_t[...])
    far_act = jnp.where(first, far_act_0[...], far_act_1[...])
    shares[1] = rows_dot(act[...], down[...]) + rows_dot(far_act, down_far[...])


def add_four_kernel(own, first, second, third, total):
    total[...] = (own[...] + first[...]) + (second[...] + third[...])


def share_kernel(place, keep_a, got_a, keep_b, got_b, keep_a2, send_a2, keep_b2, send_b2, sums):
    rows = keep_a.shape[0]
    sums[:rows] = keep_a[...] + got_a[...]
    sums[rows:] = keep_b[...] + got_b[...]
    split_rows(place[1], sums.at[:rows], keep_a2, send_a2)
    split_rows(place[0], sums.at[rows:], keep_b2, send_b2)


def pair_kernel(keep_a, got_a, keep_b, got_b, both):
    rows = keep_a.shape[0]
    both[:rows] = keep_a[...] + got_a[...]
    both[rows : 2 * rows] = keep_b[...] + got_b[...]


def pair_small_kernel(mp_copies, keep_a, got_a, keep_b, got_b, norms_one, norms_two, both):
    pair_kernel(keep_a, got_a, keep_b, got_b, both)
    rows = keep_a.shape[0]
    both[2 * rows :] = jnp.zeros((8, both.shape[1]), jnp.float32)
    both[2 * rows : 2 * rows + 4] = norms_one[...] + norms_two[...] * (1.0 / mp_copies)


def all_squares(values):
    columns = jnp.sum(values * values, axis=0, keepdims=True)
    return jnp.sum(columns, axis=1, keepdims=True)


def total_kernel(both, got, total_a, total_b, squares):
    rows = total_a.shape[0]
    total = both[...] + got[...]
    total_a[...] = total[:rows]
    total_b[...] = total[rows:]
    squares[...] = jnp.broadcast_to(all_squares(total), squares.shape)


def total_small_kernel(both, got, squares, *rest):
    total_a, total_b, small = rest[-3:]
    rows = (both.shape[0] - 8) // 2
    total_a[:rows] = both[:rows] + got[:rows]
    total_b[:rows] = both[rows : 2 * rows] + got[rows : 2 * rows]
    found = squares[:1, :1] + all_squares(total_a[:rows]) + all_squares(total_b[:rows])
    norms = both[2 * rows :] + got[2 * rows :]
    fifth = lax.broadcasted_iota(jnp.int32, norms.shape, 0) == 4
    small[...] = jnp.where(fifth, found, norms)
    total_a[rows:] = small[...]
    total_b[rows:] = small[...]


def place_rows(flag, own, got, out):
    rows = out.shape[0] // 2
    out[pl.ds(pl.multiple_of(flag * rows, 16), rows), :] = own[:rows]
    out[pl.ds(pl.multiple_of((1 - flag) * rows, 16), rows), :] = got[:rows]


def merge_kernel(place, own_a, got_a, own_b, got_b, out_a, out_b):
    place_rows(place[1], own_a, got_a, out_a)
    place_rows(place[0], own_b, got_b, out_b)


def merge_after_kernel(place, own_a, got_a, own_b, got_b, after_a, after_b, out_a, out_b):
    merge_kernel(place, own_a, got_a, own_b, got_b, out_a, out_b)


def small_kernel(own_a, got_a, got_b, diagonal, small):
    rows = own_a.shape[0] - 8
    small[...] = (own_a[rows:] + got_a[rows:]) + (got_b[rows:] + diagonal[...])


def clip_factor(small, threshold):
    squares = small[4:5, :1] + all_squares(small[:4])
    norm = jnp.sqrt(squares)
    return norm, jnp.minimum(1.0, threshold / norm)


def adam_step(weight, gradient, mean_old, square_old, rate, decay, outs):
    mean_new = beta_one * mean_old + (1.0 - beta_one) * gradient
    square_new = beta_two * square_old + (1.0 - beta_two) * gradient * gradient
    lower = jnp.sqrt(square_new * (1.0 / (1.0 - beta_two**STEP))) + adam_eps
    direction = mean_new * (1.0 / (1.0 - beta_one**STEP)) / lower
    weight_new = weight - rate * (direction + decay * weight)
    outs[0][...] = mean_new
    outs[1][...] = square_new
    outs[2][...] = weight_new
    if len(outs) > 3:
        outs[3][...] = weight_new.astype(outs[3].dtype)


def adam_feed_kernel(threshold, place, small, *refs):
    unused, factor = clip_factor(small, threshold)
    late = pl.program_id(0) // (pl.num_programs(0) // 2)
    for which, rate in enumerate((rate_downproj, rate_upproj)):
        own, got, weight, mean, square = refs[5 * which : 5 * which + 5]
        outs = refs[10 + 4 * which : 14 + 4 * which]
        gradient = jnp.where(late == place[which], own[...], got[...]) * factor
        adam_step(weight[...], gradient, mean[...], square[...], rate, decay_weight, outs)


def adam_attn_kernel(
    threshold,
    place,
    small,
    own_a,
    got_a,
    own_b,
    got_b,
    in_weight,
    in_mean,
    in_square,
    out_weight,
    out_mean,
    out_square,
    norm_weight,
    norm_mean,
    norm_square,
    *outs,
):
    norm, factor = clip_factor(small, threshold)
    step = pl.program_id(0)

    @pl.when(step < 3)
    def inside():
        pick_a = jnp.where(step == place[0], own_a[...], got_a[...])
        pick_b = jnp.where(place[1] == 0, own_b[...], got_b[...])
        gradient = jnp.where(step < 2, pick_a, pick_b) * factor
        values = in_weight[...], gradient, in_mean[...], in_square[...]
        adam_step(*values, rate_inproj, decay_weight, outs[:4])

    @pl.when(step == 3)
    def outside():
        gradient = jnp.where(place[1] == 1, own_b[...], got_b[...]) * factor
        values = out_weight[...], gradient, out_mean[...], out_square[...]
        adam_step(*values, rate_outproj, decay_weight, outs[4:8])
        gradient = small[:4] * factor
        values = norm_weight[...], gradient, norm_mean[...], norm_square[...]
        adam_step(*values, rate_norms, 0.0, outs[8:11])
        outs[11][...] = jnp.broadcast_to(norm, outs[11].shape)


def finish_kernel(tokens, temb, middle_0, middle_1, entry_one, received, norms, in_grad):
    grad_middle = jnp.where(in_first_half(), middle_0[...], middle_1[...])
    entry = entry_one[0] + received[0]
    normal, scale = norm_parts(start_rows(tokens, temb))
    total = grad_middle + norm_back(entry, norms[0:1], normal, scale)
    in_grad[...] = total.reshape(in_grad.shape)


def attn_weights_kernel(w_in, w_out, in_n, in_t, out_n, out_t):
    local = w_out.shape[0]
    pad = out_n.shape[0]
    half = jnp.bfloat16
    in_n[...] = jnp.zeros_like(in_n)
    in_t[...] = jnp.zeros_like(in_t)
    out_n[...] = jnp.zeros_like(out_n)
    out_t[...] = jnp.zeros_like(out_t)
    for part in range(3):
        piece = w_in[part * local : (part + 1) * local, :]
        in_t[part * pad : part * pad + local, :] = piece.astype(half)
        in_n[:, part * pad : part * pad + local] = piece.T.astype(half)
    out_n[:local, :] = w_out[...].astype(half)
    out_t[:, :local] = w_out[...].T.astype(half)


def attn_far_kernel(piece, own, beside, line, corner, in_n, in_t, out_n, out_t, rows):
    local = own.shape[0]
    pad = out_n.shape[0]
    half = jnp.bfloat16
    index = piece[0]
    rows[...] = jnp.zeros_like(rows)
    rows[index, :local] = own[...].astype(half)
    rows[index ^ 1, :local] = beside[...].astype(half)
    rows[index ^ 2, :local] = line[...].astype(half)
    rows[index ^ 3, :local] = corner[...].astype(half)
    for part in range(3):
        in_t[part * pad : (part + 1) * pad] = rows[part]
        in_n[:, part * pad : (part + 1) * pad] = rows[part].T
    out_n[...] = rows[3]
    out_t[...] = rows[3].T


def send_attn_kernel(piece, inside, inside_corner, outside, own, corner):
    for index, block, out in ((piece[0], inside, own), (piece[0] ^ 3, inside_corner, corner)):

        @pl.when(index < 3)
        def from_input():
            out[...] = block[...]

        @pl.when(index == 3)
        def from_output():
            out[...] = outside[...]


def send_feed_kernel(piece, up, down, up_corner, down_corner, own, corner):
    rows = up.shape[0]
    own[:rows] = up[...]
    own[rows:] = down[...]
    corner[:rows] = up_corner[...]
    corner[rows:] = down_corner[...]


def touch_kernel(*refs):
    refs[-1][...] = jnp.zeros_like(refs[-1])


def feed_weights_kernel(up, down, up_n, up_t, down_n, down_t):
    half = jnp.bfloat16
    for weight, straight, turned in ((up, up_n, up_t), (down, down_n, down_t)):
        value = weight[...].astype(half)
        straight[...] = value
        turned[...] = value.T


def feed_far_weights_kernel(piece, own, beside, line, corner, *outs):
    half = jnp.bfloat16
    index = piece[0]
    rows = own.shape[0] // 2
    pieces = (index, own), (index ^ 1, beside), (index ^ 2, line), (index ^ 3, corner)
    for which in range(2):
        straight, turned = outs[2 * which : 2 * which + 2]
        part = slice(which * rows, (which + 1) * rows)
        for place, got in pieces:
            straight[pl.ds(pl.multiple_of(place * rows, 16), rows), :] = got[part].astype(half)
        turned[...] = straight[...].T


SCALARS = pl.BlockSpec(memory_space=pltpu.SMEM)
ANYWHERE = pl.BlockSpec(memory_space=pl.ANY)
WHOLE = pl.BlockSpec(memory_space=pltpu.VMEM)


def array(shape, dtype=jnp.float32):
    return jax.ShapeDtypeStruct(shape, dtype)


STAGE_COST = 10**12
class Chain:
    def __init__(self):
        self.token = None

    def __call__(
        self,
        kernel,
        args,
        in_specs,
        out_specs,
        out_shape,
        grid=(),
        scratch=(),
        scalars=(),
        vmem=20,
        ends_stage=False,
    ):
        args, in_specs, count = list(args), list(in_specs), len(args) + len(scalars)
        run = kernel
        if self.token is not None:
            args.append(self.token)
            in_specs.append(ANYWHERE)

            def run(*refs):
                return kernel(*refs[:count], *refs[count + 1 :])

        results = pl.pallas_call(
            run,
            grid_spec=pltpu.PrefetchScalarGridSpec(
                num_scalar_prefetch=len(scalars),
                grid=grid,
                in_specs=in_specs,
                out_specs=out_specs,
                scratch_shapes=list(scratch),
            ),
            out_shape=out_shape,
            compiler_params=pltpu.CompilerParams(vmem_limit_bytes=vmem * 1024 * 1024),
            cost_estimate=pl.CostEstimate(
                flops=10**12 if ends_stage else 1, bytes_accessed=1, transcendentals=0
            ),
            name=getattr(kernel, "func", kernel).__name__,
        )(*scalars, *args)
        leaves = jax.tree.leaves(results)
        self.token = min(leaves, key=lambda leaf: leaf.size * leaf.dtype.itemsize)
        return results


def body(
    tokens,
    lengths,
    timesteps,
    cotangent,
    proj_input,
    proj_output,
    proj_upward,
    proj_downward,
    norm_params,
    input_mean,
    input_square,
    output_mean,
    output_square,
    upward_mean,
    upward_square,
    downward_mean,
    downward_square,
    norms_mean,
    norms_square,
):
    seq_count, seq_len, width = tokens.shape
    local = proj_output.shape[0]
    hidden = proj_downward.shape[0]
    heads = local // HEAD_DIM
    rows = seq_count * seq_len
    dp_count, mp_count = lax.axis_size("dp"), lax.axis_size("mp")
    by_pairs = dp_count == 8
    pad = -(-local // 128) * 128
    half = jnp.bfloat16
    seqs = SEQS_STEP
    step_rows = seqs * seq_len
    steps = seq_count // seqs
    half_steps = steps // 2
    half_seqs = seq_count // 2
    half_rows = rows // 2
    more = 2 * seqs
    more_rows = more * seq_len
    more_steps = half_steps // 2
    quarter = hidden // 4
    threshold = clip_coeff * width * math.sqrt(dp_count * rows)
    own_place = lax.axis_index("dp")
    low, high = own_place % 2, (own_place // 2) % 2
    place = jnp.stack([low, high]).astype(jnp.int32)
    piece = (own_place % 4).astype(jnp.int32)[None]
    chain = Chain()

    def across(values):
        return lax.ppermute(values, "mp", swap_pairs(mp_count, 2))

    def core(values):
        return lax.ppermute(values, "mp", swap_pairs(mp_count, 1))

    def opposite(values):
        return lax.ppermute(values, "mp", swap_pairs(mp_count, 3))

    def beside(values):
        return lax.ppermute(values, "dp", swap_pairs(dp_count, 1))

    def line(values):
        return lax.ppermute(values, "dp", swap_pairs(dp_count, 2))

    def far_line(values):
        return lax.ppermute(values, "dp", swap_pairs(dp_count, 4))

    def corner(values):
        return lax.ppermute(values, "dp", swap_pairs(dp_count, 3))

    def blocks(columns, offset=0, count=step_rows):
        return pl.BlockSpec((count, columns), lambda i, *_: (i + offset, 0))

    def near_blocks(columns):
        return pl.BlockSpec(
            (step_rows, columns), lambda i, *_: (jnp.minimum(i, half_steps - 1), 0)
        )

    def away_blocks(columns):
        return pl.BlockSpec(
            (step_rows, columns), lambda i, *_: (jnp.maximum(i - half_steps, 0), 0)
        )

    def fixed(*shape):
        return pl.BlockSpec(shape, lambda *_: (0,) * len(shape))

    def seq_blocks(middle, offset=0, count=seqs):
        return pl.BlockSpec((count, middle, width), lambda i, *_: (i + offset, 0, 0))

    wide = blocks(width)
    more_wide = blocks(width, 0, more_rows)
    norm_block = fixed(*norm_params.shape)
    temb = time_embed(timesteps, width)[:, None, :]
    input_t = jnp.transpose(proj_input, (1, 2, 0)).reshape(3 * local, width)

    def piece_block(count, flip, most=3):
        def index(i, piece):
            return (jnp.minimum(piece[0] ^ flip, most), 0)

        return pl.BlockSpec((count, width), index)

    attn_sends = chain(
        send_attn_kernel,
        (input_t, input_t, proj_output),
        [piece_block(local, 0, 2), piece_block(local, 3, 2), fixed(local, width)],
        [fixed(local, width)] * 2,
        [array((local, width))] * 2,
        grid=(1,),
        scalars=(piece,),
        vmem=60,
    )
    attn_got, attn_corner = [across(values) for values in attn_sends]
    in_n, in_t, out_n, out_t = chain(
        attn_weights_kernel,
        (input_t, proj_output),
        [WHOLE] * 2,
        [WHOLE] * 4,
        [array((width, 3 * pad), half), array((3 * pad, width), half)]
        + [array((pad, width), half), array((width, pad), half)],
    )

    def front(part):
        start = part * more_steps
        return chain(
            functools.partial(front_own_kernel, heads, part * half_seqs),
            (tokens, temb, norm_params, in_n, out_n),
            [seq_blocks(seq_len, start, more), seq_blocks(1, start, more), norm_block]
            + [fixed(width, 3 * pad), fixed(pad, width)],
            [blocks(columns, 0, more_rows) for columns in (3 * pad, width, pad, width)],
            [array((half_rows, 3 * pad), half), array((half_rows, width), half)]
            + [array((half_rows, pad), half), array((half_rows, width))],
            grid=(more_steps,),
            scalars=(lengths,),
            ends_stage=part == 1,
        )

    fronts = [front(0)]
    feed_sends = chain(
        send_feed_kernel,
        (proj_upward, proj_downward, proj_upward, proj_downward),
        [piece_block(quarter, 0)] * 2 + [piece_block(quarter, 3)] * 2,
        [fixed(2 * quarter, width)] * 2,
        [array((2 * quarter, width))] * 2,
        grid=(1,),
        scalars=(piece,),
    )
    attn_y, attn_z = beside(attn_got), line(attn_got)
    chain(touch_kernel, (attn_got,), [ANYWHERE], WHOLE, array((8, 128)), ends_stage=True)
    feed_got, feed_corner = [across(values) for values in feed_sends]
    fronts.append(front(1))
    up_n, up_t, down_n, down_t = chain(
        feed_weights_kernel,
        (proj_upward, proj_downward),
        [WHOLE] * 2,
        [WHOLE] * 4,
        [array((width, hidden), half), array((hidden, width), half)]
        + [array((hidden, width), half), array((width, hidden), half)],
    )
    far_in, far_in_t, far_out, far_out_t = chain(
        attn_far_kernel,
        (attn_got, attn_y, attn_z, attn_corner),
        [WHOLE] * 4,
        [WHOLE] * 4,
        [array((width, 3 * pad), half), array((3 * pad, width), half)]
        + [array((pad, width), half), array((width, pad), half)],
        scratch=[pltpu.VMEM((4, pad, width), half)],
        scalars=(piece,),
        ends_stage=True,
    )

    def far_front(part):
        unused, normed, unused_too, own = fronts[part]
        attended, mixed = chain(
            functools.partial(front_far_kernel, heads, more, part * half_seqs),
            (normed, far_in, far_out, own),
            [more_wide, fixed(width, 3 * pad), fixed(pad, width), more_wide],
            [more_wide, blocks(3 * pad, 0, more_rows)],
            [array((half_rows, width)), array((half_rows, 3 * pad), half)],
            grid=(more_steps,),
            scalars=(lengths,),
        )
        return attended, core(attended), mixed

    attended_0, attended_got_0, far_mixed_0 = far_front(0)
    attended_1, attended_got_1, far_mixed_1 = far_front(1)
    far_mixed = far_mixed_0, far_mixed_1
    feed_y, feed_z = beside(feed_got), line(feed_got)
    chain(touch_kernel, (feed_got,), [ANYWHERE], WHOLE, array((8, 128)), ends_stage=True)

    shared = [array((rows, width))] + [array((rows, width), half)] * 2
    shared += [array((rows, hidden), half), array((rows, width))]
    halves = [array((hidden // 2, width))] * 2 + [array((width // 2, hidden))] * 2
    middle, normed_two, grad_down_in, activated, entry, *grads = chain(
        feed_own_kernel,
        (tokens, temb, attended_0, attended_1, attended_got_0, attended_got_1)
        + (cotangent, norm_params, up_n, up_t, down_t),
        [seq_blocks(seq_len), seq_blocks(1)]
        + [near_blocks(width), away_blocks(width)] * 2
        + [seq_blocks(seq_len), norm_block]
        + [fixed(width, hidden), fixed(hidden, width), fixed(width, hidden)],
        [wide, wide, wide, blocks(hidden), wide] + [fixed(*shape.shape) for shape in halves],
        shared + halves,
        grid=(steps,),
        scratch=[pltpu.VMEM((hidden, width), jnp.float32), pltpu.VMEM((width, hidden), jnp.float32)],
        scalars=(lengths, place),
        vmem=40,
    )

    def send_pair(pair):
        keep_a, send_a, keep_b, send_b = pair
        return keep_a, beside(send_a), keep_b, line(send_b)

    def share_pair(pair, ends_stage):
        if not by_pairs:
            return pair
        size = array((pair[0].shape[0] // 2, width))
        keep_a, send_a, keep_b, send_b = chain(
            share_kernel,
            pair,
            [WHOLE] * 4,
            [WHOLE] * 4,
            [size] * 4,
            scratch=[pltpu.VMEM((4 * size.shape[0], width), jnp.float32)],
            scalars=(place,),
            ends_stage=ends_stage,
        )
        return keep_a, line(send_a), keep_b, beside(send_b)

    def merge_pair(pair, extra, kernel, after):
        size = array((2 * (pair[0].shape[0] - extra), width))
        first, second = chain(
            kernel,
            (*pair, *after),
            [WHOLE] * 4 + [ANYWHERE] * len(after),
            [WHOLE] * 2,
            [size] * 2,
            scalars=(place,),
        )
        return first, beside(first), second, line(second)

    def sum_plainly(pair):
        keep_a, send_a, keep_b, send_b = pair
        totals = []
        for flag, keep, send in ((low, keep_a, send_a), (high, keep_b, send_b)):
            whole = pick(flag == 0, jnp.concatenate([keep, send]), jnp.concatenate([send, keep]))
            total = lax.psum(whole, "dp")
            count = total.shape[0] // 2
            totals += [lax.dynamic_slice_in_dim(total, f * count, count) for f in (flag, 1 - flag)]
        return totals, sum(jnp.sum(total * total) for total in totals) / dp_count

    if by_pairs:
        grads = send_pair(grads)
    up_far_n, up_far_t, down_far_n, down_far_t = chain(
        feed_far_weights_kernel,
        (feed_got, feed_y, feed_z, feed_corner),
        [WHOLE] * 4,
        [WHOLE] * 4,
        [array((width, hidden), half), array((hidden, width), half)]
        + [array((hidden, width), half), array((width, hidden), half)],
        scalars=(piece,),
        ends_stage=True,
    )

    def far(part):
        offset = part * more_steps
        own = blocks(width, offset, more_rows)
        act, total = chain(
            feed_far_kernel,
            (normed_two, grad_down_in, up_far_n, up_far_t, down_far_t, entry),
            [own, own, fixed(width, hidden), fixed(hidden, width), fixed(width, hidden), own],
            [blocks(hidden, 0, more_rows), more_wide],
            [array((half_rows, hidden), half), array((half_rows, width))],
            grid=(more_steps,),
            vmem=24,
        )
        return act, total, core(total)

    far_0, far_1 = far(0), far(1)
    grads = share_pair(grads, True)

    def back(part, feed, before):
        start = part * half_steps
        mixed, normed_one, context, unused = fronts[part]
        shapes = [(3 * pad, width), (pad, width), norm_params.shape]
        last = before is not None
        ends = [(local, width)] * 4 if last else shapes[:2]
        return chain(
            functools.partial(back_kernel, heads, part * half_seqs, last),
            (cotangent, middle, feed[1], feed[2], mixed, context, normed_one, norm_params, out_t)
            + (before if last else ()),
            [seq_blocks(seq_len, start), blocks(width, start), wide, wide]
            + [blocks(3 * pad), blocks(pad), wide, norm_block, fixed(width, pad)]
            + ([fixed(*shape) for shape in shapes] if last else []),
            [wide, blocks(3 * pad), norm_block] + [fixed(*shape) for shape in ends],
            [array((half_rows, width)), array((half_rows, 3 * pad), half)]
            + [array(norm_params.shape)]
            + [array(shape) for shape in ends],
            grid=(half_steps,),
            scratch=[pltpu.VMEM(shape, jnp.float32) for shape in shapes[:2]] if last else (),
            scalars=(lengths, place),
            vmem=32,
        )

    grad_middle_0, grad_mixed_0, norms_0, in_0, out_0 = back(0, far_0, None)
    if by_pairs:
        both = chain(
            pair_kernel,
            grads,
            [WHOLE] * 4,
            WHOLE,
            array((2 * grads[0].shape[0], width)),
            ends_stage=True,
        )
        both_got = far_line(both)
    grad_middle_1, grad_mixed_1, norms_two, *attn_grads = back(1, far_1, (in_0, out_0, norms_0))
    if by_pairs:
        attn_grads = send_pair(attn_grads)

    def more_halves(columns):
        return [
            pl.BlockSpec((more_rows, columns), lambda i, *_: (jnp.minimum(i, more_steps - 1), 0)),
            pl.BlockSpec((more_rows, columns), lambda i, *_: (jnp.maximum(i - more_steps, 0), 0)),
        ]

    shares, norms_one = chain(
        functools.partial(back_far_kernel, heads),
        (tokens, temb, grad_middle_0, grad_middle_1, *far_mixed, grad_mixed_0, grad_mixed_1)
        + (far_out_t, far_in_t, in_t, activated, far_0[0], far_1[0], down_n, down_far_n),
        [seq_blocks(seq_len, 0, more), seq_blocks(1, 0, more)]
        + more_halves(width)
        + more_halves(3 * pad) * 2
        + [fixed(width, pad), fixed(3 * pad, width), fixed(3 * pad, width)]
        + [blocks(hidden, 0, more_rows)]
        + more_halves(hidden)
        + [fixed(hidden, width)] * 2,
        [pl.BlockSpec((2, more_rows, width), lambda i, *_: (0, i, 0)), norm_block],
        [array((2, rows, width)), array(norm_params.shape)],
        grid=(2 * more_steps,),
        scalars=(lengths,),
        vmem=52,
    )
    shares_got = core(shares)

    def share_blocks(which):
        return pl.BlockSpec((1, step_rows, width), lambda i, *_: (which, i, 0))

    if by_pairs:
        size = array((both.shape[0] // 2, width))
        first, second, squares = chain(
            total_kernel,
            (both, both_got),
            [WHOLE] * 2,
            [WHOLE] * 3,
            [size, size, array((8, 128))],
        )
        grads = first, line(first), second, beside(second)
        attn_grads = share_pair(attn_grads, True)
        grads = merge_pair(grads, 0, merge_after_kernel, attn_grads[1::2])
        attn_both = chain(
            functools.partial(pair_small_kernel, mp_count),
            (*attn_grads, norms_one, norms_two),
            [WHOLE] * 6,
            WHOLE,
            array((2 * attn_grads[0].shape[0] + 8, width)),
        )
        attn_both_got = far_line(attn_both)
    result = chain(
        result_kernel,
        (middle, shares, shares_got),
        [wide, share_blocks(1), share_blocks(1)],
        seq_blocks(seq_len),
        array(tokens.shape),
        grid=(steps,),
    )
    in_grad = chain(
        finish_kernel,
        (tokens, temb, grad_middle_0, grad_middle_1, shares, shares_got, norm_params),
        [seq_blocks(seq_len), seq_blocks(1), near_blocks(width), away_blocks(width)]
        + [share_blocks(0), share_blocks(0), norm_block],
        seq_blocks(seq_len),
        array(tokens.shape),
        grid=(steps,),
    )
    if by_pairs:
        size = array((attn_both.shape[0] // 2 + 4, width))
        first, second, small = chain(
            total_small_kernel,
            (attn_both, attn_both_got, squares, grads[1], grads[3]),
            [WHOLE] * 3 + [ANYWHERE] * 2,
            [WHOLE] * 3,
            [size, size, array((8, width))],
        )
        attn_grads = first, line(first), second, beside(second)
        small = chain(
            small_kernel,
            (*attn_grads[:2], attn_grads[3], corner(small)),
            [WHOLE] * 4,
            WHOLE,
            array(small.shape),
        )
        parts = small, core(small), across(small), opposite(small)
        attn_grads = merge_pair(attn_grads, 8, merge_kernel, ())
        small = chain(add_four_kernel, parts, [WHOLE] * 4, WHOLE, array(small.shape))
    else:
        grads, squares = sum_plainly(grads)
        attn_grads, attn_squares = sum_plainly(attn_grads)
        found = jnp.broadcast_to(squares + attn_squares, (4, width))
        small = jnp.concatenate([norms_one + norms_two / mp_count, found])
        small = lax.psum(small, ("dp", "mp"))

    def turned(values):
        return jnp.transpose(values, (1, 2, 0)).reshape(3 * local, width)

    weights = proj_downward, proj_upward
    moments = (downward_mean, downward_square), (upward_mean, upward_square)
    args, specs, outs, shapes = [small], [fixed(8, width)], [], []
    for which, weight in enumerate(weights):
        count = weight.shape[0] // 4
        block = pl.BlockSpec((count, width), lambda i, *_: (i, 0))
        part = pl.BlockSpec((count, width), lambda i, *_: (lax.rem(i, 2), 0))
        args += [*grads[2 * which : 2 * which + 2], weight, *moments[which]]
        specs += [part] * 2 + [block] * 3
        outs += [block] * 4
        shapes += [array(weight.shape)] * 3 + [array(weight.shape, half)]
    feed_states = chain(
        functools.partial(adam_feed_kernel, threshold),
        args,
        specs,
        outs,
        shapes,
        grid=(4,),
        scalars=(place,),
        vmem=32,
    )
    block = pl.BlockSpec((local, width), lambda i, *_: (jnp.minimum(i, 2), 0))
    one = fixed(local, width)
    states = chain(
        functools.partial(adam_attn_kernel, threshold),
        (small, *attn_grads)
        + (input_t, turned(input_mean), turned(input_square))
        + (proj_output, output_mean, output_square, norm_params, norms_mean, norms_square),
        [fixed(8, width)] + [one] * 4 + [block] * 3 + [one] * 3 + [norm_block] * 3,
        [block] * 4 + [one] * 4 + [norm_block] * 3 + [fixed(8, 128)],
        [array(input_t.shape)] * 3
        + [array(input_t.shape, half)]
        + [array(proj_output.shape)] * 3
        + [array(proj_output.shape, half)]
        + [array(norm_params.shape)] * 3
        + [array((8, 128))],
        grid=(4,),
        scalars=(place,),
        vmem=24,
    )
    in_state = [jnp.transpose(s.reshape(3, local, width), (2, 0, 1)) for s in states[:4]]
    grad_norm = states[11][0, 0]
    return (
        result,
        in_grad,
        grad_norm,
        *in_state,
        *states[4:8],
        *feed_states[4:],
        *feed_states[:4],
        *states[8:11],
    )


def solution(mesh):
    in_specs = (
        P("dp", None, None),
        P("dp"),
        P("dp"),
        P("dp", None, None),
        P(None, None, "mp"),
        P("mp", None),
        P(None, "mp"),
        P("mp", None),
        P(),
        P(None, None, "mp"),
        P(None, None, "mp"),
        P("mp", None),
        P("mp", None),
        P(None, "mp"),
        P(None, "mp"),
        P("mp", None),
        P("mp", None),
        P(),
        P(),
    )
    out_specs = (
        P("dp", None, None),
        P("dp", None, None),
        P(),
        P(None, None, "mp"),
        P(None, None, "mp"),
        P(None, None, "mp"),
        P(None, None, "mp"),
        P("mp", None),
        P("mp", None),
        P("mp", None),
        P("mp", None),
        P(None, "mp"),
        P(None, "mp"),
        P(None, "mp"),
        P(None, "mp"),
        P("mp", None),
        P("mp", None),
        P("mp", None),
        P("mp", None),
        P(),
        P(),
        P(),
    )
    return jax.shard_map(body, mesh=mesh, in_specs=in_specs, out_specs=out_specs, check_vma=False)
```
